128 devices in a mesh: grp: 2 (over x_hi), tp: 64 (over y, x_lo, z, core).
Axes of the slice: x: 4 (x_hi: 2, x_lo: 2; x = x_hi * 2 + x_lo), y: 4, z: 4, core: 2. Of those that a mesh axis runs over, the one named last changes fastest.
Arguments:
- tokens: bfloat16 [32768, 1664], P(('grp', 'tp')), may hold values from -6 to 6
- keep_mask: int32 [32768], P(('grp', 'tp')), may hold values 0 or 1
- shard_counts: int32 [128], P(('grp', 'tp')), may hold values from 1 to 256, 24576 in all
- latents: bfloat16 [512, 4096], P('grp', 'tp'), may hold values from -1.5 to 1.5
- query_weight: bfloat16 [4096, 1024], P('tp'), may hold values from -0.09375 to 0.09375
- keyval_weight: bfloat16 [1664, 2048], P(('grp', 'tp')), may hold values from -0.15625 to 0.15625
- output_weight: bfloat16 [1024, 4096], P(None, 'tp'), may hold values from -6 to 6
- project_weight: bfloat16 [4096, 8192], P(None, 'tp'), may hold values from -0.09375 to 0.09375
- llm_gain: bfloat16 [8192], P('tp'), may hold values from 0.5 to 1.5
- input_grad: bfloat16 [512, 8192], P('grp', 'tp'), may hold values from -6 to 6
Outputs:
- llm_input: bfloat16 [512, 8192], P('grp', 'tp')
- grad_latents: float32 [512, 4096], P('grp', 'tp')
- grad_query_weight: float32 [4096, 1024], P('tp')
- grad_keyval_weight: float32 [1664, 2048], P(('grp', 'tp'))
- grad_output_weight: float32 [1024, 4096], P(None, 'tp')
- grad_project_weight: float32 [4096, 8192], P(None, 'tp')
- grad_llm_gain: float32 [8192], P('tp')
The draws below stay inside these ranges and needn't reach their ends.
All inputs are finite; a program needn't handle non-finite values. No bound on the sum of `keep_mask` or of `shard_counts` on one device may be relied on, other than what follows from the above.
Results may differ from the reference program's by a relative error of at most 0.015.
Values may be sent and summed in bfloat16 or wider, within the bound.
A program may use at most 128 MiB of HBM per device.

```python
import math
import jax
import jax.numpy as jnp
import numpy as np
from jax import lax

D_VIS = 1664
D_LAT = 4096
LATENTS = 512
HEADS = 8
HEAD_DIM = 128
INNER = 1024
D_LLM = 8192
TOK_DEV = 256
TOKENS = 32768
N_GRP = 2
N_TP = 64


def with_ends(entries, stream_key, least, high):
    dims = entries.shape
    spot = [jax.random.randint(jax.random.fold_in(stream_key, axis), (), 0, dims[axis]) for axis in range(len(dims))]
    entries = entries.at[tuple(spot)].set(least)
    longest = dims.index(max(dims))
    spot[longest] = (spot[longest] + 1) % dims[longest]
    return entries.at[tuple(spot)].set(high)


def level_of(own_key, dims, cuts, low, largest):
    level, own = 1.0, jax.random.fold_in(own_key, 6)
    for position, shards_of in cuts:
        draws = jnp.exp(jax.random.uniform(jax.random.fold_in(own, position), (shards_of,), jnp.float32, low / len(cuts), largest / len(cuts)))
        level = level * jnp.repeat(draws, dims[position] // shards_of).reshape([-1 if axis == position else 1 for axis in range(len(dims))])
    return level


def split_up(count, total, bound, skew):
    weights = [(1 << 20) // math.isqrt(rank ** skew) + 1 for rank in range(2, count + 1)]
    spare, holding = total - bound - (count - 1), [1] * (count - 1)
    while spare > 0:
        free = [i for i in range(count - 1) if holding[i] < bound]
        pool, left = sum([weights[i] for i in free]), spare
        for i in free:
            addition = min(bound - holding[i], max(1, left * weights[i] // pool), spare)
            holding[i] = holding[i] + addition
            spare = spare - addition
    return np.array([bound] + holding)


def uneven(rng, count, total, most, slope):
    if count == 2:
        one = jax.random.randint(rng, (), max(1, total - most), min(most, total - 1) + 1)
        return jnp.stack([one, total - one])
    lengths = jnp.asarray(split_up(count, total, most, slope), jnp.int32)
    twos = (count - 1) // 2
    giver, sink = lengths[1:1 + 2 * twos:2], lengths[2:2 + 2 * twos:2]
    slack = jnp.minimum(giver - 1, most - sink)
    passed = jax.random.randint(jax.random.fold_in(rng, 1), (twos,), 0, 1 << 20) % (slack + 1)
    lengths = lengths.at[1:1 + 2 * twos:2].set(giver - passed).at[2:2 + 2 * twos:2].set(sink + passed)
    return lengths[jax.random.permutation(jax.random.fold_in(rng, 2), count)]


def scatter_about(stream_key, extent, scale, limit, cuts=(), held_as=jnp.bfloat16):
    level = level_of(stream_key, extent, cuts, -0.22, 0.18) if cuts else 1.0
    entries = jax.random.normal(stream_key, extent, jnp.float32) * scale * level
    return jnp.minimum(jnp.maximum(entries, -limit), limit).astype(held_as)


def setup_inputs(seed: int = 0) -> dict:
    streams_of = jax.random.split(jax.random.key(seed), 11)
    return {
        "tokens": scatter_about(streams_of[0], (TOKENS, D_VIS), 1.0, 6.0, ((0, 128),)),
        "keep_mask": with_ends((jax.random.randint(streams_of[1], (TOKENS,), 0, 4) < 3).astype(jnp.int32), jax.random.fold_in(streams_of[1], 1), 0, 1),
        "shard_counts": uneven(streams_of[2], N_GRP * N_TP, N_GRP * N_TP * TOK_DEV * 3 // 4, TOK_DEV, 1).astype(jnp.int32),
        "latents": scatter_about(streams_of[3], (LATENTS, D_LAT), 0.1, 1.5, ((0, 2), (1, 64))),
        "query_weight": scatter_about(streams_of[4], (D_LAT, INNER), D_LAT ** -0.5, 0.09375, ((0, 64),)),
        "keyval_weight": scatter_about(streams_of[5], (D_VIS, 2 * INNER), D_VIS ** -0.5, 0.15625, ((0, 128),)),
        "output_weight": scatter_about(streams_of[6], (INNER, D_LAT), 1 ** -0.5, 6.0, ((1, 64),)),
        "project_weight": scatter_about(streams_of[7], (D_LAT, D_LLM), D_LAT ** -0.5, 0.09375, ((1, 64),)),
        "llm_gain": jnp.clip(1.0 + 0.1 * jax.random.normal(streams_of[8], (D_LLM,), jnp.float32), 0.5, 1.5).astype(jnp.bfloat16),
        "input_grad": scatter_about(streams_of[9], (LATENTS, D_LLM), 1.0, 6.0, ((0, 2), (1, 64))),
    }


score_cap = 5.0

def head_scores(query, key_rows, valid_rows):
    query_heads = query.astype(jnp.float32).reshape(LATENTS, HEADS, HEAD_DIM)
    key_heads = key_rows.astype(jnp.float32).reshape(-1, HEADS, HEAD_DIM)
    raw_scores = jnp.einsum('qhd,khd->hqk', query_heads, key_heads) / math.sqrt(HEAD_DIM)
    capped = score_cap * jnp.tanh(raw_scores / score_cap)
    weights = jnp.exp(capped) * valid_rows[None, None, :]
    return (capped, weights)

def project_block(block, keyval_weight):
    keyval = jnp.dot(block, keyval_weight, preferred_element_type=jnp.float32)
    return (keyval[:, :INNER].astype(jnp.bfloat16), keyval[:, INNER:].astype(jnp.bfloat16))

def reference(tokens, keep_mask, shard_counts, latents, query_weight, keyval_weight, output_weight, project_weight, llm_gain, input_grad):
    shards = N_GRP * N_TP
    latent_f32 = latents.astype(jnp.float32)
    latent_rinv = lax.rsqrt(lax.optimization_barrier(jnp.mean(latent_f32 * latent_f32, axis=1)) + 1e-06)
    proj_query = jnp.dot(latents, query_weight, preferred_element_type=jnp.float32)
    query = (proj_query * latent_rinv[:, None]).astype(jnp.bfloat16)
    positions = jnp.arange(TOK_DEV, dtype=jnp.int32)
    keep_blocks = keep_mask.reshape(shards, TOK_DEV)
    valid_all = (((keep_blocks == 1) | (positions[None, :] == 0)) & (positions[None, :] < shard_counts[:, None])).astype(jnp.float32)
    token_blocks = tokens.reshape(shards, TOK_DEV, D_VIS)

    def forward_block(carry, inputs):
        numer, totals = carry
        block, valid_rows = inputs
        key_rows, values = project_block(block, keyval_weight)
        capped, weights = head_scores(query, key_rows, valid_rows)
        weights_half = weights.astype(jnp.bfloat16).astype(jnp.float32)
        value_heads = values.astype(jnp.float32).reshape(-1, HEADS, HEAD_DIM)
        numer = numer + jnp.einsum('hqk,khd->qhd', weights_half, value_heads)
        totals = totals + lax.optimization_barrier(jnp.sum(weights, axis=2)).T
        return ((numer, totals), None)
    start = (jnp.zeros((LATENTS, HEADS, HEAD_DIM), jnp.float32), jnp.zeros((LATENTS, HEADS), jnp.float32))
    (numer, totals), _ = lax.scan(forward_block, start, (token_blocks, valid_all))
    attended = (numer / totals[:, :, None]).reshape(LATENTS, INNER).astype(jnp.bfloat16)
    latents_out = (latent_f32 + jnp.dot(attended, output_weight, preferred_element_type=jnp.float32)).astype(jnp.bfloat16)
    hidden = jnp.dot(latents_out, project_weight, preferred_element_type=jnp.float32).astype(jnp.bfloat16)
    hidden_f32 = hidden.astype(jnp.float32)
    hidden_rinv = lax.rsqrt(lax.optimization_barrier(jnp.mean(hidden_f32 * hidden_f32, axis=1)) + 1e-05)
    gain_f32 = llm_gain.astype(jnp.float32)
    llm_input = (hidden_f32 * hidden_rinv[:, None] * gain_f32[None, :]).astype(jnp.bfloat16)
    grad_f32 = input_grad.astype(jnp.float32)
    scaled_dy = grad_f32 * gain_f32[None, :]
    grad_llm_gain = lax.optimization_barrier(jnp.sum(grad_f32 * hidden_f32 * hidden_rinv[:, None], axis=0))
    dot_total = lax.optimization_barrier(jnp.sum(hidden_f32 * scaled_dy, axis=1))
    grad_hidden = (hidden_rinv[:, None] * scaled_dy - (hidden_rinv ** 3 / D_LLM * dot_total)[:, None] * hidden_f32).astype(jnp.bfloat16)
    grad_project_weight = jnp.dot(latents_out.T, grad_hidden, preferred_element_type=jnp.float32)
    grad_lat_out = jnp.dot(grad_hidden, project_weight.T, preferred_element_type=jnp.float32).astype(jnp.bfloat16)
    grad_output_weight = jnp.dot(attended.T, grad_lat_out, preferred_element_type=jnp.float32)
    grad_attended = jnp.dot(grad_lat_out, output_weight.T, preferred_element_type=jnp.float32).astype(jnp.bfloat16)
    grad_heads = grad_attended.astype(jnp.float32).reshape(LATENTS, HEADS, HEAD_DIM)
    attended_heads = attended.astype(jnp.float32).reshape(LATENTS, HEADS, HEAD_DIM)
    row_delta = lax.optimization_barrier(jnp.sum(grad_heads * attended_heads, axis=2))
    scaled_grad = (grad_heads / totals[:, :, None]).astype(jnp.bfloat16).astype(jnp.float32)
    scaled_delta = (row_delta / totals).astype(jnp.bfloat16).astype(jnp.float32)
    query_heads = query.astype(jnp.float32).reshape(LATENTS, HEADS, HEAD_DIM)

    def backward_block(carry, inputs):
        grad_query, grad_weight = carry
        block, valid_rows = inputs
        key_rows, values = project_block(block, keyval_weight)
        capped, weights = head_scores(query, key_rows, valid_rows)
        weights_half = weights.astype(jnp.bfloat16).astype(jnp.float32)
        value_heads = values.astype(jnp.float32).reshape(-1, HEADS, HEAD_DIM)
        key_heads = key_rows.astype(jnp.float32).reshape(-1, HEADS, HEAD_DIM)
        prob_grad = jnp.einsum('qhd,khd->hqk', scaled_grad, value_heads)
        dscore = (weights * (prob_grad - scaled_delta.T[:, :, None]) * (1.0 - (capped / score_cap) ** 2) / math.sqrt(HEAD_DIM)).astype(jnp.bfloat16).astype(jnp.float32)
        grad_query = grad_query + jnp.einsum('hqk,khd->qhd', dscore, key_heads)
        key_grad = jnp.einsum('hqk,qhd->khd', dscore, query_heads).astype(jnp.bfloat16).reshape(-1, INNER)
        value_grad = jnp.einsum('hqk,qhd->khd', weights_half, scaled_grad).astype(jnp.bfloat16).reshape(-1, INNER)
        grad_keyval = jnp.concatenate([key_grad, value_grad], axis=1)
        grad_weight = grad_weight + jnp.dot(block.T, grad_keyval, preferred_element_type=jnp.float32)
        return ((grad_query, grad_weight), None)
    start = (jnp.zeros((LATENTS, HEADS, HEAD_DIM), jnp.float32), jnp.zeros((D_VIS, 2 * INNER), jnp.float32))
    (grad_query, grad_keyval_weight), _ = lax.scan(backward_block, start, (token_blocks, valid_all))
    grad_query = grad_query.reshape(LATENTS, INNER)
    scaled_query = (grad_query * latent_rinv[:, None]).astype(jnp.bfloat16)
    grad_query_weight = jnp.dot(latents.T, scaled_query, preferred_element_type=jnp.float32)
    ratio_dot = lax.optimization_barrier(jnp.sum(grad_query * proj_query, axis=1))
    grad_latents = grad_lat_out.astype(jnp.float32) + jnp.dot(scaled_query, query_weight.T, preferred_element_type=jnp.float32) - (latent_rinv ** 3 / D_LAT * ratio_dot)[:, None] * latent_f32
    return (llm_input, grad_latents, grad_query_weight, grad_keyval_weight, grad_output_weight, grad_project_weight, grad_llm_gain)
```

```python
import functools
import math

import jax
import jax.numpy as jnp
import numpy as np
from jax import lax
from jax.experimental import pallas as pl
from jax.experimental.pallas import tpu as pltpu
from jax.sharding import PartitionSpec as P

D_LAT = 4096
HEAD_DIM = 128
D_LLM = 8192
SCORE_CAP = 5.0
SCALE = 1.0 / math.sqrt(HEAD_DIM)
CHIPS = 64
GROUP = 64

F32 = jnp.float32
BF16 = jnp.bfloat16
MESH = pl.DeviceIdType.MESH
ANY = pl.BlockSpec(memory_space=pl.ANY)
VMEM = pl.BlockSpec(memory_space=pltpu.VMEM)

ORDERS = ((2, 1, 0), (1, 0, 2), (0, 2, 1))
WIDE = ((0, 384), (384, 384), (768, 256))
WIDE_TURNED = ((0, 256), (256, 384), (640, 384))
ROWS_64 = ((0, 16), (16, 32), (48, 16))


def row_dot(left, right):
    return lax.dot_general(left, right, (((0,), (0,)), ((), ())), preferred_element_type=F32)


def col_dot(left, right):
    return lax.dot_general(left, right, (((1,), (1,)), ((), ())), preferred_element_type=F32)


def dot(left, right):
    return jnp.dot(left, right, preferred_element_type=F32)


class Place:
    def __init__(self):
        self.g = lax.axis_index("grp")
        self.t = lax.axis_index("tp")
        self.core = self.t % 2
        self.j = self.t // 2
        self.z = self.j % 4
        self.xl = (self.j // 4) % 2
        self.y = self.j // 8
        self.x = self.g * 2 + self.xl

    def chip(self, x, y, z):
        return x // 2, (y * 2 + x % 2) * 4 + z

    def plane_peer(self, k):
        return self.chip((self.x + k // 16) % 4, (self.y + (k // 4) % 4) % 4, (self.z + k % 4) % 4)

    def group_peer(self, k):
        y = (self.y + k // 16) % 4
        xl = (self.xl + (k // 8) % 2) % 2
        z = (self.z + (k // 2) % 4) % 4
        return ((y * 2 + xl) * 4 + z) * 2 + (self.core + k % 2) % 2

    def sibling(self):
        return self.g, self.j * 2 + 1 - self.core


def remote(src, dst, sends, recvs, device):
    return pltpu.make_async_remote_copy(
        src_ref=src, dst_ref=dst, send_sem=sends, recv_sem=recvs, device_id=device, device_id_type=MESH
    )


def each_peer(n, do):
    def body(k, carry):
        do(k)
        return carry

    lax.fori_loop(1, n, body, 0)


class Gather:
    def __init__(self, place, ref, view, sends, recvs):
        self.place, self.ref, self.view, self.sends, self.recvs = place, ref, view, sends, recvs

    def copies(self, phase):
        pc = self.place
        mine = [pc.x, pc.y, pc.z]
        for part, order in enumerate(ORDERS):
            held = list(mine)
            for axis in order[:phase]:
                held[axis] = None
            block = self.view(self.ref, *held, part)
            for step in (1, 3, 2):
                peer = list(mine)
                peer[order[phase]] = (peer[order[phase]] + step) % 4
                g, j = pc.chip(*peer)
                spot = (part * 3 + phase) * 3 + step - 1
                yield remote(
                    block, block, self.sends.at[spot], self.recvs.at[spot], (g, j * 2 + pc.core)
                )

    def start(self, phase):
        for copy in self.copies(phase):
            copy.start()

    def wait(self, phase):
        for copy in self.copies(phase):
            copy.wait_recv()

    def drain(self):
        for phase in range(3):
            for copy in self.copies(phase):
                copy.wait_send()


def pick(value):
    return slice(None) if value is None else value


def halves(x):
    return (slice(None), slice(None)) if x is None else (x // 2, x % 2)


def view_weight(ref, x, y, z, part):
    return ref.at[pick(x), pick(y), pick(z), :, :, pl.ds(*WIDE[part])]


def view_output(core, ref, x, y, z, part):
    hi, lo = halves(x)
    return ref.at[pick(y), lo, pick(z), core, hi, :, pl.ds(*WIDE_TURNED[part])]


def view_latents(core, ref, x, y, z, part):
    hi, lo = halves(x)
    return ref.at[hi, pick(y), lo, pick(z), core, pl.ds(*ROWS_64[part]), :]


def total_slots(own, slots, n):
    def body(k, total):
        return total + slots[k].astype(F32)

    return lax.fori_loop(1, n, body, own.astype(F32))


def start_kernel(
    wpl, tokp, val, qpart, owt, lt,
    wg, tg, vg, qg, owg, lg, proj, rinv,
    recvq, qblk, w_s, w_r, ow_s, ow_r, l_s, l_r, q_s, q_r, qa_s, qa_r, sib_s, sib_r, loc,
):
    pc = Place()
    core = pc.core
    sib = pc.sibling()
    rows = pl.multiple_of((pc.j // 2) * 16, 16)

    w_sib = remote(wpl.at[1 - core], wg.at[pc.x, pc.y, pc.z, core], sib_s.at[0], sib_r.at[0], sib)
    w_sib.start()
    w_own = pltpu.make_async_copy(wpl.at[core], wg.at[pc.x, pc.y, pc.z, core], loc.at[0])
    w_own.start()

    def q_copy(k):
        t = pc.group_peer(k)
        j, c = t // 2, t % 2
        src = qpart.at[c * 2 + j % 2, pl.ds(pl.multiple_of((j // 2) * 16, 16), 16), :]
        return remote(src, recvq.at[k], q_s.at[k], q_r.at[k], (pc.g, t))

    each_peer(GROUP, lambda k: q_copy(k).start())
    t_sib = remote(tokp, tg.at[core], sib_s.at[1], sib_r.at[1], sib)
    t_sib.start()
    v_sib = remote(val, vg.at[core], sib_s.at[2], sib_r.at[2], sib)
    v_sib.start()
    own = [
        pltpu.make_async_copy(tokp, tg.at[core], loc.at[1]),
        pltpu.make_async_copy(val, vg.at[core], loc.at[2]),
        pltpu.make_async_copy(
            owt.at[pl.ds(pl.multiple_of(pc.g * 32, 32), 32), :],
            owg.at[pc.y, pc.xl, pc.z, core, pc.g],
            loc.at[3],
        ),
        pltpu.make_async_copy(lt, lg.at[pc.g, pc.y, pc.xl, pc.z, core], loc.at[4]),
    ]
    for copy in own:
        copy.start()

    weight = Gather(pc, wg, view_weight, w_s, w_r)
    output = Gather(pc, owg, functools.partial(view_output, core), ow_s, ow_r)
    latents = Gather(pc, lg, functools.partial(view_latents, core), l_s, l_r)
    w_own.wait()
    w_sib.wait_recv()
    weight.start(0)

    each_peer(GROUP, lambda k: q_copy(k).wait_recv())
    total = total_slots(qpart[core * 2 + pc.j % 2, pl.ds(rows, 16), :], recvq, GROUP)
    inv = lax.rsqrt(total[:, 256:] / D_LAT + 1e-06)
    rinv[...] = inv
    proj[...] = total[:, :256]
    qblk[...] = (total[:, :256] * inv[:, :1]).astype(BF16)
    columns = pl.multiple_of((pc.j % 2) * 256, 256)
    q_spot = qg.at[pl.ds(pl.multiple_of(pc.g * 256 + rows, 16), 16), pl.ds(columns, 256)]

    def qa_copy(k):
        g, j = pc.plane_peer(k)
        return remote(qblk, q_spot, qa_s.at[k], qa_r.at[k], (g, j * 2 + core))

    each_peer(CHIPS, lambda k: qa_copy(k).start())
    q_own = pltpu.make_async_copy(qblk, q_spot, loc.at[5])
    q_own.start()

    weight.wait(0)
    weight.start(1)
    for copy in own:
        copy.wait()
    latents.start(0)
    output.start(0)
    weight.wait(1)
    weight.start(2)
    latents.wait(0)
    latents.start(1)
    output.wait(0)
    output.start(1)
    weight.wait(2)
    latents.wait(1)
    latents.start(2)
    output.wait(1)
    output.start(2)
    each_peer(CHIPS, lambda k: qa_copy(k).wait_recv())
    q_own.wait()
    latents.wait(2)
    output.wait(2)
    t_sib.wait()
    v_sib.wait()
    w_sib.wait_send()
    each_peer(GROUP, lambda k: q_copy(k).wait_send())
    each_peer(CHIPS, lambda k: qa_copy(k).wait_send())
    for gather in (weight, latents, output):
        gather.drain()


def attend_kernel(
    npk, owi, li,
    attf, ow, la, ablk, tot,
    recv, s_s, s_r, a_s, a_r, sib_s, sib_r, loc,
):
    pc = Place()
    core = pc.core
    sib = pc.sibling()
    rows = pl.multiple_of(pc.g * 256 + (pc.j // 2) * 16, 16)
    pair = pc.j % 2

    def n_copy(k):
        g, j = pc.plane_peer(k)
        src = npk.at[j % 2, pl.ds(pl.multiple_of(g * 256 + (j // 2) * 16, 16), 16), :]
        return remote(src, recv.at[k], s_s.at[k], s_r.at[k], (g, j * 2 + core))

    each_peer(CHIPS, lambda k: n_copy(k).start())
    big = [
        remote(ow.at[:, :, :, core], ow.at[:, :, :, core], sib_s.at[0], sib_r.at[0], sib),
        remote(la.at[:, :, :, :, core], la.at[:, :, :, :, core], sib_s.at[1], sib_r.at[1], sib),
    ]
    for copy in big:
        copy.start()
    each_peer(CHIPS, lambda k: n_copy(k).wait_recv())
    total = total_slots(npk[pair, pl.ds(rows, 16), :], recv, CHIPS)
    first = total[:, 256:257]
    second = total[:, 320:321]
    both = jnp.concatenate(
        [jnp.broadcast_to(first, (16, 128)), jnp.broadcast_to(second, (16, 128))], axis=1
    )
    tot[...] = both
    ablk[...] = (total[:, :256] / both).astype(BF16)
    spot = attf.at[core, pl.ds(rows, 16), pl.ds(pl.multiple_of(pair * 256, 256), 256)]

    def a_copy(k):
        g, j = pc.plane_peer(k)
        return remote(ablk, spot, a_s.at[k], a_r.at[k], (g, j * 2 + core))

    each_peer(CHIPS, lambda k: a_copy(k).start())
    own = pltpu.make_async_copy(ablk, spot, loc.at[0])
    own.start()
    own.wait()
    each_peer(CHIPS, lambda k: a_copy(k).wait_recv())
    cross = remote(attf.at[core], attf.at[core], sib_s.at[2], sib_r.at[2], sib)
    cross.start()
    cross.wait()
    for copy in big:
        copy.wait()
    each_peer(CHIPS, lambda k: n_copy(k).wait_send())
    each_peer(CHIPS, lambda k: a_copy(k).wait_send())


def sums_kernel(part, out, recv, s_s, s_r):
    pc = Place()

    def copy(k):
        return remote(part, recv.at[k], s_s.at[k], s_r.at[k], (pc.g, pc.group_peer(k)))

    each_peer(GROUP, lambda k: copy(k).start())
    each_peer(GROUP, lambda k: copy(k).wait_recv())
    out[...] = total_slots(part[...], recv, GROUP)
    each_peer(GROUP, lambda k: copy(k).wait_send())


def grad_kernel(
    gap, glp, gh, att, tot,
    gg, gl, ghf,
    recv, recvl, gblk, lblk, g_s, g_r, l_s, l_r, a_s, a_r, x_s, x_r, loc,
):
    pc = Place()
    core = pc.core
    pair = pc.j % 2
    rows = pl.multiple_of((pc.j // 2) * 16, 16)
    partner = (1 - pc.g, pc.t)

    def g_copy(k):
        t = pc.group_peer(k)
        j, c = t // 2, t % 2
        src = gap.at[
            pl.ds(pl.multiple_of((j // 2) * 16, 16), 16),
            pl.ds(pl.multiple_of((c * 2 + j % 2) * 256, 256), 256),
        ]
        return remote(src, recv.at[k], g_s.at[k], g_r.at[k], (pc.g, t))

    def l_copy(k):
        t = pc.group_peer(k)
        return remote(glp.at[t], recvl.at[k], l_s.at[k], l_r.at[k], (pc.g, t))

    each_peer(GROUP, lambda k: g_copy(k).start())
    h_cross = remote(gh, ghf.at[pc.g], x_s.at[0], x_r.at[0], partner)
    h_cross.start()
    each_peer(GROUP, lambda k: l_copy(k).start())
    own = [
        pltpu.make_async_copy(gh, ghf.at[pc.g], loc.at[0]),
        pltpu.make_async_copy(glp.at[pc.t], recvl.at[0], loc.at[1]),
    ]
    for copy in own:
        copy.start()

    each_peer(GROUP, lambda k: g_copy(k).wait_recv())
    mine = gap[pl.ds(rows, 16), pl.ds(pl.multiple_of((core * 2 + pair) * 256, 256), 256)]
    grad = total_slots(mine, recv, GROUP).astype(BF16).astype(F32)
    whole = tot[...]
    prod = grad * att[...].astype(F32)
    first = jnp.sum(prod[:, :128], axis=1, keepdims=True) / whole[:, :1]
    second = jnp.sum(prod[:, 128:], axis=1, keepdims=True) / whole[:, 128:129]
    lane = lax.broadcasted_iota(jnp.int32, (16, 128), 1)
    gblk[:, :256] = (grad / whole).astype(BF16)
    gblk[:, 256:] = jnp.where(lane < 64, first, second).astype(BF16)
    spot = gg.at[pair, pl.ds(pl.multiple_of(pc.g * 256 + rows, 16), 16), :]

    def a_copy(k):
        g, j = pc.plane_peer(k)
        return remote(gblk, spot, a_s.at[k], a_r.at[k], (g, j * 2 + core))

    each_peer(CHIPS, lambda k: a_copy(k).start())
    mine_g = pltpu.make_async_copy(gblk, spot, loc.at[2])
    mine_g.start()

    for copy in own:
        copy.wait()
    each_peer(GROUP, lambda k: l_copy(k).wait_recv())
    lblk[...] = total_slots(recvl[0], recvl, GROUP).astype(BF16)
    l_cross = remote(lblk, gl.at[pc.g], x_s.at[1], x_r.at[1], partner)
    l_cross.start()
    mine_l = pltpu.make_async_copy(lblk, gl.at[pc.g], loc.at[3])
    mine_l.start()
    each_peer(CHIPS, lambda k: a_copy(k).wait_recv())
    l_cross.wait()
    h_cross.wait()
    mine_g.wait()
    mine_l.wait()
    each_peer(GROUP, lambda k: g_copy(k).wait_send())
    each_peer(GROUP, lambda k: l_copy(k).wait_send())
    each_peer(CHIPS, lambda k: a_copy(k).wait_send())


def end_kernel(
    gqp, gp, proj, rinv,
    sq, gw,
    recv, sblk, r1a, r1b, r1c, s1a, s1b, s1c, r2a, r2b, r2c, s2a, s2b, s2c, r3a, r3b, r3c, fin, oth,
    g_s, g_r, a_s, a_r, p_s, p_r, x_s, x_r, loc,
):
    pc = Place()
    core = pc.core
    pair = pc.j % 2
    sib = pc.sibling()
    rows = pl.multiple_of(pc.g * 256 + (pc.j // 2) * 16, 16)
    mine = [pc.x, pc.y, pc.z]
    first, once = (r1a, r1b, r1c), (s1a, s1b, s1c)
    second, twice = (r2a, r2b, r2c), (s2a, s2b, s2c)
    third = (r3a, r3b, r3c)

    def g_copy(k):
        g, j = pc.plane_peer(k)
        src = gqp.at[
            pl.ds(pl.multiple_of(g * 256 + (j // 2) * 16, 16), 16),
            pl.ds(pl.multiple_of((j % 2) * 256, 256), 256),
        ]
        return remote(src, recv.at[k], g_s.at[k], g_r.at[k], (g, j * 2 + core))

    def slab(part, phase, spot):
        order = ORDERS[part]
        index = [spot if axis == order[phase] else slice(None) for axis in range(3) if axis not in order[:phase]]
        if phase == 0:
            return gp.at[(*index, slice(None), pl.ds(*WIDE[part]))]
        return (once, twice)[phase - 1][part].at[tuple(index)]

    def copies(part, phase):
        axis = ORDERS[part][phase]
        for step in (1, 3, 2):
            peer = list(mine)
            peer[axis] = (peer[axis] + step) % 4
            g, j = pc.chip(*peer)
            spot = (part * 3 + phase) * 3 + step - 1
            yield remote(
                slab(part, phase, peer[axis]),
                (first, second, third)[phase][part].at[step],
                p_s.at[spot], p_r.at[spot], (g, j * 2 + core),
            )

    each_peer(CHIPS, lambda k: g_copy(k).start())
    own = []
    for part in range(3):
        for copy in copies(part, 0):
            copy.start()
        copy = pltpu.make_async_copy(
            slab(part, 0, mine[ORDERS[part][0]]), first[part].at[0], loc.at[part]
        )
        copy.start()
        own.append(copy)

    each_peer(CHIPS, lambda k: g_copy(k).wait_recv())
    grad = total_slots(
        gqp[pl.ds(rows, 16), pl.ds(pl.multiple_of(pair * 256, 256), 256)], recv, CHIPS
    )
    sblk[:, :256] = (grad * rinv[:, :1]).astype(BF16)
    ratio = jnp.sum(grad * proj[...], axis=1, keepdims=True)
    sblk[:, 256:] = jnp.broadcast_to(ratio, (16, 128)).astype(BF16)
    spot_q = sq.at[core, pair, pl.ds(rows, 16), :]

    def a_copy(k):
        g, j = pc.plane_peer(k)
        return remote(sblk, spot_q, a_s.at[k], a_r.at[k], (g, j * 2 + core))

    each_peer(CHIPS, lambda k: a_copy(k).start())
    own_q = pltpu.make_async_copy(sblk, spot_q, loc.at[3])
    own_q.start()

    for part in range(3):
        own[part].wait()
        for copy in copies(part, 0):
            copy.wait_recv()
        src, dst = first[part], once[part]

        def add_first(n, carry, src=src, dst=dst):
            a, b = n // 4, n % 4
            dst[a, b] = sum(src[s, a, b].astype(F32) for s in range(4)).astype(BF16)
            return carry

        lax.fori_loop(0, 16, add_first, 0)
        for copy in copies(part, 1):
            copy.start()

    own_q.wait()
    each_peer(CHIPS, lambda k: a_copy(k).wait_recv())
    cross = remote(sq.at[core], sq.at[core], x_s.at[0], x_r.at[0], sib)
    cross.start()

    for part in range(3):
        for copy in copies(part, 1):
            copy.wait_recv()
        src, dst, held = second[part], twice[part], once[part]
        left = [axis for axis in range(3) if axis != ORDERS[part][0]]
        leading = left[0] == ORDERS[part][1]
        here = mine[ORDERS[part][1]]

        def add_second(n, carry, src=src, dst=dst, held=held, leading=leading, here=here):
            base = held[here, n] if leading else held[n, here]
            dst[n] = (base.astype(F32) + sum(src[s, n].astype(F32) for s in range(1, 4))).astype(BF16)
            return carry

        lax.fori_loop(0, 4, add_second, 0)
        for copy in copies(part, 2):
            copy.start()
    for part in range(3):
        for copy in copies(part, 2):
            copy.wait_recv()
        here = mine[ORDERS[part][2]]
        fin[:, pl.ds(*WIDE[part])] = twice[part][here].astype(F32) + sum(
            third[part][s].astype(F32) for s in range(1, 4)
        )
    give = remote(
        fin.at[pl.ds(pl.multiple_of((1 - core) * 16, 16), 16), :], oth, x_s.at[1], x_r.at[1], sib
    )
    give.start()
    gw[core] = fin[pl.ds(pl.multiple_of(core * 16, 16), 16), :]
    give.wait()
    gw[1 - core] = oth[...]
    cross.wait()
    for part in range(3):
        for phase in range(3):
            for copy in copies(part, phase):
                copy.wait_send()
    each_peer(CHIPS, lambda k: g_copy(k).wait_send())
    each_peer(CHIPS, lambda k: a_copy(k).wait_send())


def sems(*counts):
    return [pltpu.SemaphoreType.DMA((n,)) for n in counts]


def call(body, outs, ins_any, outs_any, scratch, aliases=None, name=None):
    def spec(is_any):
        return ANY if is_any else VMEM

    return pl.pallas_call(
        body,
        out_shape=[jax.ShapeDtypeStruct(s, d) for s, d in outs],
        in_specs=[spec(a) for a in ins_any],
        out_specs=[spec(a) for a in outs_any],
        scratch_shapes=scratch,
        input_output_aliases=aliases or {},
        compiler_params=pltpu.CompilerParams(has_side_effects=True, vmem_limit_bytes=40 << 20),
        name=name,
    )


def spread_matrix():
    row = lax.broadcasted_iota(jnp.int32, (1664, 2048), 0)
    col = lax.broadcasted_iota(jnp.int32, (1664, 2048), 1)
    dev, rest = col // 16, col % 16
    core, z, y, x = dev % 2, (dev // 2) % 4, (dev // 8) % 4, dev // 32
    t = ((y * 2 + x % 2) * 4 + z) * 2 + core
    src = ((x // 2) * 64 + t) * 13 + rest
    return ((row == src) & (rest < 13)).astype(BF16)


def local(
    tokens, keep_mask, shard_counts, latents, query_weight, keyval_weight, output_weight,
    project_weight, llm_gain, input_grad,
):
    g = lax.axis_index("grp")
    t = lax.axis_index("tp")
    latent_f32 = latents.astype(F32)

    squares = jnp.sum(latent_f32 * latent_f32, axis=1)
    product = dot(latents, query_weight)
    qpart = jnp.concatenate(
        [
            product.reshape(256, 4, 256).transpose(1, 0, 2),
            jnp.broadcast_to(squares[None, :, None], (4, 256, 128)),
        ],
        axis=2,
    ).astype(BF16)
    padded = jnp.pad(keyval_weight, ((0, 3), (0, 0)))
    wpl = padded.reshape(16, 2, 2, 512).transpose(2, 0, 1, 3).reshape(2, 16, 1024)
    tokp = dot(tokens, spread_matrix()).astype(BF16)
    positions = jnp.arange(256, dtype=jnp.int32)
    valid = (((keep_mask == 1) | (positions == 0)) & (positions < shard_counts[0])).astype(F32)
    val = jnp.broadcast_to(valid[None, :], (8, 256))
    owt = output_weight.T
    lt = latents.T

    wg, tg, vg, qg, owg, lg, proj, rinv = call(
        start_kernel,
        [
            ((4, 4, 4, 2, 16, 1024), BF16),
            ((2, 256, 2048), BF16),
            ((2, 8, 256), F32),
            ((512, 512), BF16),
            ((4, 2, 4, 2, 2, 32, 1024), BF16),
            ((2, 4, 2, 4, 2, 64, 256), BF16),
            ((16, 256), F32),
            ((16, 128), F32),
        ],
        [1, 1, 1, 0, 1, 1],
        [1, 1, 1, 1, 1, 1, 0, 0],
        [pltpu.VMEM((64, 16, 384), BF16), pltpu.VMEM((16, 256), BF16)]
        + sems(27, 27, 27, 27, 27, 27, 64, 64, 64, 64, 3, 3, 6),
        name="start",
    )(wpl, tokp, val, qpart, owt, lt)

    tok = tg.reshape(512, 2048)
    keyval = dot(tok, wg.reshape(2048, 1024)).astype(BF16)
    valid_rows = vg[:, 0, :].reshape(512)
    saved = []
    numer_list = []
    for pair in range(2):
        cols = []
        sums = []
        for half in range(2):
            lower = (pair * 2 + half) * HEAD_DIM
            raw = col_dot(qg[:, lower : lower + HEAD_DIM], keyval[:, lower : lower + HEAD_DIM]) * SCALE
            squash = jnp.tanh(raw / SCORE_CAP)
            weights = jnp.exp(SCORE_CAP * squash) * valid_rows[None, :]
            weights_half = weights.astype(BF16)
            cols.append(dot(weights_half, keyval[:, 512 + lower : 512 + lower + HEAD_DIM]))
            sums.append(jnp.broadcast_to(jnp.sum(weights, axis=1)[:, None], (512, 64)))
            saved.append((squash, weights, weights_half))
        numer_list.append(jnp.concatenate(cols + sums, axis=1))
    npk = jnp.stack(numer_list, axis=0).astype(BF16)

    attf, ow, la, ablk, tot = call(
        attend_kernel,
        [
            ((2, 512, 512), BF16),
            ((4, 2, 4, 2, 2, 32, 1024), BF16),
            ((2, 4, 2, 4, 2, 64, 256), BF16),
            ((16, 256), BF16),
            ((16, 256), F32),
        ],
        [0, 1, 1],
        [1, 1, 1, 0, 0],
        [pltpu.VMEM((64, 16, 384), BF16)] + sems(64, 64, 64, 64, 3, 3, 1),
        aliases={1: 1, 2: 2},
        name="attend",
    )(npk, owg, lg)

    out_t = ow.reshape(4096, 1024)
    lat_t = la.reshape(2, 4096, 256)
    fold = row_dot(out_t, project_weight).astype(BF16)
    lat_own = lax.dynamic_index_in_dim(lat_t, g, 0, keepdims=False)
    att_own = lax.dynamic_slice_in_dim(attf, g * 256, 256, 1)
    hidden = (
        row_dot(lat_own, project_weight) + dot(att_own[0], fold[:512]) + dot(att_own[1], fold[512:])
    ).astype(BF16)
    hidden_f32 = hidden.astype(F32)
    gain_f32 = llm_gain.astype(F32)
    grad_f32 = input_grad.astype(F32)
    scaled_dy = grad_f32 * gain_f32[None, :]
    sums = jnp.concatenate(
        [
            jnp.sum(hidden_f32 * hidden_f32, axis=1).reshape(2, 128),
            jnp.sum(hidden_f32 * scaled_dy, axis=1).reshape(2, 128),
            jnp.zeros((4, 128), F32),
        ],
        axis=0,
    )
    (sums_all,) = call(
        sums_kernel,
        [((8, 128), F32)],
        [0],
        [0],
        [pltpu.VMEM((64, 8, 128), F32)] + sems(64, 64),
        name="sums",
    )(sums)
    hidden_rinv = lax.rsqrt(sums_all[0:2].reshape(256) / D_LLM + 1e-05)
    dot_total = sums_all[2:4].reshape(256)
    normed = hidden_f32 * hidden_rinv[:, None]
    llm_input = (normed * gain_f32[None, :]).astype(BF16)
    gain_part = jnp.sum(grad_f32 * normed, axis=0)
    grad_hidden = (
        hidden_rinv[:, None] * scaled_dy
        - (hidden_rinv**3 / D_LLM * dot_total)[:, None] * hidden_f32
    ).astype(BF16)
    gap = col_dot(grad_hidden, fold).astype(BF16)
    glp = col_dot(project_weight, grad_hidden).astype(BF16).reshape(64, 64, 256)

    gg, gl, ghf = call(
        grad_kernel,
        [((2, 512, 384), BF16), ((2, 64, 256), BF16), ((2, 256, 128), BF16)],
        [0, 1, 1, 0, 0],
        [1, 1, 1],
        [
            pltpu.VMEM((64, 16, 256), BF16),
            pltpu.VMEM((64, 64, 256), BF16),
            pltpu.VMEM((16, 384), BF16),
            pltpu.VMEM((64, 256), BF16),
        ]
        + sems(64, 64, 64, 64, 64, 64, 2, 2, 4),
        name="grad",
    )(gap, glp, grad_hidden, ablk, tot)

    query_list, key_list, value_list = [], [], []
    for head in range(4):
        lower = head * HEAD_DIM
        pair, half = head // 2, head % 2
        squash, weights, weights_half = saved[head]
        grad_head = gg[pair, :, half * 128 : half * 128 + 128]
        delta = gg[pair, :, 256 + half * 64 : 257 + half * 64].astype(F32)
        prob_grad = col_dot(grad_head, keyval[:, 512 + lower : 512 + lower + HEAD_DIM])
        dscore = (weights * (prob_grad - delta) * (1.0 - squash * squash) * SCALE).astype(BF16)
        query_list.append(dot(dscore, keyval[:, lower : lower + HEAD_DIM]))
        key_list.append(row_dot(dscore, qg[:, lower : lower + HEAD_DIM]).astype(BF16))
        value_list.append(row_dot(weights_half, grad_head).astype(BF16))
    gqp = jnp.concatenate(query_list, axis=1).astype(BF16)
    grad_keyval = jnp.concatenate(key_list + value_list, axis=1)
    gp = row_dot(tok, grad_keyval).astype(BF16).reshape(4, 4, 4, 32, 1024)

    widths = [w for _, w in WIDE]
    sq, gw = call(
        end_kernel,
        [((2, 2, 512, 384), BF16), ((2, 16, 1024), F32)],
        [0, 1, 0, 0],
        [1, 0],
        [pltpu.VMEM((64, 16, 256), BF16), pltpu.VMEM((16, 384), BF16)]
        + [pltpu.VMEM((4, 4, 4, 32, w), BF16) for w in widths]
        + [pltpu.VMEM((4, 4, 32, w), BF16) for w in widths]
        + [pltpu.VMEM((4, 4, 32, w), BF16) for w in widths]
        + [pltpu.VMEM((4, 32, w), BF16) for w in widths]
        + [pltpu.VMEM((4, 32, w), BF16) for w in widths]
        + [pltpu.VMEM((32, 1024), F32), pltpu.VMEM((16, 1024), F32)]
        + sems(64, 64, 64, 64, 27, 27, 2, 2, 4),
        name="end",
    )(gqp, gp, proj, rinv)

    grad_keyval_weight = gw[:, :13].reshape(2, 13, 2, 512).transpose(1, 2, 0, 3).reshape(13, 2048)

    gh_all = ghf.reshape(512, 128)
    att_all = jnp.concatenate([attf[0], attf[1]], axis=1)
    mixed = row_dot(att_all, gh_all).astype(BF16)
    grad_project_weight = (
        row_dot(lat_t[0].T, ghf[0]) + row_dot(lat_t[1].T, ghf[1]) + dot(out_t, mixed)
    )
    grad_llm_gain = lax.psum(gain_part, "grp")
    gl_all = gl.transpose(1, 0, 2).reshape(64, 512)
    grad_output_weight = col_dot(att_all.T, gl_all)

    scaled_query = sq[..., :256].transpose(2, 0, 1, 3).reshape(512, 1024)
    ratio = jnp.sum(sq[..., 256].astype(F32), axis=(0, 1))
    lat_feats = lax.dynamic_slice_in_dim(lat_t, t * 64, 64, 1)
    grad_query_weight = dot(lat_feats[0], scaled_query[:256]) + dot(lat_feats[1], scaled_query[256:])
    own_query = lax.dynamic_slice_in_dim(scaled_query, g * 256, 256, 0)
    own_ratio = lax.dynamic_slice_in_dim(ratio, g * 256, 256, 0)
    gl_own = lax.dynamic_index_in_dim(gl, g, 0, keepdims=False)
    square_total = jnp.sum(jnp.square(lat_own.astype(F32)), axis=0)
    latent_rinv = lax.rsqrt(square_total / D_LAT + 1e-06)
    grad_latents = (
        gl_own.T.astype(F32)
        + col_dot(own_query, query_weight)
        - (latent_rinv**3 / D_LAT * own_ratio)[:, None] * latent_f32
    )
    return (
        llm_input,
        grad_latents,
        grad_query_weight,
        grad_keyval_weight,
        grad_output_weight,
        grad_project_weight,
        grad_llm_gain,
    )


def solution(mesh):
    in_specs = (
        P(("grp", "tp"), None),
        P(("grp", "tp")),
        P(("grp", "tp")),
        P("grp", "tp"),
        P("tp", None),
        P(("grp", "tp"), None),
        P(None, "tp"),
        P(None, "tp"),
        P("tp"),
        P("grp", "tp"),
    )
    out_specs = (
        P("grp", "tp"),
        P("grp", "tp"),
        P("tp", None),
        P(("grp", "tp"), None),
        P(None, "tp"),
        P(None, "tp"),
        P("tp"),
    )
    return jax.shard_map(local, mesh=mesh, in_specs=in_specs, out_specs=out_specs, check_vma=False)
```

```python
import functools
import math

import jax
import jax.numpy as jnp
import numpy as np
from jax import lax
from jax.experimental import pallas as pl
from jax.experimental.pallas import tpu as pltpu
from jax.sharding import PartitionSpec as P

D_LAT = 4096
HEAD_DIM = 128
D_LLM = 8192
SCORE_CAP = 5.0
SCALE = 1.0 / math.sqrt(HEAD_DIM)
CHIPS = 64
GROUP = 32

F32 = jnp.float32
BF16 = jnp.bfloat16
MESH = pl.DeviceIdType.MESH
ANY = pl.BlockSpec(memory_space=pl.ANY)
VMEM = pl.BlockSpec(memory_space=pltpu.VMEM)

ORDERS = ((2, 1, 0), (1, 0, 2), (0, 2, 1))
WIDE = ((0, 384), (384, 384), (768, 256))
WIDE_TURNED = ((0, 256), (256, 384), (640, 384))
ROWS_64 = ((0, 16), (16, 32), (48, 16))


def row_dot(left, right):
    return lax.dot_general(left, right, (((0,), (0,)), ((), ())), preferred_element_type=F32)


def col_dot(left, right):
    return lax.dot_general(left, right, (((1,), (1,)), ((), ())), preferred_element_type=F32)


def dot(left, right):
    return jnp.dot(left, right, preferred_element_type=F32)


class Place:
    def __init__(self):
        self.g = lax.axis_index("grp")
        self.t = lax.axis_index("tp")
        self.core = self.t % 2
        self.j = self.t // 2
        self.z = self.j % 4
        self.xl = (self.j // 4) % 2
        self.y = self.j // 8
        self.x = self.g * 2 + self.xl

    def chip(self, x, y, z):
        return x // 2, (y * 2 + x % 2) * 4 + z

    def plane_peer(self, k):
        return self.chip((self.x + k // 16) % 4, (self.y + (k // 4) % 4) % 4, (self.z + k % 4) % 4)

    def group_peer(self, k):
        y = (self.y + k // 8) % 4
        xl = (self.xl + (k // 4) % 2) % 2
        z = (self.z + k % 4) % 4
        return (y * 2 + xl) * 4 + z

    def sibling(self):
        return self.g, self.j * 2 + 1 - self.core


def remote(src, dst, sends, recvs, device):
    return pltpu.make_async_remote_copy(
        src_ref=src, dst_ref=dst, send_sem=sends, recv_sem=recvs, device_id=device, device_id_type=MESH
    )


def each_peer(n, do):
    def body(k, carry):
        do(k)
        return carry

    lax.fori_loop(1, n, body, 0)


class Gather:
    def __init__(self, place, ref, view, sends, recvs):
        self.place, self.ref, self.view, self.sends, self.recvs = place, ref, view, sends, recvs

    def copies(self, phase):
        pc = self.place
        mine = [pc.x, pc.y, pc.z]
        for part, order in enumerate(ORDERS):
            held = list(mine)
            for axis in order[:phase]:
                held[axis] = None
            block = self.view(self.ref, *held, part)
            for step in (1, 3, 2):
                peer = list(mine)
                peer[order[phase]] = (peer[order[phase]] + step) % 4
                g, j = pc.chip(*peer)
                spot = (part * 3 + phase) * 3 + step - 1
                yield remote(
                    block, block, self.sends.at[spot], self.recvs.at[spot], (g, j * 2 + pc.core)
                )

    def start(self, phase):
        for copy in self.copies(phase):
            copy.start()

    def wait(self, phase):
        for copy in self.copies(phase):
            copy.wait_recv()

    def drain(self):
        for phase in range(3):
            for copy in self.copies(phase):
                copy.wait_send()


def pick(value):
    return slice(None) if value is None else value


def halves(x):
    return (slice(None), slice(None)) if x is None else (x // 2, x % 2)


def view_weight(ref, x, y, z, part):
    return ref.at[pick(x), pick(y), pick(z), :, pl.ds(*WIDE[part])]


def view_output(core, ref, x, y, z, part):
    hi, lo = halves(x)
    return ref.at[pick(y), lo, pick(z), core, hi, :, pl.ds(*WIDE_TURNED[part])]


def view_latents(core, ref, x, y, z, part):
    hi, lo = halves(x)
    return ref.at[hi, pick(y), lo, pick(z), core, pl.ds(*ROWS_64[part]), :]


def total_slots(own, slots, n):
    def body(k, total):
        return total + slots[k].astype(F32)

    return lax.fori_loop(1, n, body, own.astype(F32))


class Pushes:
    def __init__(self, n, make):
        self.n, self.make = n, make

    def start(self):
        each_peer(self.n, lambda k: self.make(k).start())

    def landed(self):
        each_peer(self.n, lambda k: self.make(k).wait_recv())

    def drain(self):
        each_peer(self.n, lambda k: self.make(k).wait_send())


def at16(n):
    return pl.ds(pl.multiple_of(n * 16, 16), 16)


def at256(n):
    return pl.ds(pl.multiple_of(n * 256, 256), 256)


def turned(value, dtype=BF16):
    return value.astype(F32).T.astype(dtype)


def whole_kernel(
    tokens, val, qpart, wpl, owt, lt, pw, igrad, gain, qw,
    llm_t, gain_out, gpw, gow_t, gqw, gl_out, gw,
    wg, tokb, tok_t, valb, qx, qsum, recvq, qblk, qg, ow, la, kv, kv_t, fac, half, npk, recvn,
    ablk, attf, pw_t, pwx, fold, foldx, sumx, sumo, sumr, gh_t, ghx, ghp, gap, recvg, glp, recvl,
    lblk, glf, gblk, gg, ds, gqp, recvgq, gkv, sblk, sq, r1a, r1b, r1c, s1a, s1b, s1c,
    r2a, r2b, r2c, s2a, s2b, s2c, r3a, r3b, r3c, fin, oth,
    w_s, w_r, ow_s, ow_r, l_s, l_r, q_s, q_r, qa_s, qa_r, n_s, n_r, a_s, a_r, t_s, t_r,
    g_s, g_r, gl_s, gl_r, gga_s, gga_r, gq_s, gq_r, sqa_s, sqa_r, p_s, p_r, x_s, x_r, loc,
):
    pc = Place()
    core = pc.core
    sib = pc.sibling()
    partner = (1 - pc.g, pc.t)
    mine = [pc.x, pc.y, pc.z]
    pair = pc.j % 2
    own_rows = at16(pc.j // 2)
    all_rows = at16(pc.g * 16 + pc.j // 2)

    def chip_device(g, j):
        return (g, j * 2 + core)

    def over(index, src, dst, device):
        return remote(src, dst, x_s.at[index], x_r.at[index], device)

    barrier = pltpu.get_barrier_semaphore()

    def greet(k):
        pl.semaphore_signal(barrier, inc=1, device_id=chip_device(*pc.plane_peer(k)), device_id_type=MESH)

    pl.semaphore_signal(barrier, inc=1, device_id=sib, device_id_type=MESH)
    each_peer(CHIPS, greet)

    local_copies = [
        pltpu.make_async_copy(
            owt.at[pl.ds(pl.multiple_of(pc.g * 32, 32), 32), :],
            ow.at[pc.y, pc.xl, pc.z, core, pc.g],
            loc.at[0],
        ),
        pltpu.make_async_copy(lt, la.at[pc.g, pc.y, pc.xl, pc.z, core], loc.at[1]),
        pltpu.make_async_copy(val, valb.at[core], loc.at[2]),
        pltpu.make_async_copy(wpl.at[core], wg.at[pc.x, pc.y, pc.z, at16(core)], loc.at[3]),
    ]
    for copy in local_copies:
        copy.start()
    pl.semaphore_wait(barrier, CHIPS)

    w_sib = over(0, wpl.at[1 - core], wg.at[pc.x, pc.y, pc.z, at16(core)], sib)
    w_sib.start()
    q_sib = over(1, qpart.at[1 - core], qx, sib)
    q_sib.start()

    for block in range(16):
        x, y = block // 4, block % 4
        begin = (((x // 2) * 4 + y) * 2 + x % 2) * 104
        base = begin // 128 * 128
        width = min(256, 1664 - base)
        row = lax.broadcasted_iota(jnp.int32, (width, 128), 0)
        col = lax.broadcasted_iota(jnp.int32, (width, 128), 1)
        rest = col & 15
        hit = (row == (begin - base) + (col >> 4) * 13 + rest) & (rest < 13)
        place = jnp.where(hit, 1.0, 0.0).astype(BF16)
        tokb[core, :, pl.ds(block * 128, 128)] = dot(tokens[:, pl.ds(base, width)], place).astype(BF16)

    weight = Gather(pc, wg, view_weight, w_s, w_r)
    output = Gather(pc, ow, functools.partial(view_output, core), ow_s, ow_r)
    latents = Gather(pc, la, functools.partial(view_latents, core), l_s, l_r)
    for copy in local_copies:
        copy.wait()
    w_sib.wait_recv()
    weight.start(0)

    q_sib.wait_recv()
    for p in range(2):
        qsum[p] = (qpart[core, p].astype(F32) + qx[p].astype(F32)).astype(BF16)

    def q_copy(k):
        j = pc.group_peer(k)
        return remote(
            qsum.at[j % 2, at16(j // 2), :], recvq.at[k], q_s.at[k], q_r.at[k], chip_device(pc.g, j)
        )

    q_push = Pushes(GROUP, q_copy)
    q_push.start()
    t_sib = over(2, tokb.at[core], tokb.at[core], sib)
    t_sib.start()
    v_sib = over(3, val, valb.at[core], sib)
    v_sib.start()
    pw_sib = over(4, pw.at[:, 1 - core], pwx, sib)
    pw_sib.start()
    weight.wait(0)
    weight.start(1)
    q_push.landed()
    total = total_slots(qsum[pair, own_rows, :], recvq, GROUP)
    rinv = lax.rsqrt(total[:, 256:] / D_LAT + 1e-06)
    proj = total[:, :256]
    qblk[...] = (proj * rinv[:, :1]).astype(BF16)
    q_spot = qg.at[all_rows, at256(pair)]
    qa_push = Pushes(
        CHIPS,
        lambda k: remote(qblk, q_spot, qa_s.at[k], qa_r.at[k], chip_device(*pc.plane_peer(k))),
    )
    qa_push.start()
    q_own = pltpu.make_async_copy(qblk, q_spot, loc.at[4])
    q_own.start()
    latents.start(0)
    t_sib.wait()
    v_sib.wait()
    weight.wait(1)
    weight.start(2)
    output.start(0)

    for y in range(4):
        pw_t[:, pl.ds(y * 1024, 1024)] = turned(pw[pl.ds(y * 8, 8)].reshape(1024, 128))
    for block in range(4):
        tok_t[pl.ds(block * 512, 512), :] = turned(
            tokb[:, :, pl.ds(block * 512, 512)].reshape(512, 512)
        )
    latents.wait(0)
    weight.wait(2)
    latents.start(1)
    output.wait(0)
    output.start(1)

    tok = tokb[...].reshape(512, 2048)

    def project(n, carry):
        columns = at256(n)
        kv[:, columns] = dot(tok, wg[:, :, :, :, columns].reshape(2048, 256)).astype(BF16)
        return carry

    lax.fori_loop(0, 4, project, 0)
    for n in range(4):
        kv_t[pl.ds(n * 256, 256), :] = turned(kv[:, n * 256 : n * 256 + 256])
    q_own.wait()
    qa_push.landed()

    def n_copy(p, k):
        g, j = pc.plane_peer(k)
        return remote(
            npk.at[j % 2, at16(g * 16 + j // 2), :], recvn.at[k], n_s.at[k], n_r.at[k], chip_device(g, j)
        )

    for p in range(2):
        packed = []
        sums = []
        for side in range(2):
            head = p * 2 + side
            columns = pl.ds(head * 128, 128)
            query = qg[:, columns]
            total = jnp.zeros((1, 512), F32)
            for chunk in range(4):
                slots = pl.ds(chunk * 128, 128)
                raw = col_dot(kv[slots, columns], query)
                squash = jnp.tanh(raw * (SCALE / SCORE_CAP))
                keep = valb[chunk // 2, pl.ds(chunk % 2 * 128, 128), :][:, :1]
                weights = jnp.exp(SCORE_CAP * squash) * keep
                half[head, slots, :] = weights.astype(BF16)
                fac[head, slots, :] = weights * (1.0 - squash * squash) * SCALE
                total = total + jnp.sum(weights, axis=0, keepdims=True)
            packed.append(dot(kv_t[pl.ds(512 + head * 128, 128), :], half[head]))
            sums.append(jnp.broadcast_to(total, (64, 512)))
        npk[p] = jnp.concatenate(packed + sums, axis=0).T.astype(BF16)
    n_push = Pushes(CHIPS, lambda k: n_copy(0, k))
    n_push.start()

    latents.wait(1)
    latents.start(2)
    output.wait(1)
    output.start(2)
    weight.drain()
    n_push.landed()
    total = total_slots(npk[pair, all_rows, :], recvn, CHIPS)
    whole = jnp.concatenate(
        [jnp.broadcast_to(total[:, 256:257], (16, 128)), jnp.broadcast_to(total[:, 320:321], (16, 128))],
        axis=1,
    )
    ablk[...] = (total[:, :256] / whole).astype(BF16)
    a_spot = attf.at[core, all_rows, at256(pair)]
    a_push = Pushes(
        CHIPS,
        lambda k: remote(ablk, a_spot, a_s.at[k], a_r.at[k], chip_device(*pc.plane_peer(k))),
    )
    a_push.start()
    a_own = pltpu.make_async_copy(ablk, a_spot, loc.at[5])
    a_own.start()

    latents.wait(2)
    la_sib = over(5, la.at[:, :, :, :, core], la.at[:, :, :, :, core], sib)
    la_sib.start()
    output.wait(2)
    ow_sib = over(6, ow.at[:, :, :, core], ow.at[:, :, :, core], sib)
    ow_sib.start()
    a_own.wait()
    a_push.landed()
    a_sib = over(7, attf.at[core], attf.at[core], sib)
    a_sib.start()

    la_sib.wait()
    ow_sib.wait()

    def fold_in(n, carry):
        columns = at256(n)
        fold[:, columns] = dot(pw_t[...], ow[:, :, :, :, :, :, columns].reshape(4096, 256)).astype(BF16)
        return carry

    lax.fori_loop(0, 4, fold_in, 0)
    f_sib = over(8, fold.at[:, pl.ds(pl.multiple_of((1 - core) * 512, 512), 512)], foldx, sib)
    f_sib.start()
    hidden = dot(pw_t[...], la[pc.g].reshape(4096, 256))
    a_sib.wait()
    group_rows = at256(pc.g)
    hidden = hidden + col_dot(fold[:, :512], attf[0, group_rows, :])
    hidden = (hidden + col_dot(fold[:, 512:], attf[1, group_rows, :])).astype(BF16).astype(F32)
    grad_y = igrad[...].astype(F32).T
    scaled_dy = grad_y * gain[...]
    sumo[...] = jnp.concatenate(
        [
            jnp.sum(hidden * hidden, axis=0, keepdims=True),
            jnp.sum(hidden * scaled_dy, axis=0, keepdims=True),
            jnp.zeros((6, 256), F32),
        ],
        axis=0,
    )
    s_sib = over(9, sumo, sumx.at[0], sib)
    s_sib.start()
    s_sib.wait()
    sumx[1] = sumx[0] + sumo[...]
    t_push = Pushes(
        GROUP,
        lambda k: remote(sumx.at[1], sumr.at[k], t_s.at[k], t_r.at[k], chip_device(pc.g, pc.group_peer(k))),
    )
    t_push.start()
    t_push.landed()
    total = total_slots(sumx[1], sumr, GROUP)
    hrinv = lax.rsqrt(total[0:1, :] / D_LLM + 1e-05)
    normed = hidden * hrinv
    llm_t[...] = (normed * gain[...]).astype(BF16)
    gain_own = jnp.broadcast_to(jnp.sum(grad_y * normed, axis=1, keepdims=True), (128, 128))
    grad_h = hrinv * scaled_dy - (hrinv * hrinv * hrinv / D_LLM * total[1:2, :]) * hidden
    gh_t[...] = grad_h.astype(BF16)
    h_sib = over(10, gh_t, ghx, sib)
    h_sib.start()
    ghp[pc.g] = gh_t[...]
    h_part = over(11, gh_t, ghp.at[pc.g], partner)
    h_part.start()
    gain_out[pc.g] = gain_own
    gain_part = over(12, gain_out.at[pc.g], gain_out.at[pc.g], partner)
    gain_part.start()

    f_sib.wait()
    own_half = fold[:, pl.ds(pl.multiple_of(core * 512, 512), 512)]
    partial = dot(turned(gh_t[...]), own_half)
    h_sib.wait()
    gap[...] = (partial + dot(turned(ghx[...]), foldx[...])).astype(BF16)

    def g_copy(k):
        j = pc.group_peer(k)
        return remote(
            gap.at[at16(j // 2), at256(j % 2)], recvg.at[k], g_s.at[k], g_r.at[k], chip_device(pc.g, j)
        )

    g_push = Pushes(GROUP, g_copy)
    g_push.start()

    pw_sib.wait()
    for n in range(4):
        part = dot(pw[pl.ds(n * 8, 8), core].reshape(512, 128), gh_t[...])
        part = part + dot(pwx[pl.ds(n * 8, 8)].reshape(512, 128), ghx[...])
        glp[pl.ds(n * 8, 8)] = part.astype(BF16).reshape(8, 64, 256)

    def l_copy(k):
        j = pc.group_peer(k)
        return remote(glp.at[j], recvl.at[k], gl_s.at[k], gl_r.at[k], chip_device(pc.g, j))

    l_push = Pushes(GROUP, l_copy)
    l_push.start()
    g_push.landed()
    grad = total_slots(gap[own_rows, at256(pair)], recvg, GROUP).astype(BF16).astype(F32)
    prod = grad * ablk[...].astype(F32)
    first = jnp.sum(prod[:, :128], axis=1, keepdims=True) / whole[:, :1]
    second = jnp.sum(prod[:, 128:], axis=1, keepdims=True) / whole[:, 128:129]
    lane = lax.broadcasted_iota(jnp.int32, (16, 128), 1)
    gblk[:, :256] = (grad / whole).astype(BF16)
    gblk[:, 256:] = jnp.where(lane < 64, first, second).astype(BF16)
    g_spot = gg.at[pair, all_rows, :]
    gga_push = Pushes(
        CHIPS,
        lambda k: remote(gblk, g_spot, gga_s.at[k], gga_r.at[k], chip_device(*pc.plane_peer(k))),
    )
    gga_push.start()
    g_own = pltpu.make_async_copy(gblk, g_spot, loc.at[6])
    g_own.start()
    l_push.landed()
    lblk[...] = total_slots(glp[pc.j], recvl, GROUP).astype(BF16)
    glf[pc.g] = lblk[...]
    l_part = over(13, lblk, glf.at[pc.g], partner)
    l_part.start()
    g_own.wait()
    gga_push.landed()

    for p in range(2):
        deltas = gg[p, :, 256:].astype(F32).T
        for side in range(2):
            head = p * 2 + side
            columns = pl.ds(head * 128, 128)
            grads = gg[p, :, side * 128 : side * 128 + 128]
            query = qg[:, columns]
            delta = deltas[side * 64 : side * 64 + 1, :]
            for chunk in range(4):
                slots = pl.ds(chunk * 128, 128)
                prob = col_dot(kv[slots, 512 + head * 128 : 640 + head * 128], grads)
                score = (fac[head, slots, :] * (prob - delta)).astype(BF16)
                ds[head, slots, :] = score
                gkv[slots, columns] = dot(score, query).astype(BF16)
                gkv[slots, 512 + head * 128 : 640 + head * 128] = dot(half[head, slots, :], grads).astype(BF16)

    first, once = (r1a, r1b, r1c), (s1a, s1b, s1c)
    second, twice = (r2a, r2b, r2c), (s2a, s2b, s2c)
    third = (r3a, r3b, r3c)

    for x in range(4):
        for n in range(2):
            wg[x, :, :, :, n * 512 : n * 512 + 512] = (
                dot(tok_t[x * 512 : x * 512 + 512, :], gkv[:, n * 512 : n * 512 + 512])
                .astype(BF16)
                .reshape(4, 4, 32, 512)
            )

    def slab(part, phase, spot):
        order = ORDERS[part]
        index = [spot if axis == order[phase] else slice(None) for axis in range(3) if axis not in order[:phase]]
        if phase == 0:
            return wg.at[(*index, slice(None), pl.ds(*WIDE[part]))]
        return (once, twice)[phase - 1][part].at[tuple(index)]

    def copies(part, phase):
        axis = ORDERS[part][phase]
        for step in (1, 3, 2):
            peer = list(mine)
            peer[axis] = (peer[axis] + step) % 4
            spot = (part * 3 + phase) * 3 + step - 1
            yield remote(
                slab(part, phase, peer[axis]),
                (first, second, third)[phase][part].at[step],
                p_s.at[spot], p_r.at[spot], chip_device(*pc.chip(*peer)),
            )

    held_first = []
    for part in range(3):
        for copy in copies(part, 0):
            copy.start()
        copy = pltpu.make_async_copy(slab(part, 0, mine[ORDERS[part][0]]), first[part].at[0], loc.at[7 + part])
        copy.start()
        held_first.append(copy)

    for p in range(2):
        parts = [
            dot(kv_t[pl.ds(head * 128, 128), :], ds[head]) for head in (p * 2, p * 2 + 1)
        ]
        gqp[:, p * 256 : p * 256 + 256] = jnp.concatenate(parts, axis=0).T.astype(BF16)

    def gq_copy(k):
        g, j = pc.plane_peer(k)
        return remote(
            gqp.at[at16(g * 16 + j // 2), at256(j % 2)], recvgq.at[k], gq_s.at[k], gq_r.at[k], chip_device(g, j)
        )

    gq_push = Pushes(CHIPS, gq_copy)
    gq_push.start()

    h_part.wait()
    mixed = [
        (dot(ghp[0], attf[c, :256, :]) + dot(ghp[1], attf[c, 256:, :])).astype(BF16) for c in range(2)
    ]
    mixed_t = jnp.concatenate(mixed, axis=1)
    gh_both = [turned(ghp[n]) for n in range(2)]

    def project_grad(n, carry):
        y, xl = n // 2, n % 2
        gpw[y, xl] = (
            dot(la[0, y, xl].reshape(512, 256), gh_both[0])
            + dot(la[1, y, xl].reshape(512, 256), gh_both[1])
            + col_dot(ow[y, xl].reshape(512, 1024), mixed_t)
        )
        return carry

    lax.fori_loop(0, 8, project_grad, 0)

    gq_push.landed()
    grad = total_slots(gqp[all_rows, at256(pair)], recvgq, CHIPS)
    sblk[:, :256] = (grad * rinv[:, :1]).astype(BF16)
    ratio = jnp.sum(grad * proj, axis=1, keepdims=True) * (rinv * rinv * rinv / D_LAT)
    sblk[:, 256:] = ratio.astype(BF16)
    s_spot = sq.at[core, pair, all_rows, :]
    sqa_push = Pushes(
        CHIPS,
        lambda k: remote(sblk, s_spot, sqa_s.at[k], sqa_r.at[k], chip_device(*pc.plane_peer(k))),
    )
    sqa_push.start()
    s_own = pltpu.make_async_copy(sblk, s_spot, loc.at[10])
    s_own.start()

    for part in range(3):
        held_first[part].wait()
        for copy in copies(part, 0):
            copy.wait_recv()
        src, dst = first[part], once[part]

        def add_first(n, carry, src=src, dst=dst):
            a, b = n // 4, n % 4
            dst[a, b] = sum(src[s, a, b].astype(F32) for s in range(4)).astype(BF16)
            return carry

        lax.fori_loop(0, 16, add_first, 0)
        for copy in copies(part, 1):
            copy.start()

    l_part.wait()
    gow_t[...] = jnp.concatenate(
        [dot(glf[0], attf[c, :256, :]) + dot(glf[1], attf[c, 256:, :]) for c in range(2)], axis=1
    )
    s_own.wait()
    sqa_push.landed()
    s_sib2 = over(14, sq.at[core], sq.at[core], sib)
    s_sib2.start()

    for part in range(3):
        for copy in copies(part, 1):
            copy.wait_recv()
        src, dst, held = second[part], twice[part], once[part]
        left = [axis for axis in range(3) if axis != ORDERS[part][0]]
        leading = left[0] == ORDERS[part][1]
        here = mine[ORDERS[part][1]]

        def add_second(n, carry, src=src, dst=dst, held=held, leading=leading, here=here):
            base = held[here, n] if leading else held[n, here]
            dst[n] = (base.astype(F32) + sum(src[s, n].astype(F32) for s in range(1, 4))).astype(BF16)
            return carry

        lax.fori_loop(0, 4, add_second, 0)
        for copy in copies(part, 2):
            copy.start()

    s_sib2.wait()
    feats = [la[n, pc.y, pc.xl, pc.z, core] for n in range(2)]
    for c in range(2):
        for p in range(2):
            columns = pl.ds((c * 2 + p) * 256, 256)
            gqw[:, columns] = dot(feats[0], sq[c, p, :256, :256]) + dot(feats[1], sq[c, p, 256:, :256])
    mine_f = la[pc.g, pc.y, pc.xl, pc.z, core].astype(F32)
    back = glf[pc.g].astype(F32)
    coef = jnp.zeros((256, 128), F32)
    for c in range(2):
        for p in range(2):
            block = sq[c, p, group_rows, :]
            back = back + col_dot(qw[:, (c * 2 + p) * 256 : (c * 2 + p) * 256 + 256], block[:, :256])
            coef = coef + block[:, 256:].astype(F32)
    gl_out[...] = back - coef.T[:1, :] * mine_f

    for part in range(3):
        for copy in copies(part, 2):
            copy.wait_recv()
        here = mine[ORDERS[part][2]]
        fin[:, pl.ds(*WIDE[part])] = twice[part][here].astype(F32) + sum(
            third[part][s].astype(F32) for s in range(1, 4)
        )
    give = over(15, fin.at[at16(1 - core), :], oth, sib)
    give.start()
    gw[core] = fin[at16(core), :]
    give.wait()
    gw[1 - core] = oth[...]

    gain_part.wait()
    w_sib.wait_send()
    q_sib.wait_send()
    for gather in (latents, output):
        gather.drain()
    for push in (q_push, qa_push, n_push, a_push, t_push, g_push, l_push, gga_push, gq_push, sqa_push):
        push.drain()
    for part in range(3):
        for phase in range(3):
            for copy in copies(part, phase):
                copy.wait_send()


def sems(*counts):
    return [pltpu.SemaphoreType.DMA((n,)) for n in counts]


def local(
    tokens, keep_mask, shard_counts, latents, query_weight, keyval_weight, output_weight,
    project_weight, llm_gain, input_grad,
):
    latent_f32 = latents.astype(F32)
    squares = jnp.sum(latent_f32 * latent_f32, axis=1)
    product = dot(latents, query_weight)
    qpart = jnp.concatenate(
        [
            product.reshape(256, 4, 256).transpose(1, 0, 2),
            jnp.broadcast_to(squares[None, :, None], (4, 256, 128)),
        ],
        axis=2,
    ).astype(BF16)
    padded = jnp.pad(keyval_weight, ((0, 3), (0, 0)))
    wpl = padded.reshape(16, 2, 2, 512).transpose(2, 0, 1, 3).reshape(2, 16, 1024)
    positions = jnp.arange(256, dtype=jnp.int32)
    valid = (((keep_mask == 1) | (positions == 0)) & (positions < shard_counts[0])).astype(F32)
    val = jnp.broadcast_to(valid[:, None], (256, 128))
    gain = jnp.broadcast_to(llm_gain.astype(F32)[:, None], (128, 256))

    widths = [w for _, w in WIDE]
    scratch = [
        ((4, 4, 4, 32, 1024), BF16),
        ((2, 256, 2048), BF16),
        ((2048, 512), BF16),
        ((2, 256, 128), F32),
        ((2, 256, 384), BF16),
        ((2, 256, 384), BF16),
        ((32, 16, 384), BF16),
        ((16, 256), BF16),
        ((512, 512), BF16),
        ((4, 2, 4, 2, 2, 32, 1024), BF16),
        ((2, 4, 2, 4, 2, 64, 256), BF16),
        ((512, 1024), BF16),
        ((1024, 512), BF16),
        ((4, 512, 512), F32),
        ((4, 512, 512), BF16),
        ((2, 512, 384), BF16),
        ((64, 16, 384), BF16),
        ((16, 256), BF16),
        ((2, 512, 512), BF16),
        ((128, 4096), BF16),
        ((32, 64, 128), BF16),
        ((128, 1024), BF16),
        ((128, 512), BF16),
        ((2, 8, 256), F32),
        ((8, 256), F32),
        ((32, 8, 256), F32),
        ((128, 256), BF16),
        ((128, 256), BF16),
        ((2, 128, 256), BF16),
        ((256, 512), BF16),
        ((32, 16, 256), BF16),
        ((32, 64, 256), BF16),
        ((32, 64, 256), BF16),
        ((64, 256), BF16),
        ((2, 64, 256), BF16),
        ((16, 384), BF16),
        ((2, 512, 384), BF16),
        ((4, 512, 512), BF16),
        ((512, 512), BF16),
        ((64, 16, 256), BF16),
        ((512, 1024), BF16),
        ((16, 384), BF16),
        ((2, 2, 512, 384), BF16),
        *[((4, 4, 4, 32, w), BF16) for w in widths],
        *[((4, 4, 32, w), BF16) for w in widths],
        *[((4, 4, 32, w), BF16) for w in widths],
        *[((4, 32, w), BF16) for w in widths],
        *[((4, 32, w), BF16) for w in widths],
        ((32, 1024), F32),
        ((16, 1024), F32),
    ]
    llm_t, gain_out, gpw, gow_t, gqw, gl_out, gw = pl.pallas_call(
        whole_kernel,
        out_shape=[
            jax.ShapeDtypeStruct(s, d)
            for s, d in (
                ((128, 256), BF16),
                ((2, 128, 128), F32),
                ((4, 2, 512, 128), F32),
                ((64, 1024), F32),
                ((64, 1024), F32),
                ((64, 256), F32),
                ((2, 16, 1024), F32),
            )
        ],
        in_specs=[VMEM] * 10,
        out_specs=[VMEM] * 7,
        scratch_shapes=[pltpu.VMEM(s, d) for s, d in scratch]
        + sems(27, 27, 27, 27, 27, 27, 32, 32, 64, 64, 64, 64, 64, 64, 32, 32)
        + sems(32, 32, 32, 32, 64, 64, 64, 64, 64, 64, 27, 27, 16, 16, 11),
        compiler_params=pltpu.CompilerParams(
            has_side_effects=True, vmem_limit_bytes=62 << 20, collective_id=0
        ),
        name="whole",
    )(
        tokens, val, qpart.reshape(2, 2, 256, 384), wpl, output_weight.T, latents.T,
        project_weight.reshape(32, 2, 64, 128), input_grad, gain, query_weight,
    )

    return (
        llm_t.T,
        gl_out.T,
        gqw,
        gw[:, :13].reshape(2, 13, 2, 512).transpose(1, 2, 0, 3).reshape(13, 2048),
        gow_t.T,
        gpw.reshape(4096, 128),
        gain_out[0, :, 0] + gain_out[1, :, 0],
    )


def solution(mesh):
    in_specs = (
        P(("grp", "tp"), None),
        P(("grp", "tp")),
        P(("grp", "tp")),
        P("grp", "tp"),
        P("tp", None),
        P(("grp", "tp"), None),
        P(None, "tp"),
        P(None, "tp"),
        P("tp"),
        P("grp", "tp"),
    )
    out_specs = (
        P("grp", "tp"),
        P("grp", "tp"),
        P("tp", None),
        P(("grp", "tp"), None),
        P(None, "tp"),
        P(None, "tp"),
        P("tp"),
    )
    return jax.shard_map(local, mesh=mesh, in_specs=in_specs, out_specs=out_specs, check_vma=False)
```

```python
import functools
import math

import jax
import jax.numpy as jnp
import numpy as np
from jax import lax
from jax.experimental import pallas as pl
from jax.experimental.pallas import tpu as pltpu
from jax.sharding import PartitionSpec as P

D_LAT = 4096
HEAD_DIM = 128
D_LLM = 8192
SCORE_CAP = 5.0
SCALE = 1.0 / math.sqrt(HEAD_DIM)
CHIPS = 64
GROUP = 32

F32 = jnp.float32
BF16 = jnp.bfloat16
MESH = pl.DeviceIdType.MESH
ANY = pl.BlockSpec(memory_space=pl.ANY)
VMEM = pl.BlockSpec(memory_space=pltpu.VMEM)

ORDERS = ((2, 1, 0), (1, 0, 2), (0, 2, 1))
WIDE = ((0, 384), (384, 384), (768, 256))
COLUMNS_512 = ((0, 256), (256, 128), (384, 128))
ROWS_64 = ((0, 16), (16, 32), (48, 16))


def row_dot(left, right):
    return lax.dot_general(left, right, (((0,), (0,)), ((), ())), preferred_element_type=F32)


def col_dot(left, right):
    return lax.dot_general(left, right, (((1,), (1,)), ((), ())), preferred_element_type=F32)


def dot(left, right):
    return jnp.dot(left, right, preferred_element_type=F32)


class Place:
    def __init__(self):
        self.g = lax.axis_index("grp")
        self.t = lax.axis_index("tp")
        self.core = self.t % 2
        self.j = self.t // 2
        self.z = self.j % 4
        self.xl = (self.j // 4) % 2
        self.y = self.j // 8
        self.x = self.g * 2 + self.xl

    def chip(self, x, y, z):
        return x // 2, (y * 2 + x % 2) * 4 + z

    def plane_peer(self, k):
        return self.chip((self.x + k // 16) % 4, (self.y + (k // 4) % 4) % 4, (self.z + k % 4) % 4)

    def group_peer(self, k):
        y = (self.y + k // 8) % 4
        xl = (self.xl + (k // 4) % 2) % 2
        z = (self.z + k % 4) % 4
        return (y * 2 + xl) * 4 + z

    def sibling(self):
        return self.g, self.j * 2 + 1 - self.core


def remote(src, dst, sends, recvs, device):
    return pltpu.make_async_remote_copy(
        src_ref=src, dst_ref=dst, send_sem=sends, recv_sem=recvs, device_id=device, device_id_type=MESH
    )


def each_peer(n, do):
    def body(k, carry):
        do(k)
        return carry

    lax.fori_loop(1, n, body, 0)


class Gather:
    def __init__(self, place, ref, view, sends, recvs, whole=True):
        self.place, self.ref, self.view, self.sends, self.recvs = place, ref, view, sends, recvs
        self.whole = whole

    def copies(self, phase):
        pc = self.place
        mine = [pc.x, pc.y, pc.z]
        for part, order in enumerate(ORDERS):
            held = list(mine)
            for axis in order[:phase]:
                held[axis] = None
            block = self.view(self.ref, *held, part)
            near = order[phase] == 0 and not self.whole
            for step in (1,) if near else (1, 3, 2):
                peer = list(mine)
                if near:
                    peer[0] = pc.g * 2 + 1 - pc.xl
                else:
                    peer[order[phase]] = (peer[order[phase]] + step) % 4
                g, j = pc.chip(*peer)
                spot = (part * 3 + phase) * 3 + step - 1
                yield remote(
                    block, block, self.sends.at[spot], self.recvs.at[spot], (g, j * 2 + pc.core)
                )

    def start(self, phase):
        for copy in self.copies(phase):
            copy.start()

    def wait(self, phase):
        for copy in self.copies(phase):
            copy.wait_recv()

    def drain(self):
        for phase in range(3):
            for copy in self.copies(phase):
                copy.wait_send()


def pick(value):
    return slice(None) if value is None else value


def halves(x):
    return (slice(None), slice(None)) if x is None else (x // 2, x % 2)


def view_weight(ref, x, y, z, part):
    return ref.at[pick(x), pick(y), pick(z), :, pl.ds(*WIDE[part])]


def view_output(core, ref, x, y, z, part):
    return ref.at[pick(y), slice(None) if x is None else x % 2, pick(z), core, :, pl.ds(*COLUMNS_512[part])]


def view_own(core, ref, x, y, z, part):
    return ref.at[pick(y), slice(None) if x is None else x % 2, pick(z), core, pl.ds(*ROWS_64[part]), :]


def view_latents(core, ref, x, y, z, part):
    hi, lo = halves(x)
    return ref.at[hi, pick(y), lo, pick(z), core, pl.ds(*ROWS_64[part]), :]


def total_slots(own, slots, n):
    def body(k, total):
        return total + slots[k].astype(F32)

    return lax.fori_loop(1, n, body, own.astype(F32))


class Pushes:
    def __init__(self, n, make):
        self.n, self.make = n, make

    def start(self):
        each_peer(self.n, lambda k: self.make(k).start())

    def landed(self):
        each_peer(self.n, lambda k: self.make(k).wait_recv())

    def drain(self):
        each_peer(self.n, lambda k: self.make(k).wait_send())


class PairPushes(Pushes):
    def __init__(self, place, make):
        super().__init__(CHIPS, make)
        self.place = place

    def start_pair(self, p):
        def body(i, carry):
            k = (i // 2) * 4 + (i % 2) * 2 + (self.place.z + p) % 2

            @pl.when(k > 0)
            def _():
                self.make(k).start()

            return carry

        lax.fori_loop(0, 32, body, 0)


def at16(n):
    return pl.ds(pl.multiple_of(n * 16, 16), 16)


def at256(n):
    return pl.ds(pl.multiple_of(n * 256, 256), 256)


def turned(value, dtype=BF16):
    return value.astype(F32).T.astype(dtype)


def whole_kernel(
    tokens, keep, count, lat, qw, keyval_w, owt, lt, pw, igrad, gain_in,
    llm_t, gain_out, gpw, gow_t, gqw, gl_out, gw,
    val, qpart, wpl, gain,
    wg, tokb, tok_t, valb, qx, qsum, recvq, qblk, qg, qo, owe, lown, ltp, la, kv, kv_t, fac, half, npk, recvn,
    ablk, attf, pw_t, pwx, fold, foldx, sumx, sumo, sumr, gh_t, ghx, ghp, gap, recvg, glp, recvl,
    lblk, glf, gblk, gg, ds, gqp, recvgq, gkv, sblk, sq, r1a, r1b, r1c, s1a, s1b, s1c,
    r2a, r2b, r2c, s2a, s2b, s2c, r3a, r3b, r3c, fin, oth,
    w_s, w_r, ow_s, ow_r, lo_s, lo_r, l_s, l_r, q_s, q_r, qa_s, qa_r, n_s, n_r, a_s, a_r, t_s, t_r,
    g_s, g_r, gl_s, gl_r, gga_s, gga_r, gq_s, gq_r, sqa_s, sqa_r, p_s, p_r, x_s, x_r, loc,
):
    pc = Place()
    core = pc.core
    sib = pc.sibling()
    partner = (1 - pc.g, pc.t)
    mine = [pc.x, pc.y, pc.z]
    pair = pc.j % 2
    own_rows = at16(pc.j // 2)
    all_rows = at16(pc.g * 16 + pc.j // 2)

    def chip_device(g, j):
        return (g, j * 2 + core)

    def over(index, src, dst, device):
        return remote(src, dst, x_s.at[index], x_r.at[index], device)

    barrier = pltpu.get_barrier_semaphore()

    def greet(k):
        pl.semaphore_signal(barrier, inc=1, device_id=chip_device(*pc.plane_peer(k)), device_id_type=MESH)

    pl.semaphore_signal(barrier, inc=1, device_id=sib, device_id_type=MESH)
    each_peer(CHIPS, greet)

    rows_f32 = jnp.concatenate([keyval_w[...].astype(F32), jnp.zeros((3, 2048), F32)], axis=0).astype(BF16)
    for c in range(2):
        wpl[c, :, :512] = rows_f32[:, c * 512 : c * 512 + 512]
        wpl[c, :, 512:] = rows_f32[:, 1024 + c * 512 : 1536 + c * 512]
    feats_f32 = lat[...].astype(F32)
    squares = jnp.broadcast_to(jnp.sum(feats_f32 * feats_f32, axis=1, keepdims=True), (256, 128)).astype(BF16)
    for c in range(2):
        for p in range(2):
            columns = (c * 2 + p) * 256
            qpart[c, p, :, :256] = dot(lat[...], qw[:, columns : columns + 256]).astype(BF16)
            qpart[c, p, :, 256:] = squares
    spot = lax.broadcasted_iota(jnp.int32, (1, 256), 1)
    kept = ((keep[...] == 1) | (spot == 0)) & (spot < count[...])
    val[...] = jnp.broadcast_to(jnp.where(kept, 1.0, 0.0), (128, 256)).T
    gain[...] = jnp.broadcast_to(gain_in[...].astype(F32), (256, 128)).T

    group_half = pl.ds(pl.multiple_of(pc.g * 512, 512), 512)
    local_copies = [
        pltpu.make_async_copy(owt.at[:, group_half], owe.at[pc.y, pc.xl, pc.z, core], loc.at[0]),
        pltpu.make_async_copy(lt, lown.at[pc.y, pc.xl, pc.z, core], loc.at[1]),
        pltpu.make_async_copy(lt, ltp.at[pc.g], loc.at[11]),
        pltpu.make_async_copy(val, valb.at[core], loc.at[2]),
        pltpu.make_async_copy(wpl.at[core], wg.at[pc.x, pc.y, pc.z, at16(core)], loc.at[3]),
    ]
    for copy in local_copies:
        copy.start()
    pl.semaphore_wait(barrier, CHIPS)

    w_sib = over(0, wpl.at[1 - core], wg.at[pc.x, pc.y, pc.z, at16(core)], sib)
    w_sib.start()
    q_sib = over(1, qpart.at[1 - core], qx, sib)
    q_sib.start()

    for block in range(16):
        x, y = block // 4, block % 4
        begin = (((x // 2) * 4 + y) * 2 + x % 2) * 104
        base = begin // 128 * 128
        width = min(256, 1664 - base)
        row = lax.broadcasted_iota(jnp.int32, (width, 128), 0)
        col = lax.broadcasted_iota(jnp.int32, (width, 128), 1)
        rest = col & 15
        hit = (row == (begin - base) + (col >> 4) * 13 + rest) & (rest < 13)
        place = jnp.where(hit, 1.0, 0.0).astype(BF16)
        tokb[core, :, pl.ds(block * 128, 128)] = dot(tokens[:, pl.ds(base, width)], place).astype(BF16)

    weight = Gather(pc, wg, view_weight, w_s, w_r)
    output = Gather(pc, owe, functools.partial(view_output, core), ow_s, ow_r, False)
    latents = Gather(pc, lown, functools.partial(view_own, core), lo_s, lo_r, False)
    resampled = Gather(pc, la, functools.partial(view_latents, core), l_s, l_r)
    for copy in local_copies:
        copy.wait()
    w_sib.wait_recv()
    weight.start(0)

    q_sib.wait_recv()
    for p in range(2):
        qsum[p] = (qpart[core, p].astype(F32) + qx[p].astype(F32)).astype(BF16)

    def q_copy(k):
        j = pc.group_peer(k)
        return remote(
            qsum.at[j % 2, at16(j // 2), :], recvq.at[k], q_s.at[k], q_r.at[k], chip_device(pc.g, j)
        )

    q_push = Pushes(GROUP, q_copy)
    q_push.start()
    t_sib = over(2, tokb.at[core], tokb.at[core], sib)
    t_sib.start()
    v_sib = over(3, val, valb.at[core], sib)
    v_sib.start()
    weight.wait(0)
    weight.start(1)
    q_push.landed()
    total = total_slots(qsum[pair, own_rows, :], recvq, GROUP)
    rinv = lax.rsqrt(total[:, 256:] / D_LAT + 1e-06)
    proj = total[:, :256]
    qblk[...] = (proj * rinv[:, :1]).astype(BF16)
    q_spot = qg.at[all_rows, at256(pair)]
    qa_push = Pushes(
        CHIPS,
        lambda k: remote(qblk, q_spot, qa_s.at[k], qa_r.at[k], chip_device(*pc.plane_peer(k))),
    )
    qa_push.start()
    q_own = pltpu.make_async_copy(qblk, q_spot, loc.at[4])
    q_own.start()
    t_sib.wait()
    v_sib.wait()
    weight.wait(1)
    weight.start(2)
    pw_sib = over(4, pw.at[:, 1 - core], pwx, sib)
    pw_sib.start()
    lt_part = over(16, lt, ltp.at[pc.g], partner)
    lt_part.start()

    for y in range(4):
        pw_t[:, pl.ds(y * 1024, 1024)] = turned(pw[pl.ds(y * 8, 8)].reshape(1024, 128))
    for block in range(4):
        tok_t[pl.ds(block * 512, 512), :] = turned(
            tokb[:, :, pl.ds(block * 512, 512)].reshape(512, 512)
        )
    q_push.drain()
    q_own.wait()
    qa_push.landed()
    qo_sib = over(17, qg.at[at256(pc.g), :], qo, sib)
    qo_sib.start()
    latents.start(0)
    output.start(0)
    weight.wait(2)

    tok = tokb[...].reshape(512, 2048)

    def project(n, carry):
        columns = at256(n)
        kv[:, columns] = dot(tok, wg[:, :, :, :, columns].reshape(2048, 256)).astype(BF16)
        return carry

    lax.fori_loop(0, 4, project, 0)
    for n in range(4):
        kv_t[pl.ds(n * 256, 256), :] = turned(kv[:, n * 256 : n * 256 + 256])
    latents.wait(0)
    latents.start(1)
    output.wait(0)
    output.start(1)

    def n_copy(k):
        g, j = pc.plane_peer(k)
        return remote(
            npk.at[j % 2, at16(g * 16 + j // 2), :], recvn.at[k], n_s.at[k], n_r.at[k], chip_device(g, j)
        )

    n_push = PairPushes(pc, n_copy)
    for p in range(2):
        packed = []
        sums = []
        for side in range(2):
            head = p * 2 + side
            columns = pl.ds(head * 128, 128)
            query = qg[:, columns]
            total = jnp.zeros((1, 512), F32)
            for chunk in range(4):
                slots = pl.ds(chunk * 128, 128)
                raw = col_dot(kv[slots, columns], query)
                squash = jnp.tanh(raw * (SCALE / SCORE_CAP))
                keep = valb[chunk // 2, pl.ds(chunk % 2 * 128, 128), :][:, :1]
                weights = jnp.exp(SCORE_CAP * squash) * keep
                half[head, slots, :] = weights.astype(BF16)
                fac[head, slots, :] = weights * (1.0 - squash * squash) * SCALE
                total = total + jnp.sum(weights, axis=0, keepdims=True)
            packed.append(dot(kv_t[pl.ds(512 + head * 128, 128), :], half[head]))
            sums.append(jnp.broadcast_to(total, (64, 512)))
        npk[p] = jnp.concatenate(packed + sums, axis=0).T.astype(BF16)
        n_push.start_pair(p)

    latents.wait(1)
    latents.start(2)
    output.wait(1)
    output.start(2)
    weight.drain()
    qa_push.drain()
    n_push.landed()
    total = total_slots(npk[pair, all_rows, :], recvn, CHIPS)
    whole = jnp.concatenate(
        [jnp.broadcast_to(total[:, 256:257], (16, 128)), jnp.broadcast_to(total[:, 320:321], (16, 128))],
        axis=1,
    )
    ablk[...] = (total[:, :256] / whole).astype(BF16)
    a_spot = attf.at[core, all_rows, at256(pair)]
    a_push = Pushes(
        CHIPS,
        lambda k: remote(ablk, a_spot, a_s.at[k], a_r.at[k], chip_device(*pc.plane_peer(k))),
    )
    a_push.start()
    a_own = pltpu.make_async_copy(ablk, a_spot, loc.at[5])
    a_own.start()

    n_push.drain()
    latents.wait(2)
    lown_sib = over(5, lown.at[:, :, :, core], lown.at[:, :, :, core], sib)
    lown_sib.start()
    output.wait(2)
    owe_sib = over(6, owe.at[:, :, :, core], owe.at[:, :, :, core], sib)
    owe_sib.start()
    lown_sib.wait()
    owe_sib.wait()

    for n in range(2):
        folded = dot(pw_t[...], owe[:, :, :, :, :, n * 256 : n * 256 + 256].reshape(4096, 256))
        fold[:, at256(pc.g * 2 + n)] = folded.astype(BF16)
    f_part = over(18, fold.at[:, group_half], fold.at[:, group_half], partner)
    f_part.start()
    hidden = dot(pw_t[...], lown[...].reshape(4096, 256))
    squares = jnp.zeros((1, 256), F32)
    for y in range(4):
        feats = lown[y].reshape(1024, 256).astype(F32)
        squares = squares + jnp.sum(feats * feats, axis=0, keepdims=True)
    rinv_row = lax.rsqrt(squares / D_LAT + 1e-06)
    a_own.wait()
    a_push.landed()
    a_sib = over(7, attf.at[core], attf.at[core], sib)
    a_sib.start()
    f_part.wait()
    f_sib = over(8, fold.at[:, pl.ds(pl.multiple_of((1 - core) * 512, 512), 512)], foldx, sib)
    f_sib.start()
    a_sib.wait()
    group_rows = at256(pc.g)
    hidden = hidden + col_dot(fold[:, :512], attf[0, group_rows, :])
    hidden = (hidden + col_dot(fold[:, 512:], attf[1, group_rows, :])).astype(BF16).astype(F32)
    grad_y = igrad[...].astype(F32).T
    scaled_dy = grad_y * gain[...]
    square_row = jnp.sum(hidden * hidden, axis=0, keepdims=True)
    inner_row = jnp.sum(hidden * scaled_dy, axis=0, keepdims=True)
    sumo[...] = jnp.concatenate(
        [
            square_row[:, :128], square_row[:, 128:], inner_row[:, :128], inner_row[:, 128:],
            jnp.zeros((4, 128), F32),
        ],
        axis=0,
    )
    s_sib = over(9, sumo, sumx.at[0], sib)
    s_sib.start()
    s_sib.wait()
    sumx[1] = sumx[0] + sumo[...]
    t_push = Pushes(
        GROUP,
        lambda k: remote(sumx.at[1], sumr.at[k], t_s.at[k], t_r.at[k], chip_device(pc.g, pc.group_peer(k))),
    )
    t_push.start()
    lat_out = lt[...].astype(F32) + col_dot(owt[:, :512], attf[0, group_rows, :])
    la[pc.g, pc.y, pc.xl, pc.z, core] = (lat_out + col_dot(owt[:, 512:], attf[1, group_rows, :])).astype(BF16)
    t_push.landed()
    total = total_slots(sumx[1], sumr, GROUP)
    square_row = jnp.concatenate([total[0:1], total[1:2]], axis=1)
    inner_row = jnp.concatenate([total[2:3], total[3:4]], axis=1)
    hrinv = lax.rsqrt(square_row / D_LLM + 1e-05)
    normed = hidden * hrinv
    llm_t[...] = (normed * gain[...]).astype(BF16)
    gain_own = jnp.broadcast_to(jnp.sum(grad_y * normed, axis=1, keepdims=True), (128, 128))
    grad_h = hrinv * scaled_dy - (hrinv * hrinv * hrinv / D_LLM * inner_row) * hidden
    gh_t[...] = grad_h.astype(BF16)
    h_sib = over(10, gh_t, ghx, sib)
    h_sib.start()
    ghp[pc.g] = gh_t[...]
    h_part = over(11, gh_t, ghp.at[pc.g], partner)
    h_part.start()
    gain_out[pc.g] = gain_own
    gain_part = over(12, gain_out.at[pc.g], gain_out.at[pc.g], partner)
    gain_part.start()

    f_sib.wait()
    own_half = fold[:, pl.ds(pl.multiple_of(core * 512, 512), 512)]
    partial = dot(turned(gh_t[...]), own_half)
    h_sib.wait()
    gap[...] = (partial + dot(turned(ghx[...]), foldx[...])).astype(BF16)

    def g_copy(k):
        j = pc.group_peer(k)
        return remote(
            gap.at[at16(j // 2), at256(j % 2)], recvg.at[k], g_s.at[k], g_r.at[k], chip_device(pc.g, j)
        )

    g_push = Pushes(GROUP, g_copy)
    g_push.start()

    resampled.start(0)
    for push in (a_push, t_push):
        push.drain()
    g_push.landed()
    grad = total_slots(gap[own_rows, at256(pair)], recvg, GROUP).astype(BF16).astype(F32)
    gblk[...] = (grad / whole).astype(BF16)
    g_spot = gg.at[all_rows, at256(pair)]
    gga_push = Pushes(
        CHIPS,
        lambda k: remote(gblk, g_spot, gga_s.at[k], gga_r.at[k], chip_device(*pc.plane_peer(k))),
    )
    gga_push.start()
    g_own = pltpu.make_async_copy(gblk, g_spot, loc.at[6])
    g_own.start()

    pw_sib.wait()
    for n in range(4):
        part = dot(pw[pl.ds(n * 8, 8), core].reshape(512, 128), gh_t[...])
        part = part + dot(pwx[pl.ds(n * 8, 8)].reshape(512, 128), ghx[...])
        glp[pl.ds(n * 8, 8)] = part.astype(BF16).reshape(8, 64, 256)

    def l_copy(k):
        j = pc.group_peer(k)
        return remote(glp.at[j], recvl.at[k], gl_s.at[k], gl_r.at[k], chip_device(pc.g, j))

    l_push = Pushes(GROUP, l_copy)
    resampled.wait(0)
    resampled.start(1)
    g_push.drain()
    g_own.wait()
    gga_push.landed()
    l_push.start()

    def gq_copy(k):
        g, j = pc.plane_peer(k)
        return remote(
            gqp.at[at16(g * 16 + j // 2), at256(j % 2)], recvgq.at[k], gq_s.at[k], gq_r.at[k], chip_device(g, j)
        )

    gq_push = PairPushes(pc, gq_copy)
    ones = jnp.ones((8, 128), BF16)
    for p in range(2):
        parts = []
        for head in (p * 2, p * 2 + 1):
            columns = pl.ds(head * 128, 128)
            grads = gg[:, columns]
            prod = grads.astype(F32) * attf[core, :, columns].astype(F32)
            high = prod.astype(BF16)
            rest = (prod - high.astype(F32)).astype(BF16)
            delta = (col_dot(ones, high) + col_dot(ones, rest))[:1, :].astype(BF16).astype(F32)
            for chunk in range(4):
                slots = pl.ds(chunk * 128, 128)
                prob = col_dot(kv[slots, 512 + head * 128 : 640 + head * 128], grads)
                ds[head, slots, :] = (fac[head, slots, :] * (prob - delta)).astype(BF16)
            parts.append(dot(kv_t[pl.ds(head * 128, 128), :], ds[head]))
        gqp[:, p * 256 : p * 256 + 256] = jnp.concatenate(parts, axis=0).T.astype(BF16)
        gq_push.start_pair(p)
    resampled.wait(1)
    resampled.start(2)
    for head in range(4):
        columns = pl.ds(head * 128, 128)
        gkv[:, columns] = dot(ds[head], qg[:, columns]).astype(BF16)
        gkv[:, 512 + head * 128 : 640 + head * 128] = dot(half[head], gg[:, columns]).astype(BF16)

    first, once = (r1a, r1b, r1c), (s1a, s1b, s1c)
    second, twice = (r2a, r2b, r2c), (s2a, s2b, s2c)
    third = (r3a, r3b, r3c)

    for x in range(4):
        for n in range(2):
            wg[x, :, :, :, n * 512 : n * 512 + 512] = (
                dot(tok_t[x * 512 : x * 512 + 512, :], gkv[:, n * 512 : n * 512 + 512])
                .astype(BF16)
                .reshape(4, 4, 32, 512)
            )

    def slab(part, phase, spot):
        order = ORDERS[part]
        index = [spot if axis == order[phase] else slice(None) for axis in range(3) if axis not in order[:phase]]
        if phase == 0:
            return wg.at[(*index, slice(None), pl.ds(*WIDE[part]))]
        return (once, twice)[phase - 1][part].at[tuple(index)]

    def copies(part, phase):
        axis = ORDERS[part][phase]
        for step in (1, 3, 2):
            peer = list(mine)
            peer[axis] = (peer[axis] + step) % 4
            spot = (part * 3 + phase) * 3 + step - 1
            yield remote(
                slab(part, phase, peer[axis]),
                (first, second, third)[phase][part].at[step],
                p_s.at[spot], p_r.at[spot], chip_device(*pc.chip(*peer)),
            )

    held_first = []
    for part in range(3):
        for copy in copies(part, 0):
            copy.start()
        copy = pltpu.make_async_copy(slab(part, 0, mine[ORDERS[part][0]]), first[part].at[0], loc.at[7 + part])
        copy.start()
        held_first.append(copy)

    gga_push.drain()
    l_push.landed()
    lblk[...] = total_slots(glp[pc.j], recvl, GROUP).astype(BF16)
    glf[pc.g] = lblk[...]
    l_part = over(13, lblk, glf.at[pc.g], partner)
    l_part.start()
    gq_push.landed()
    grad = total_slots(gqp[all_rows, at256(pair)], recvgq, CHIPS)
    sblk[...] = (grad * rinv[:, :1]).astype(BF16)
    s_spot = sq.at[core, all_rows, at256(pair)]
    sqa_push = Pushes(
        CHIPS,
        lambda k: remote(sblk, s_spot, sqa_s.at[k], sqa_r.at[k], chip_device(*pc.plane_peer(k))),
    )
    sqa_push.start()
    s_own = pltpu.make_async_copy(sblk, s_spot, loc.at[10])
    s_own.start()

    resampled.wait(2)
    la_sib = over(14, la.at[:, :, :, :, core], la.at[:, :, :, :, core], sib)
    la_sib.start()

    for part in range(3):
        held_first[part].wait()
        for copy in copies(part, 0):
            copy.wait_recv()
        src, dst = first[part], once[part]

        def add_first(n, carry, src=src, dst=dst):
            a, b = n // 4, n % 4
            dst[a, b] = sum(src[s, a, b].astype(F32) for s in range(4)).astype(BF16)
            return carry

        lax.fori_loop(0, 16, add_first, 0)
        for copy in copies(part, 1):
            copy.start()

    l_part.wait()
    l_push.drain()
    gq_push.drain()
    s_own.wait()
    sqa_push.landed()
    s_sib2 = over(15, sq.at[core], sq.at[core], sib)
    s_sib2.start()

    for part in range(3):
        for copy in copies(part, 1):
            copy.wait_recv()
        src, dst, held = second[part], twice[part], once[part]
        left = [axis for axis in range(3) if axis != ORDERS[part][0]]
        leading = left[0] == ORDERS[part][1]
        here = mine[ORDERS[part][1]]

        def add_second(n, carry, src=src, dst=dst, held=held, leading=leading, here=here):
            base = held[here, n] if leading else held[n, here]
            dst[n] = (base.astype(F32) + sum(src[s, n].astype(F32) for s in range(1, 4))).astype(BF16)
            return carry

        lax.fori_loop(0, 4, add_second, 0)
        for copy in copies(part, 2):
            copy.start()

    h_part.wait()
    la_sib.wait()
    gh_both = [turned(ghp[n]) for n in range(2)]

    def project_grad(n, carry):
        y, xl = n // 2, n % 2
        gpw[y, xl] = dot(la[0, y, xl].reshape(512, 256), gh_both[0]) + dot(
            la[1, y, xl].reshape(512, 256), gh_both[1]
        )
        return carry

    lax.fori_loop(0, 8, project_grad, 0)
    for c in range(2):
        gow_t[:, c * 512 : c * 512 + 512] = dot(glf[0], attf[c, :256, :]) + dot(glf[1], attf[c, 256:, :])
    lt_part.wait()
    qo_sib.wait()
    s_sib2.wait()
    back = glf[pc.g].astype(F32)
    ratio = jnp.zeros((256, 128), F32)
    for c in range(2):
        columns = pl.ds(c * 512, 512)
        gqw[:, columns] = dot(ltp[0], sq[c, :256, :]) + dot(ltp[1], sq[c, 256:, :])
        block = sq[c, group_rows, :]
        back = back + col_dot(qw[:, columns], block)
    for block, query in ((sq[core, group_rows, :], qg[group_rows, :]), (sq[1 - core, group_rows, :], qo[...])):
        prod = block.astype(F32) * query.astype(F32)
        for n in range(4):
            ratio = ratio + prod[:, n * 128 : n * 128 + 128]
    coef = jnp.sum(ratio.T, axis=0, keepdims=True) * rinv_row / D_LAT
    gl_out[...] = back - coef * lt[...].astype(F32)
    sqa_push.drain()
    for gather in (latents, output, resampled):
        gather.drain()

    for part in range(3):
        for copy in copies(part, 2):
            copy.wait_recv()
        here = mine[ORDERS[part][2]]
        fin[:, pl.ds(*WIDE[part])] = twice[part][here].astype(F32) + sum(
            third[part][s].astype(F32) for s in range(1, 4)
        )
    give = over(19, fin.at[at16(1 - core), :], oth, sib)
    give.start()
    gw[core] = fin[at16(core), :]
    give.wait()
    gw[1 - core] = oth[...]

    gain_part.wait()
    w_sib.wait_send()
    q_sib.wait_send()
    for part in range(3):
        for phase in range(3):
            for copy in copies(part, phase):
                copy.wait_send()


def sems(*counts):
    return [pltpu.SemaphoreType.DMA((n,)) for n in counts]


def finish_kernel(llm_t, gl_t, gqw, gw, gow_t, gains, gpw, llm, gl, gqw_out, gkw, gow, gpw_out, gain, done):
    copy = pltpu.make_async_copy(gpw, gpw_out, done)
    copy.start()
    llm[...] = turned(llm_t[...])
    gl[...] = gl_t[...].T
    gqw_out[...] = gqw[...]
    gow[...] = gow_t[...].T
    for c in range(2):
        rows = gw[c]
        gkw[:, c * 512 : c * 512 + 512] = rows[:13, :512]
        gkw[:, 1024 + c * 512 : 1536 + c * 512] = rows[:13, 512:]
    gain[...] = (gains[0] + gains[1]).T[0, :]
    copy.wait()


def local(
    tokens, keep_mask, shard_counts, latents, query_weight, keyval_weight, output_weight,
    project_weight, llm_gain, input_grad,
):
    widths = [w for _, w in WIDE]
    scratch = [
        ((256, 128), F32),
        ((2, 2, 256, 384), BF16),
        ((2, 16, 1024), BF16),
        ((128, 256), F32),
        ((4, 4, 4, 32, 1024), BF16),
        ((2, 256, 2048), BF16),
        ((2048, 512), BF16),
        ((2, 256, 128), F32),
        ((2, 256, 384), BF16),
        ((2, 256, 384), BF16),
        ((32, 16, 384), BF16),
        ((16, 256), BF16),
        ((512, 512), BF16),
        ((256, 512), BF16),
        ((4, 2, 4, 2, 64, 512), BF16),
        ((4, 2, 4, 2, 64, 256), BF16),
        ((2, 64, 256), BF16),
        ((2, 4, 2, 4, 2, 64, 256), BF16),
        ((512, 1024), BF16),
        ((1024, 512), BF16),
        ((4, 512, 512), F32),
        ((4, 512, 512), BF16),
        ((2, 512, 384), BF16),
        ((64, 16, 384), BF16),
        ((16, 256), BF16),
        ((2, 512, 512), BF16),
        ((128, 4096), BF16),
        ((32, 64, 128), BF16),
        ((128, 1024), BF16),
        ((128, 512), BF16),
        ((2, 8, 128), F32),
        ((8, 128), F32),
        ((32, 8, 128), F32),
        ((128, 256), BF16),
        ((128, 256), BF16),
        ((2, 128, 256), BF16),
        ((256, 512), BF16),
        ((32, 16, 256), BF16),
        ((32, 64, 256), BF16),
        ((32, 64, 256), BF16),
        ((64, 256), BF16),
        ((2, 64, 256), BF16),
        ((16, 256), BF16),
        ((512, 512), BF16),
        ((4, 512, 512), BF16),
        ((512, 512), BF16),
        ((64, 16, 256), BF16),
        ((512, 1024), BF16),
        ((16, 256), BF16),
        ((2, 512, 512), BF16),
        *[((4, 4, 4, 32, w), BF16) for w in widths],
        *[((4, 4, 32, w), BF16) for w in widths],
        *[((4, 4, 32, w), BF16) for w in widths],
        *[((4, 32, w), BF16) for w in widths],
        *[((4, 32, w), BF16) for w in widths],
        ((32, 1024), F32),
        ((16, 1024), F32),
    ]
    llm_t, gain_out, gpw, gow_t, gqw, gl_out, gw = pl.pallas_call(
        whole_kernel,
        out_shape=[
            jax.ShapeDtypeStruct(s, d)
            for s, d in (
                ((128, 256), BF16),
                ((2, 128, 128), F32),
                ((4, 2, 512, 128), F32),
                ((64, 1024), F32),
                ((64, 1024), F32),
                ((64, 256), F32),
                ((2, 16, 1024), F32),
            )
        ],
        in_specs=[VMEM] * 11,
        out_specs=[VMEM] * 7,
        scratch_shapes=[pltpu.VMEM(s, d) for s, d in scratch]
        + sems(27, 27, 27, 27, 27, 27, 27, 27, 32, 32, 64, 64, 64, 64, 64, 64, 32, 32)
        + sems(32, 32, 32, 32, 64, 64, 64, 64, 64, 64, 27, 27, 20, 20, 12),
        compiler_params=pltpu.CompilerParams(
            has_side_effects=True, vmem_limit_bytes=62 << 20, collective_id=0
        ),
        name="whole",
    )(
        tokens, keep_mask.reshape(1, 256), shard_counts.reshape(1, 1), latents, query_weight, keyval_weight,
        output_weight.T, latents.T, project_weight.reshape(32, 2, 64, 128), input_grad,
        llm_gain.reshape(1, 128),
    )

    return pl.pallas_call(
        finish_kernel,
        out_shape=[
            jax.ShapeDtypeStruct(shape, dtype)
            for shape, dtype in (
                ((256, 128), BF16),
                ((256, 64), F32),
                ((64, 1024), F32),
                ((13, 2048), F32),
                ((1024, 64), F32),
                ((4096, 128), F32),
                ((128,), F32),
            )
        ],
        in_specs=[VMEM] * 6 + [ANY],
        out_specs=[VMEM] * 5 + [ANY, VMEM],
        scratch_shapes=[pltpu.SemaphoreType.DMA],
        compiler_params=pltpu.CompilerParams(vmem_limit_bytes=32 << 20),
        name="finish",
    )(llm_t, gl_out, gqw, gw, gow_t, gain_out, gpw.reshape(4096, 128))


def solution(mesh):
    in_specs = (
        P(("grp", "tp"), None),
        P(("grp", "tp")),
        P(("grp", "tp")),
        P("grp", "tp"),
        P("tp", None),
        P(("grp", "tp"), None),
        P(None, "tp"),
        P(None, "tp"),
        P("tp"),
        P("grp", "tp"),
    )
    out_specs = (
        P("grp", "tp"),
        P("grp", "tp"),
        P("tp", None),
        P(("grp", "tp"), None),
        P(None, "tp"),
        P(None, "tp"),
        P("tp"),
    )
    return jax.shard_map(local, mesh=mesh, in_specs=in_specs, out_specs=out_specs, check_vma=False)
```

```python
import functools
import math

import jax
import jax.numpy as jnp
import numpy as np
from jax import lax
from jax.experimental import pallas as pl
from jax.experimental.pallas import tpu as pltpu
from jax.sharding import PartitionSpec as P

D_LAT = 4096
HEAD_DIM = 128
D_LLM = 8192
SCORE_CAP = 5.0
SCALE = 1.0 / math.sqrt(HEAD_DIM)
CHIPS = 64
GROUP = 32

F32 = jnp.float32
BF16 = jnp.bfloat16
MESH = pl.DeviceIdType.MESH
ANY = pl.BlockSpec(memory_space=pl.ANY)
VMEM = pl.BlockSpec(memory_space=pltpu.VMEM)

ORDERS = ((2, 1, 0), (1, 0, 2), (0, 2, 1))
WIDE = ((0, 384), (384, 384), (768, 256))
COLUMNS_512 = ((0, 256), (256, 128), (384, 128))
ROWS_64 = ((0, 16), (16, 32), (48, 16))


def row_dot(left, right):
    return lax.dot_general(left, right, (((0,), (0,)), ((), ())), preferred_element_type=F32)


def col_dot(left, right):
    return lax.dot_general(left, right, (((1,), (1,)), ((), ())), preferred_element_type=F32)


def dot(left, right):
    return jnp.dot(left, right, preferred_element_type=F32)


class Place:
    def __init__(self):
        self.g = lax.axis_index("grp")
        self.t = lax.axis_index("tp")
        self.core = self.t % 2
        self.j = self.t // 2
        self.z = self.j % 4
        self.xl = (self.j // 4) % 2
        self.y = self.j // 8
        self.x = self.g * 2 + self.xl

    def chip(self, x, y, z):
        return x // 2, (y * 2 + x % 2) * 4 + z

    def plane_peer(self, k):
        return self.chip((self.x + k // 16) % 4, (self.y + (k // 4) % 4) % 4, (self.z + k % 4) % 4)

    def group_peer(self, k):
        y = (self.y + k // 8) % 4
        xl = (self.xl + (k // 4) % 2) % 2
        z = (self.z + k % 4) % 4
        return (y * 2 + xl) * 4 + z

    def sibling(self):
        return self.g, self.j * 2 + 1 - self.core


def remote(src, dst, sends, recvs, device):
    return pltpu.make_async_remote_copy(
        src_ref=src, dst_ref=dst, send_sem=sends, recv_sem=recvs, device_id=device, device_id_type=MESH
    )


class Later:
    def __init__(self, make):
        self.make = make

    def start(self):
        self.make().start()

    def wait_recv(self):
        self.make().wait_recv()

    def wait_send(self):
        self.make().wait_send()


def each_peer(n, do):
    def body(k, carry):
        do(k)
        return carry

    lax.fori_loop(1, n, body, 0)


class Gather:
    def __init__(self, place, ref, view, sends, recvs, whole=True):
        self.place, self.ref, self.view, self.sends, self.recvs = place, ref, view, sends, recvs
        self.whole = whole

    def copies(self, phase):
        pc = self.place
        mine = [pc.x, pc.y, pc.z]
        for part, order in enumerate(ORDERS):
            held = list(mine)
            for axis in order[:phase]:
                held[axis] = None
            block = self.view(self.ref, *held, part)
            near = order[phase] == 0 and not self.whole
            for step in (1,) if near else (1, 3, 2):
                peer = list(mine)
                if near:
                    peer[0] = pc.g * 2 + 1 - pc.xl
                else:
                    peer[order[phase]] = (peer[order[phase]] + step) % 4
                yield self.push(block, (part * 2 + phase) * 3 + step - 1, peer)

    def push(self, block, spot, peer):
        g, j = self.place.chip(*peer)
        device = (g, j * 2 + self.place.core)
        return Later(lambda: remote(block, block, self.sends.at[spot], self.recvs.at[spot], device))

    def last(self, part):
        pc = self.place
        order = ORDERS[part]
        axis = order[2]
        mine = [pc.x, pc.y, pc.z]
        base = 18 + part * 6
        if axis == 0 and not self.whole:
            held = [mine[0], None, None]
            block = self.view(self.ref, *held, part)
            return [self.push(block, base, [pc.g * 2 + 1 - pc.xl, pc.y, pc.z])]

        def at(place, half):
            held = [None, None, None]
            held[axis] = place
            held[order[0]] = Half(half)
            return self.view(self.ref, *held, part)

        here, up, down = mine[axis], (mine[axis] + 1) % 4, (mine[axis] + 3) % 4
        above, below = list(mine), list(mine)
        above[axis], below[axis] = up, down
        return [
            self.push(at(here, 0), base, above),
            self.push(at(here, 1), base + 1, above),
            self.push(at(here, 1), base + 2, below),
            self.push(at(here, 0), base + 3, below),
            self.push(at(down, 0), base + 4, above),
            self.push(at(up, 1), base + 5, below),
        ]

    def start(self, phase):
        if phase < 2:
            for copy in self.copies(phase):
                copy.start()
            return
        for part in range(3):
            copies = self.last(part)
            for n in (0,) if len(copies) == 1 else (0, 2, 1, 3):
                copies[n].start()

    def relay(self):
        for part in range(3):
            copies = self.last(part)
            if len(copies) > 1:
                copies[0].wait_recv()
                copies[4].start()
                copies[2].wait_recv()
                copies[5].start()

    def wait(self, phase):
        if phase < 2:
            for copy in self.copies(phase):
                copy.wait_recv()
            return
        for part in range(3):
            copies = self.last(part)
            for n in (0,) if len(copies) == 1 else (1, 3, 4, 5):
                copies[n].wait_recv()

    def drain(self):
        for phase in range(2):
            for copy in self.copies(phase):
                copy.wait_send()
        for part in range(3):
            for copy in self.last(part):
                copy.wait_send()


class Half:
    def __init__(self, n):
        self.n = n


def pick(value):
    if isinstance(value, Half):
        return slice(value.n * 2, value.n * 2 + 2)
    return slice(None) if value is None else value


def halves(x):
    if isinstance(x, Half):
        return x.n, slice(None)
    return (slice(None), slice(None)) if x is None else (x // 2, x % 2)


def in_group(x):
    if isinstance(x, Half):
        return slice(x.n, x.n + 1)
    return slice(None) if x is None else x % 2


def view_weight(ref, x, y, z, part):
    return ref.at[pick(x), pick(y), pick(z), :, pl.ds(*WIDE[part])]


def view_output(core, ref, x, y, z, part):
    return ref.at[pick(y), in_group(x), pick(z), core, :, pl.ds(*COLUMNS_512[part])]


def view_own(core, ref, x, y, z, part):
    return ref.at[pick(y), in_group(x), pick(z), core, pl.ds(*ROWS_64[part]), :]


def view_latents(core, ref, x, y, z, part):
    hi, lo = halves(x)
    return ref.at[hi, pick(y), lo, pick(z), core, pl.ds(*ROWS_64[part]), :]


def total_slots(own, slots, n):
    def body(k, total):
        return total + slots[k].astype(F32)

    return lax.fori_loop(1, n, body, own.astype(F32))


class Pushes:
    def __init__(self, n, make):
        self.n, self.make = n, make

    def start(self):
        each_peer(self.n, lambda k: self.make(k).start())

    def landed(self):
        each_peer(self.n, lambda k: self.make(k).wait_recv())

    def drain(self):
        each_peer(self.n, lambda k: self.make(k).wait_send())


class PairPushes(Pushes):
    def __init__(self, place, make):
        super().__init__(CHIPS, make)
        self.place = place

    def start_pair(self, p):
        def body(i, carry):
            k = (i // 2) * 4 + (i % 2) * 2 + (self.place.z + p) % 2

            @pl.when(k > 0)
            def _():
                self.make(k).start()

            return carry

        lax.fori_loop(0, 32, body, 0)


def at16(n):
    return pl.ds(pl.multiple_of(n * 16, 16), 16)


def at256(n):
    return pl.ds(pl.multiple_of(n * 256, 256), 256)


def turned(value, dtype=BF16):
    return value.astype(F32).T.astype(dtype)


def whole_kernel(
    keep, count, gain_in, tokens_in, keyval_in, qw_in, lt_in, owt_in, pw_in, igrad_in,
    llm_to, gl_to, gqw_to, gkw_to, gow_to, gpw_to, gain_to,
    tokens, keyval_w, qw, lt, owt, pw, igrad, llm, gl_out, gqw, gkw, gow_t, gpw, gain_row, gain_out,
    val, qpart, wpl, gain,
    wg, tokb, tok_t, valb, qx, qsum, recvq, qblk, qg, qo, owe, lown, ltp, la, kv, kv_t, fac, half, npk, recvn,
    ablk, attf, pw_t, pwx, fold, foldx, sumx, sumo, sumr, gh_t, ghx, ghp, gap, recvg, glp, recvl,
    lblk, glf, gblk, gg, ds, gqp, recvgq, gkv, sblk, sq, r1a, r1b, r1c, s1a, s1b, s1c,
    r2a, r2b, r2c, s2a, s2b, s2c, r3a, r3b, r3c, fara, farb, farc, fin, oth,
    w_s, w_r, ow_s, ow_r, lo_s, lo_r, l_s, l_r, q_s, q_r, qa_s, qa_r, n_s, n_r, a_s, a_r, t_s, t_r,
    g_s, g_r, gl_s, gl_r, gga_s, gga_r, gq_s, gq_r, sqa_s, sqa_r, p_s, p_r, x_s, x_r, loc, out_s,
):
    pc = Place()
    core = pc.core
    sib = pc.sibling()
    partner = (1 - pc.g, pc.t)
    mine = [pc.x, pc.y, pc.z]
    pair = pc.j % 2
    own_rows = at16(pc.j // 2)
    all_rows = at16(pc.g * 16 + pc.j // 2)

    def chip_device(g, j):
        return (g, j * 2 + core)

    def over(index, src, dst, device):
        return remote(src, dst, x_s.at[index], x_r.at[index], device)

    barrier = pltpu.get_barrier_semaphore()

    def greet(k):
        pl.semaphore_signal(barrier, inc=1, device_id=chip_device(*pc.plane_peer(k)), device_id_type=MESH)

    pl.semaphore_signal(barrier, inc=1, device_id=sib, device_id_type=MESH)
    each_peer(CHIPS, greet)

    loads = [
        pltpu.make_async_copy(src, dst, loc.at[12 + n])
        for n, (src, dst) in enumerate(
            (
                (keyval_in, keyval_w), (lt_in, lt), (qw_in, qw), (owt_in, owt),
                (tokens_in, tokens), (pw_in, pw), (igrad_in, igrad),
            )
        )
    ]
    for copy in loads:
        copy.start()
    for copy in loads:
        copy.wait()

    rows_f32 = jnp.concatenate([keyval_w[...].astype(F32), jnp.zeros((3, 2048), F32)], axis=0).astype(BF16)
    for c in range(2):
        wpl[c, :, :512] = rows_f32[:, c * 512 : c * 512 + 512]
        wpl[c, :, 512:] = rows_f32[:, 1024 + c * 512 : 1536 + c * 512]
    feats_f32 = lt[...].astype(F32)
    lat = feats_f32.T.astype(BF16)
    squares = jnp.sum(feats_f32 * feats_f32, axis=0, keepdims=True)
    squares = jnp.broadcast_to(squares, (128, 256)).T.astype(BF16)
    for c in range(2):
        for p in range(2):
            columns = (c * 2 + p) * 256
            qpart[c, p, :, :256] = dot(lat, qw[:, columns : columns + 256]).astype(BF16)
            qpart[c, p, :, 256:] = squares
    spot = lax.broadcasted_iota(jnp.int32, (1, 256), 1)
    kept = ((keep[...] == 1) | (spot == 0)) & (spot < count[...])
    val[...] = jnp.broadcast_to(jnp.where(kept, 1.0, 0.0), (128, 256)).T
    gain[...] = jnp.broadcast_to(gain_in[...].astype(F32), (256, 128)).T

    group_half = pl.ds(pl.multiple_of(pc.g * 512, 512), 512)
    local_copies = [
        pltpu.make_async_copy(owt.at[:, group_half], owe.at[pc.y, pc.xl, pc.z, core], loc.at[0]),
        pltpu.make_async_copy(lt, lown.at[pc.y, pc.xl, pc.z, core], loc.at[1]),
        pltpu.make_async_copy(lt, ltp.at[pc.g], loc.at[11]),
        pltpu.make_async_copy(val, valb.at[core], loc.at[2]),
        pltpu.make_async_copy(wpl.at[core], wg.at[pc.x, pc.y, pc.z, at16(core)], loc.at[3]),
    ]
    for copy in local_copies:
        copy.start()
    pl.semaphore_wait(barrier, CHIPS)

    w_sib = over(0, wpl.at[1 - core], wg.at[pc.x, pc.y, pc.z, at16(core)], sib)
    w_sib.start()
    q_sib = over(1, qpart.at[1 - core], qx, sib)
    q_sib.start()

    for block in range(16):
        x, y = block // 4, block % 4
        begin = (((x // 2) * 4 + y) * 2 + x % 2) * 104
        base = begin // 128 * 128
        width = min(256, 1664 - base)
        row = lax.broadcasted_iota(jnp.int32, (width, 128), 0)
        col = lax.broadcasted_iota(jnp.int32, (width, 128), 1)
        rest = col & 15
        hit = (row == (begin - base) + (col >> 4) * 13 + rest) & (rest < 13)
        place = jnp.where(hit, 1.0, 0.0).astype(BF16)
        tokb[core, :, pl.ds(block * 128, 128)] = dot(tokens[:, pl.ds(base, width)], place).astype(BF16)

    weight = Gather(pc, wg, view_weight, w_s, w_r)
    output = Gather(pc, owe, functools.partial(view_output, core), ow_s, ow_r, False)
    latents = Gather(pc, lown, functools.partial(view_own, core), lo_s, lo_r, False)
    resampled = Gather(pc, la, functools.partial(view_latents, core), l_s, l_r)
    for copy in local_copies:
        copy.wait()
    w_sib.wait_recv()
    weight.start(0)

    q_sib.wait_recv()
    for p in range(2):
        qsum[p] = (qpart[core, p].astype(F32) + qx[p].astype(F32)).astype(BF16)

    def q_copy(k):
        j = pc.group_peer(k)
        return remote(
            qsum.at[j % 2, at16(j // 2), :], recvq.at[k], q_s.at[k], q_r.at[k], chip_device(pc.g, j)
        )

    q_push = Pushes(GROUP, q_copy)
    q_push.start()
    t_sib = over(2, tokb.at[core], tokb.at[core], sib)
    t_sib.start()
    v_sib = over(3, val, valb.at[core], sib)
    v_sib.start()
    weight.wait(0)
    weight.start(1)
    q_push.landed()
    total = total_slots(qsum[pair, own_rows, :], recvq, GROUP)
    rinv = lax.rsqrt(total[:, 256:] / D_LAT + 1e-06)
    proj = total[:, :256]
    qblk[...] = (proj * rinv[:, :1]).astype(BF16)
    q_spot = qg.at[all_rows, at256(pair)]
    qa_push = Pushes(
        CHIPS,
        lambda k: remote(qblk, q_spot, qa_s.at[k], qa_r.at[k], chip_device(*pc.plane_peer(k))),
    )
    qa_push.start()
    q_own = pltpu.make_async_copy(qblk, q_spot, loc.at[4])
    q_own.start()
    t_sib.wait()
    v_sib.wait()
    weight.wait(1)
    weight.start(2)
    pw_sib = over(4, pw.at[:, 1 - core], pwx, sib)
    pw_sib.start()
    lt_part = over(16, lt, ltp.at[pc.g], partner)
    lt_part.start()

    weight.relay()

    for y in range(4):
        pw_t[:, pl.ds(y * 1024, 1024)] = turned(pw[pl.ds(y * 8, 8)].reshape(1024, 128))
    for block in range(4):
        tok_t[pl.ds(block * 512, 512), :] = turned(
            tokb[:, :, pl.ds(block * 512, 512)].reshape(512, 512)
        )
    q_push.drain()
    q_own.wait()
    qa_push.landed()
    qo_sib = over(17, qg.at[at256(pc.g), :], qo, sib)
    qo_sib.start()
    latents.start(0)
    output.start(0)
    weight.wait(2)
    latents.wait(0)
    latents.start(1)
    output.wait(0)
    output.start(1)

    tok = tokb[...].reshape(512, 2048)

    def project(n, carry):
        columns = at256(n)
        kv[:, columns] = dot(tok, wg[:, :, :, :, columns].reshape(2048, 256)).astype(BF16)
        return carry

    lax.fori_loop(0, 4, project, 0)
    for n in range(4):
        kv_t[pl.ds(n * 256, 256), :] = turned(kv[:, n * 256 : n * 256 + 256])

    def n_copy(k):
        g, j = pc.plane_peer(k)
        return remote(
            npk.at[j % 2, at16(g * 16 + j // 2), :], recvn.at[k], n_s.at[k], n_r.at[k], chip_device(g, j)
        )

    n_push = PairPushes(pc, n_copy)
    for p in range(2):
        packed = []
        sums = []
        for side in range(2):
            head = p * 2 + side
            columns = pl.ds(head * 128, 128)
            query = qg[:, columns]
            total = jnp.zeros((1, 512), F32)
            for chunk in range(4):
                slots = pl.ds(chunk * 128, 128)
                raw = col_dot(kv[slots, columns], query)
                squash = jnp.tanh(raw * (SCALE / SCORE_CAP))
                keep = valb[chunk // 2, pl.ds(chunk % 2 * 128, 128), :][:, :1]
                weights = jnp.exp(SCORE_CAP * squash) * keep
                half[head, slots, :] = weights.astype(BF16)
                fac[head, slots, :] = weights * (1.0 - squash * squash) * SCALE
                total = total + jnp.sum(weights, axis=0, keepdims=True)
            packed.append(dot(kv_t[pl.ds(512 + head * 128, 128), :], half[head]))
            sums.append(jnp.broadcast_to(total, (64, 512)))
        npk[p] = jnp.concatenate(packed + sums, axis=0).T.astype(BF16)
        n_push.start_pair(p)
        if p == 0:
            latents.wait(1)
            latents.start(2)
            output.wait(1)
            output.start(2)

    latents.relay()
    output.relay()
    weight.drain()
    qa_push.drain()
    n_push.landed()
    total = total_slots(npk[pair, all_rows, :], recvn, CHIPS)
    whole = jnp.concatenate(
        [jnp.broadcast_to(total[:, 256:257], (16, 128)), jnp.broadcast_to(total[:, 320:321], (16, 128))],
        axis=1,
    )
    ablk[...] = (total[:, :256] / whole).astype(BF16)
    a_spot = attf.at[core, all_rows, at256(pair)]
    a_push = Pushes(
        CHIPS,
        lambda k: remote(ablk, a_spot, a_s.at[k], a_r.at[k], chip_device(*pc.plane_peer(k))),
    )
    a_push.start()
    a_own = pltpu.make_async_copy(ablk, a_spot, loc.at[5])
    a_own.start()

    n_push.drain()
    latents.wait(2)
    lown_sib = over(5, lown.at[:, :, :, core], lown.at[:, :, :, core], sib)
    lown_sib.start()
    output.wait(2)
    owe_sib = over(6, owe.at[:, :, :, core], owe.at[:, :, :, core], sib)
    owe_sib.start()
    lown_sib.wait()
    owe_sib.wait()

    for n in range(2):
        folded = dot(pw_t[...], owe[:, :, :, :, :, n * 256 : n * 256 + 256].reshape(4096, 256))
        fold[:, at256(pc.g * 2 + n)] = folded.astype(BF16)
    f_part = over(18, fold.at[:, group_half], fold.at[:, group_half], partner)
    f_part.start()
    hidden = dot(pw_t[...], lown[...].reshape(4096, 256))
    squares = jnp.zeros((1, 256), F32)
    for y in range(4):
        feats = lown[y].reshape(1024, 256).astype(F32)
        squares = squares + jnp.sum(feats * feats, axis=0, keepdims=True)
    rinv_row = lax.rsqrt(squares / D_LAT + 1e-06)
    a_own.wait()
    a_push.landed()
    a_sib = over(7, attf.at[core], attf.at[core], sib)
    a_sib.start()
    f_part.wait()
    f_sib = over(8, fold.at[:, pl.ds(pl.multiple_of((1 - core) * 512, 512), 512)], foldx, sib)
    f_sib.start()
    a_sib.wait()
    group_rows = at256(pc.g)
    hidden = hidden + col_dot(fold[:, :512], attf[0, group_rows, :])
    hidden = (hidden + col_dot(fold[:, 512:], attf[1, group_rows, :])).astype(BF16).astype(F32)
    grad_y = igrad[...].astype(F32).T
    scaled_dy = grad_y * gain[...]
    square_row = jnp.sum(hidden * hidden, axis=0, keepdims=True)
    inner_row = jnp.sum(hidden * scaled_dy, axis=0, keepdims=True)
    sumo[...] = jnp.concatenate(
        [
            square_row[:, :128], square_row[:, 128:], inner_row[:, :128], inner_row[:, 128:],
            jnp.zeros((4, 128), F32),
        ],
        axis=0,
    )
    s_sib = over(9, sumo, sumx.at[0], sib)
    s_sib.start()
    s_sib.wait()
    sumx[1] = sumx[0] + sumo[...]
    t_push = Pushes(
        GROUP,
        lambda k: remote(sumx.at[1], sumr.at[k], t_s.at[k], t_r.at[k], chip_device(pc.g, pc.group_peer(k))),
    )
    t_push.start()
    lat_out = lt[...].astype(F32) + col_dot(owt[:, :512], attf[0, group_rows, :])
    la[pc.g, pc.y, pc.xl, pc.z, core] = (lat_out + col_dot(owt[:, 512:], attf[1, group_rows, :])).astype(BF16)
    resampled.start(0)
    t_push.landed()
    total = total_slots(sumx[1], sumr, GROUP)
    square_row = jnp.concatenate([total[0:1], total[1:2]], axis=1)
    inner_row = jnp.concatenate([total[2:3], total[3:4]], axis=1)
    hrinv = lax.rsqrt(square_row / D_LLM + 1e-05)
    normed = hidden * hrinv
    llm[...] = turned(normed * gain[...])
    give_llm = pltpu.make_async_copy(llm, llm_to, out_s.at[0])
    give_llm.start()
    gain_own = jnp.broadcast_to(jnp.sum(grad_y * normed, axis=1, keepdims=True), (128, 128))
    grad_h = hrinv * scaled_dy - (hrinv * hrinv * hrinv / D_LLM * inner_row) * hidden
    gh_t[...] = grad_h.astype(BF16)
    h_sib = over(10, gh_t, ghx, sib)
    h_sib.start()
    ghp[pc.g] = gh_t[...]
    h_part = over(11, gh_t, ghp.at[pc.g], partner)
    h_part.start()
    gain_out[pc.g] = gain_own
    gain_part = over(12, gain_out.at[pc.g], gain_out.at[pc.g], partner)
    gain_part.start()

    f_sib.wait()
    own_half = fold[:, pl.ds(pl.multiple_of(core * 512, 512), 512)]
    partial = dot(turned(gh_t[...]), own_half)
    h_sib.wait()
    gap[...] = (partial + dot(turned(ghx[...]), foldx[...])).astype(BF16)

    def g_copy(k):
        j = pc.group_peer(k)
        return remote(
            gap.at[at16(j // 2), at256(j % 2)], recvg.at[k], g_s.at[k], g_r.at[k], chip_device(pc.g, j)
        )

    g_push = Pushes(GROUP, g_copy)
    g_push.start()

    resampled.wait(0)
    resampled.start(1)
    for push in (a_push, t_push):
        push.drain()
    g_push.landed()
    grad = total_slots(gap[own_rows, at256(pair)], recvg, GROUP).astype(BF16).astype(F32)
    gblk[...] = (grad / whole).astype(BF16)
    g_spot = gg.at[all_rows, at256(pair)]
    gga_push = Pushes(
        CHIPS,
        lambda k: remote(gblk, g_spot, gga_s.at[k], gga_r.at[k], chip_device(*pc.plane_peer(k))),
    )
    gga_push.start()
    g_own = pltpu.make_async_copy(gblk, g_spot, loc.at[6])
    g_own.start()

    pw_sib.wait()
    for n in range(4):
        part = dot(pw[pl.ds(n * 8, 8), core].reshape(512, 128), gh_t[...])
        part = part + dot(pwx[pl.ds(n * 8, 8)].reshape(512, 128), ghx[...])
        glp[pl.ds(n * 8, 8)] = part.astype(BF16).reshape(8, 64, 256)

    def l_copy(k):
        j = pc.group_peer(k)
        return remote(glp.at[j], recvl.at[k], gl_s.at[k], gl_r.at[k], chip_device(pc.g, j))

    l_push = Pushes(GROUP, l_copy)
    resampled.wait(1)
    resampled.start(2)
    g_push.drain()
    g_own.wait()
    gga_push.landed()
    l_push.start()

    def gq_copy(k):
        g, j = pc.plane_peer(k)
        return remote(
            gqp.at[at16(g * 16 + j // 2), at256(j % 2)], recvgq.at[k], gq_s.at[k], gq_r.at[k], chip_device(g, j)
        )

    gq_push = PairPushes(pc, gq_copy)
    ones = jnp.ones((8, 128), BF16)
    for p in range(2):
        parts = []
        for head in (p * 2, p * 2 + 1):
            columns = pl.ds(head * 128, 128)
            grads = gg[:, columns]
            prod = grads.astype(F32) * attf[core, :, columns].astype(F32)
            high = prod.astype(BF16)
            rest = (prod - high.astype(F32)).astype(BF16)
            delta = (col_dot(ones, high) + col_dot(ones, rest))[:1, :].astype(BF16).astype(F32)
            for chunk in range(4):
                slots = pl.ds(chunk * 128, 128)
                prob = col_dot(kv[slots, 512 + head * 128 : 640 + head * 128], grads)
                ds[head, slots, :] = (fac[head, slots, :] * (prob - delta)).astype(BF16)
            parts.append(dot(kv_t[pl.ds(head * 128, 128), :], ds[head]))
        gqp[:, p * 256 : p * 256 + 256] = jnp.concatenate(parts, axis=0).T.astype(BF16)
        gq_push.start_pair(p)
    resampled.relay()
    for head in range(4):
        columns = pl.ds(head * 128, 128)
        gkv[:, columns] = dot(ds[head], qg[:, columns]).astype(BF16)
        gkv[:, 512 + head * 128 : 640 + head * 128] = dot(half[head], gg[:, columns]).astype(BF16)

    first, once = (r1a, r1b, r1c), (s1a, s1b, s1c)
    second, twice = (r2a, r2b, r2c), (s2a, s2b, s2c)
    third = (r3a, r3b, r3c)

    for x in range(4):
        for n in range(2):
            wg[x, :, :, :, n * 512 : n * 512 + 512] = (
                dot(tok_t[x * 512 : x * 512 + 512, :], gkv[:, n * 512 : n * 512 + 512])
                .astype(BF16)
                .reshape(4, 4, 32, 512)
            )

    far = (fara, farb, farc)

    def slab(part, spot, half=None):
        axis = ORDERS[part][0]
        index = [pick(None if half is None else Half(half))] + [slice(None)]
        index.insert(axis, spot)
        return wg.at[(*index, slice(None), pl.ds(*WIDE[part]))]

    def ring(part):
        axis = ORDERS[part][0]
        up, down = (mine[axis] + 1) % 4, (mine[axis] + 3) % 4
        beyond = (mine[axis] + 2) % 4
        above, below = list(mine), list(mine)
        above[axis], below[axis] = up, down
        moves = (
            (slab(part, beyond, 0), far[part].at[0], above),
            (slab(part, beyond, 1), far[part].at[1], below),
            (slab(part, up, 1), first[part].at[1, 2:4], above),
            (slab(part, down, 0), first[part].at[2, 0:2], below),
            (slab(part, up, 0), first[part].at[1, 0:2], above),
            (slab(part, down, 1), first[part].at[2, 2:4], below),
        )

        def move(n):
            src, dst, peer = moves[n]
            spot = part * 6 + n
            return remote(src, dst, p_s.at[spot], p_r.at[spot], chip_device(*pc.chip(*peer)))

        return [Later(functools.partial(move, n)) for n in range(6)]

    def add_far(part, spot, half):
        axis = ORDERS[part][0]
        columns = pl.ds(*WIDE[part])

        def body(n, carry):
            index = [half * 2 + n // 4, n % 4]
            index.insert(axis, spot)
            held = wg[(*index, slice(None), columns)].astype(F32)
            wg[(*index, slice(None), columns)] = (held + far[part][half, n // 4, n % 4].astype(F32)).astype(BF16)
            return carry

        lax.fori_loop(0, 8, body, 0)

    def copies(part, phase):
        axis = ORDERS[part][phase]
        for step in (1, 3, 2):
            peer = list(mine)
            peer[axis] = (peer[axis] + step) % 4
            spot = 18 + (part * 2 + phase - 1) * 3 + step - 1
            order = ORDERS[part]
            index = [
                peer[axis] if n == axis else slice(None) for n in range(3) if n not in order[:phase]
            ]
            yield remote(
                (once, twice)[phase - 1][part].at[tuple(index)],
                (second, third)[phase - 1][part].at[step],
                p_s.at[spot], p_r.at[spot], chip_device(*pc.chip(*peer)),
            )

    for part in range(3):
        sent = ring(part)
        for n in range(2):
            sent[n].start()
    held_first = []
    for part in range(3):
        sent = ring(part)
        for n in range(2, 4):
            sent[n].start()
        copy = pltpu.make_async_copy(slab(part, mine[ORDERS[part][0]]), first[part].at[0], loc.at[7 + part])
        copy.start()
        held_first.append(copy)
    for part in range(3):
        sent = ring(part)
        place = mine[ORDERS[part][0]]
        sent[0].wait_recv()
        add_far(part, (place + 1) % 4, 0)
        sent[4].start()
        sent[1].wait_recv()
        add_far(part, (place + 3) % 4, 1)
        sent[5].start()

    gga_push.drain()
    l_push.landed()
    lblk[...] = total_slots(glp[pc.j], recvl, GROUP).astype(BF16)
    glf[pc.g] = lblk[...]
    l_part = over(13, lblk, glf.at[pc.g], partner)
    l_part.start()
    gq_push.landed()
    grad = total_slots(gqp[all_rows, at256(pair)], recvgq, CHIPS)
    sblk[...] = (grad * rinv[:, :1]).astype(BF16)
    s_spot = sq.at[core, all_rows, at256(pair)]
    sqa_push = Pushes(
        CHIPS,
        lambda k: remote(sblk, s_spot, sqa_s.at[k], sqa_r.at[k], chip_device(*pc.plane_peer(k))),
    )
    sqa_push.start()
    s_own = pltpu.make_async_copy(sblk, s_spot, loc.at[10])
    s_own.start()

    resampled.wait(2)
    la_sib = over(14, la.at[:, :, :, :, core], la.at[:, :, :, :, core], sib)
    la_sib.start()

    for part in range(3):
        held_first[part].wait()
        sent = ring(part)
        for n in range(2, 6):
            sent[n].wait_recv()
        src, dst = first[part], once[part]

        def add_first(n, carry, src=src, dst=dst):
            a, b = n // 4, n % 4
            dst[a, b] = sum(src[s, a, b].astype(F32) for s in range(3)).astype(BF16)
            return carry

        lax.fori_loop(0, 16, add_first, 0)
        for copy in copies(part, 1):
            copy.start()

    l_part.wait()
    l_push.drain()
    gq_push.drain()
    s_own.wait()
    sqa_push.landed()
    s_sib2 = over(15, sq.at[core], sq.at[core], sib)
    s_sib2.start()

    for part in range(3):
        for copy in copies(part, 1):
            copy.wait_recv()
        src, dst, held = second[part], twice[part], once[part]
        left = [axis for axis in range(3) if axis != ORDERS[part][0]]
        leading = left[0] == ORDERS[part][1]
        here = mine[ORDERS[part][1]]

        def add_second(n, carry, src=src, dst=dst, held=held, leading=leading, here=here):
            base = held[here, n] if leading else held[n, here]
            dst[n] = (base.astype(F32) + sum(src[s, n].astype(F32) for s in range(1, 4))).astype(BF16)
            return carry

        lax.fori_loop(0, 4, add_second, 0)
        for copy in copies(part, 2):
            copy.start()

    h_part.wait()
    la_sib.wait()
    gh_both = [turned(ghp[n]) for n in range(2)]

    def project_grad(n, carry):
        y, xl = n // 2, n % 2
        gpw[y, xl] = dot(la[0, y, xl].reshape(512, 256), gh_both[0]) + dot(
            la[1, y, xl].reshape(512, 256), gh_both[1]
        )
        return carry

    lax.fori_loop(0, 8, project_grad, 0)
    give_gpw = pltpu.make_async_copy(gpw, gpw_to, out_s.at[1])
    give_gpw.start()
    for c in range(2):
        gow_t[:, c * 512 : c * 512 + 512] = dot(glf[0], attf[c, :256, :]) + dot(glf[1], attf[c, 256:, :])
    give_gow = pltpu.make_async_copy(gow_t, gow_to, out_s.at[2])
    give_gow.start()
    gain_part.wait()
    gain_row[...] = (gain_out[0] + gain_out[1]).T[:1, :]
    give_gain = pltpu.make_async_copy(gain_row, gain_to, out_s.at[3])
    give_gain.start()
    lt_part.wait()
    qo_sib.wait()
    s_sib2.wait()
    back = glf[pc.g].astype(F32)
    ratio = jnp.zeros((256, 128), F32)
    for c in range(2):
        columns = pl.ds(c * 512, 512)
        gqw[:, columns] = dot(ltp[0], sq[c, :256, :]) + dot(ltp[1], sq[c, 256:, :])
        block = sq[c, group_rows, :]
        back = back + col_dot(qw[:, columns], block)
    for block, query in ((sq[core, group_rows, :], qg[group_rows, :]), (sq[1 - core, group_rows, :], qo[...])):
        prod = block.astype(F32) * query.astype(F32)
        for n in range(4):
            ratio = ratio + prod[:, n * 128 : n * 128 + 128]
    coef = jnp.sum(ratio.T, axis=0, keepdims=True) * rinv_row / D_LAT
    gl_out[...] = back - coef * lt[...].astype(F32)
    give_gl = pltpu.make_async_copy(gl_out, gl_to, out_s.at[4])
    give_gl.start()
    give_gqw = pltpu.make_async_copy(gqw, gqw_to, out_s.at[5])
    give_gqw.start()
    sqa_push.drain()
    for gather in (latents, output, resampled):
        gather.drain()

    for part in range(3):
        for copy in copies(part, 2):
            copy.wait_recv()
        here = mine[ORDERS[part][2]]
        fin[:, pl.ds(*WIDE[part])] = twice[part][here].astype(F32) + sum(
            third[part][s].astype(F32) for s in range(1, 4)
        )
    give = over(19, fin.at[at16(1 - core), :], oth, sib)
    give.start()

    def put(plane, rows):
        for n in range(2):
            spot = pl.multiple_of(n * 1024 + plane * 512, 512)
            gkw[:, pl.ds(spot, 512)] = rows[:13, n * 512 : n * 512 + 512]

    put(core, fin[at16(core), :])
    w_sib.wait_send()
    q_sib.wait_send()
    for part in range(3):
        for copy in ring(part):
            copy.wait_send()
        for phase in (1, 2):
            for copy in copies(part, phase):
                copy.wait_send()
    give.wait()
    put(1 - core, oth[...])
    give_gkw = pltpu.make_async_copy(gkw, gkw_to, out_s.at[6])
    give_gkw.start()
    for copy in (give_llm, give_gpw, give_gow, give_gain, give_gl, give_gqw, give_gkw):
        copy.wait()


def sems(*counts):
    return [pltpu.SemaphoreType.DMA((n,)) for n in counts]


def finish_kernel(*refs):
    got, done = refs[-2:]
    n = len(refs) // 3
    moves = []
    for i in range(n):
        src, dst, held = refs[i], refs[n + i], refs[2 * n + i]
        if len(src.shape) > 2:
            moves += [(src.at[m], held.at[m], dst.at[m]) for m in range(src.shape[0])]
        else:
            moves.append((src, held, dst))
    loads = [pltpu.make_async_copy(src, held, got.at[m]) for m, (src, held, dst) in enumerate(moves)]
    stores = [pltpu.make_async_copy(held, dst, done.at[m]) for m, (src, held, dst) in enumerate(moves)]
    for copy in loads:
        copy.start()
    for load, store in zip(loads, stores):
        load.wait()
        store.start()
    for copy in stores:
        copy.wait()


def local(
    tokens, keep_mask, shard_counts, latents, query_weight, keyval_weight, output_weight,
    project_weight, llm_gain, input_grad,
):
    widths = [w for _, w in WIDE]
    scratch = [
        ((256, 1664), BF16),
        ((13, 2048), BF16),
        ((64, 1024), BF16),
        ((64, 256), BF16),
        ((64, 1024), BF16),
        ((32, 2, 64, 128), BF16),
        ((256, 128), BF16),
        ((256, 128), BF16),
        ((64, 256), F32),
        ((64, 1024), F32),
        ((13, 2048), F32),
        ((64, 1024), F32),
        ((4, 2, 512, 128), F32),
        ((1, 128), F32),
        ((2, 128, 128), F32),
        ((256, 128), F32),
        ((2, 2, 256, 384), BF16),
        ((2, 16, 1024), BF16),
        ((128, 256), F32),
        ((4, 4, 4, 32, 1024), BF16),
        ((2, 256, 2048), BF16),
        ((2048, 512), BF16),
        ((2, 256, 128), F32),
        ((2, 256, 384), BF16),
        ((2, 256, 384), BF16),
        ((32, 16, 384), BF16),
        ((16, 256), BF16),
        ((512, 512), BF16),
        ((256, 512), BF16),
        ((4, 2, 4, 2, 64, 512), BF16),
        ((4, 2, 4, 2, 64, 256), BF16),
        ((2, 64, 256), BF16),
        ((2, 4, 2, 4, 2, 64, 256), BF16),
        ((512, 1024), BF16),
        ((1024, 512), BF16),
        ((4, 512, 512), F32),
        ((4, 512, 512), BF16),
        ((2, 512, 384), BF16),
        ((64, 16, 384), BF16),
        ((16, 256), BF16),
        ((2, 512, 512), BF16),
        ((128, 4096), BF16),
        ((32, 64, 128), BF16),
        ((128, 1024), BF16),
        ((128, 512), BF16),
        ((2, 8, 128), F32),
        ((8, 128), F32),
        ((32, 8, 128), F32),
        ((128, 256), BF16),
        ((128, 256), BF16),
        ((2, 128, 256), BF16),
        ((256, 512), BF16),
        ((32, 16, 256), BF16),
        ((32, 64, 256), BF16),
        ((32, 64, 256), BF16),
        ((64, 256), BF16),
        ((2, 64, 256), BF16),
        ((16, 256), BF16),
        ((512, 512), BF16),
        ((4, 512, 512), BF16),
        ((512, 512), BF16),
        ((64, 16, 256), BF16),
        ((512, 1024), BF16),
        ((16, 256), BF16),
        ((2, 512, 512), BF16),
        *[((3, 4, 4, 32, w), BF16) for w in widths],
        *[((4, 4, 32, w), BF16) for w in widths],
        *[((4, 4, 32, w), BF16) for w in widths],
        *[((4, 32, w), BF16) for w in widths],
        *[((4, 32, w), BF16) for w in widths],
        *[((2, 2, 4, 32, w), BF16) for w in widths],
        ((32, 1024), F32),
        ((16, 1024), F32),
    ]
    results = [
        jax.ShapeDtypeStruct(shape, dtype)
        for shape, dtype in (
            ((256, 128), BF16),
            ((64, 256), F32),
            ((64, 1024), F32),
            ((13, 2048), F32),
            ((64, 1024), F32),
            ((4, 2, 512, 128), F32),
            ((1, 128), F32),
        )
    ]
    made = pl.pallas_call(
        whole_kernel,
        out_shape=results,
        in_specs=[VMEM] * 3 + [ANY] * 7,
        out_specs=[ANY] * 7,
        scratch_shapes=[pltpu.VMEM(s, d) for s, d in scratch]
        + sems(36, 36, 36, 36, 36, 36, 36, 36, 32, 32, 64, 64, 64, 64, 64, 64, 32, 32)
        + sems(32, 32, 32, 32, 64, 64, 64, 64, 64, 64, 36, 36, 20, 20, 20, 7),
        compiler_params=pltpu.CompilerParams(
            has_side_effects=True, vmem_limit_bytes=62 << 20, collective_id=0
        ),
        name="whole",
    )(
        keep_mask.reshape(1, 256), shard_counts.reshape(1, 1), llm_gain.reshape(1, 128), tokens,
        keyval_weight, query_weight, latents.T, output_weight.T, project_weight.reshape(32, 2, 64, 128),
        input_grad,
    )
    llm, gl, gqw, gkw, gow, gpw, gain = pl.pallas_call(
        finish_kernel,
        out_shape=results,
        in_specs=[ANY] * 7,
        out_specs=[ANY] * 7,
        scratch_shapes=[pltpu.VMEM(r.shape, r.dtype) for r in results] + sems(10, 10),
        compiler_params=pltpu.CompilerParams(vmem_limit_bytes=62 << 20),
        name="finish",
    )(*made)
    return (llm, gl.T, gqw, gkw, gow.T, gpw.reshape(4096, 128), gain.reshape(128))


def solution(mesh):
    in_specs = (
        P(("grp", "tp"), None),
        P(("grp", "tp")),
        P(("grp", "tp")),
        P("grp", "tp"),
        P("tp", None),
        P(("grp", "tp"), None),
        P(None, "tp"),
        P(None, "tp"),
        P("tp"),
        P("grp", "tp"),
    )
    out_specs = (
        P("grp", "tp"),
        P("grp", "tp"),
        P("tp", None),
        P(("grp", "tp"), None),
        P(None, "tp"),
        P(None, "tp"),
        P("tp"),
    )
    return jax.shard_map(local, mesh=mesh, in_specs=in_specs, out_specs=out_specs, check_vma=False)
```

```python
import functools
import math

import jax
import jax.numpy as jnp
import numpy as np
from jax import lax
from jax.experimental import pallas as pl
from jax.experimental.pallas import tpu as pltpu
from jax.sharding import PartitionSpec as P

D_LAT = 4096
HEAD_DIM = 128
D_LLM = 8192
SCORE_CAP = 5.0
SCALE = 1.0 / math.sqrt(HEAD_DIM)
CHIPS = 64
GROUP = 32

F32 = jnp.float32
BF16 = jnp.bfloat16
MESH = pl.DeviceIdType.MESH
ANY = pl.BlockSpec(memory_space=pl.ANY)
VMEM = pl.BlockSpec(memory_space=pltpu.VMEM)

ORDERS = ((2, 1, 0), (1, 0, 2), (0, 2, 1))
WIDE = ((0, 384), (384, 384), (768, 256))
COLUMNS_512 = ((0, 128), (128, 256), (384, 128))
ROWS_64 = ((0, 16), (16, 32), (48, 16))
ROWS_OWN = ((0, 16), (16, 16), (32, 32))
PAIR_ORDERS = ((2, 1, 0), (1, 0, 2))


def row_dot(left, right):
    return lax.dot_general(left, right, (((0,), (0,)), ((), ())), preferred_element_type=F32)


def col_dot(left, right):
    return lax.dot_general(left, right, (((1,), (1,)), ((), ())), preferred_element_type=F32)


def dot(left, right):
    return jnp.dot(left, right, preferred_element_type=F32)


class Place:
    def __init__(self):
        self.g = lax.axis_index("grp")
        self.t = lax.axis_index("tp")
        self.core = self.t % 2
        self.j = self.t // 2
        self.z = self.j % 4
        self.xl = (self.j // 4) % 2
        self.y = self.j // 8
        self.x = self.g * 2 + self.xl

    def chip(self, x, y, z):
        return x // 2, (y * 2 + x % 2) * 4 + z

    def plane_peer(self, k):
        return self.chip((self.x + k // 16) % 4, (self.y + (k // 4) % 4) % 4, (self.z + k % 4) % 4)

    def group_peer(self, k):
        y = (self.y + k // 8) % 4
        xl = (self.xl + (k // 4) % 2) % 2
        z = (self.z + k % 4) % 4
        return (y * 2 + xl) * 4 + z

    def sibling(self):
        return self.g, self.j * 2 + 1 - self.core


def remote(src, dst, sends, recvs, device):
    return pltpu.make_async_remote_copy(
        src_ref=src, dst_ref=dst, send_sem=sends, recv_sem=recvs, device_id=device, device_id_type=MESH
    )


class Later:
    def __init__(self, make):
        self.make = make

    def start(self):
        self.make().start()

    def wait_recv(self):
        self.make().wait_recv()

    def wait_send(self):
        self.make().wait_send()


def each_peer(n, do):
    def body(k, carry):
        do(k)
        return carry

    lax.fori_loop(1, n, body, 0)


class Gather:
    def __init__(self, place, ref, view, sends, recvs, whole=True, orders=ORDERS, ring=True):
        self.place, self.ref, self.view, self.sends, self.recvs = place, ref, view, sends, recvs
        self.whole, self.orders, self.ring = whole, orders, ring

    def copies(self, phase):
        pc = self.place
        mine = [pc.x, pc.y, pc.z]
        for part, order in enumerate(self.orders):
            held = list(mine)
            for axis in order[:phase]:
                held[axis] = None
            block = self.view(self.ref, *held, part)
            near = order[phase] == 0 and not self.whole
            for step in (1,) if near else (1, 3, 2):
                peer = list(mine)
                if near:
                    peer[0] = pc.g * 2 + 1 - pc.xl
                else:
                    peer[order[phase]] = (peer[order[phase]] + step) % 4
                yield self.push(block, (part * (2 if self.ring else 3) + phase) * 3 + step - 1, peer)

    def push(self, block, spot, peer):
        g, j = self.place.chip(*peer)
        device = (g, j * 2 + self.place.core)
        return Later(lambda: remote(block, block, self.sends.at[spot], self.recvs.at[spot], device))

    def last(self, part):
        pc = self.place
        order = self.orders[part]
        axis = order[2]
        mine = [pc.x, pc.y, pc.z]
        base = 18 + part * 6
        if axis == 0 and not self.whole:
            held = [mine[0], None, None]
            block = self.view(self.ref, *held, part)
            return [self.push(block, base, [pc.g * 2 + 1 - pc.xl, pc.y, pc.z])]

        def at(place, half):
            held = [None, None, None]
            held[axis] = place
            held[order[0]] = Half(half)
            return self.view(self.ref, *held, part)

        here, up, down = mine[axis], (mine[axis] + 1) % 4, (mine[axis] + 3) % 4
        above, below = list(mine), list(mine)
        above[axis], below[axis] = up, down
        return [
            self.push(at(here, 0), base, above),
            self.push(at(here, 1), base + 1, above),
            self.push(at(here, 1), base + 2, below),
            self.push(at(here, 0), base + 3, below),
            self.push(at(down, 0), base + 4, above),
            self.push(at(up, 1), base + 5, below),
        ]

    def start(self, phase):
        if phase < 2 or not self.ring:
            for copy in self.copies(phase):
                copy.start()
            return
        for part in range(3):
            copies = self.last(part)
            for n in (0,) if len(copies) == 1 else (0, 2, 1, 3):
                copies[n].start()

    def relay(self):
        for part in range(3):
            copies = self.last(part)
            if len(copies) > 1:
                copies[0].wait_recv()
                copies[4].start()
                copies[2].wait_recv()
                copies[5].start()

    def wait(self, phase):
        if phase < 2 or not self.ring:
            for copy in self.copies(phase):
                copy.wait_recv()
            return
        for part in range(3):
            copies = self.last(part)
            for n in (0,) if len(copies) == 1 else (1, 3, 4, 5):
                copies[n].wait_recv()

    def drain(self):
        for phase in range(2 if self.ring else 3):
            for copy in self.copies(phase):
                copy.wait_send()
        for part in range(3 if self.ring else 0):
            for copy in self.last(part):
                copy.wait_send()


class Half:
    def __init__(self, n):
        self.n = n


def pick(value):
    if isinstance(value, Half):
        return slice(value.n * 2, value.n * 2 + 2)
    return slice(None) if value is None else value


def halves(x):
    if isinstance(x, Half):
        return x.n, slice(None)
    return (slice(None), slice(None)) if x is None else (x // 2, x % 2)


def in_group(x):
    if isinstance(x, Half):
        return slice(x.n, x.n + 1)
    return slice(None) if x is None else x % 2


def view_weight(ref, x, y, z, part):
    return ref.at[pick(x), pick(y), pick(z), :, pl.ds(*WIDE[part])]


def view_output(ref, x, y, z, part):
    return ref.at[pick(y), in_group(x), pick(z), :, pl.ds(*COLUMNS_512[part])]


def view_own(ref, x, y, z, part):
    return ref.at[pick(y), in_group(x), pick(z), pl.ds(*ROWS_OWN[part]), :]


def view_rows(ref, x, y, z, part):
    hi, lo = halves(x)
    up, pair = halves(z)
    return ref.at[hi, pick(y), lo, up, pair, :, pl.ds(part * 128, 128)]


def view_latents(core, ref, x, y, z, part):
    hi, lo = halves(x)
    return ref.at[hi, pick(y), lo, pick(z), core, pl.ds(*ROWS_64[part]), :]


def total_slots(own, slots, n):
    def body(k, total):
        return total + slots[k].astype(F32)

    return lax.fori_loop(1, n, body, own.astype(F32))


class Pushes:
    def __init__(self, n, make):
        self.n, self.make = n, make

    def start(self):
        each_peer(self.n, lambda k: self.make(k).start())

    def landed(self):
        each_peer(self.n, lambda k: self.make(k).wait_recv())

    def drain(self):
        each_peer(self.n, lambda k: self.make(k).wait_send())


class PairPushes(Pushes):
    def __init__(self, place, make):
        super().__init__(CHIPS, make)
        self.place = place

    def start_pair(self, p):
        def body(i, carry):
            k = (i // 2) * 4 + (i % 2) * 2 + (self.place.z + p) % 2

            @pl.when(k > 0)
            def _():
                self.make(k).start()

            return carry

        lax.fori_loop(0, 32, body, 0)


def at16(n):
    return pl.ds(pl.multiple_of(n * 16, 16), 16)


def at256(n):
    return pl.ds(pl.multiple_of(n * 256, 256), 256)


def heads_of(ref, pair, side):
    return ref[:, :, :, :, pair, :, side * 128 : side * 128 + 128].reshape(512, 128)


def turned(value, dtype=BF16):
    return value.astype(F32).T.astype(dtype)


def whole_kernel(
    keep, count, gain_in, tokens_in, keyval_in, qw_in, lt_in, owt_in, pw_in, igrad_in,
    llm_to, gl_to, gqw_to, gkw_to, gow_to, gpw_to, gain_to,
    tokens, keyval_w, qw, lt, owt, pw, igrad, llm, gl_out, gqw, gkw, gow_t, gpw, gain_row, gain_out,
    val, qpart, wpl, gain,
    wg, tokb, tok_t, valb, qx, qsum, recvq, qg, qo, owe, lown, ltp, la, kv, kv_t, fac, half, npk, recvn,
    ablk, attf, pw_t, pwx, lat_s, lat_x, fold_s, fold_x, fold, foldx, sumx, sumo, sumr, gh_t, ghx, ghp, gap, recvg, glp, recvl,
    lblk, glf, gblk, gg, ds, gqp, recvgq, gkv, sq, r1a, r1b, r1c, s1a, s1b, s1c,
    r2a, r2b, r2c, s2a, s2b, s2c, r3a, r3b, r3c, fara, farb, farc, fin, oth,
    w_s, w_r, ow_s, ow_r, lo_s, lo_r, l_s, l_r, q_s, q_r, qa_s, qa_r, n_s, n_r, a_s, a_r, t_s, t_r,
    g_s, g_r, gl_s, gl_r, gga_s, gga_r, gq_s, gq_r, sqa_s, sqa_r, p_s, p_r, x_s, x_r, loc, out_s,
):
    pc = Place()
    core = pc.core
    sib = pc.sibling()
    partner = (1 - pc.g, pc.t)
    mine = [pc.x, pc.y, pc.z]
    pair = pc.j % 2
    own_rows = at16(pc.j // 2)
    all_rows = at16(pc.g * 16 + pc.j // 2)

    def chip_device(g, j):
        return (g, j * 2 + core)

    def over(index, src, dst, device):
        return remote(src, dst, x_s.at[index], x_r.at[index], device)

    barrier = pltpu.get_barrier_semaphore()

    def greet(k):
        pl.semaphore_signal(barrier, inc=1, device_id=chip_device(*pc.plane_peer(k)), device_id_type=MESH)

    pl.semaphore_signal(barrier, inc=1, device_id=sib, device_id_type=MESH)
    each_peer(CHIPS, greet)

    loads = [
        pltpu.make_async_copy(src, dst, loc.at[12 + n])
        for n, (src, dst) in enumerate(
            (
                (keyval_in, keyval_w), (lt_in, lt), (qw_in, qw), (owt_in, owt),
                (tokens_in, tokens), (pw_in, pw), (igrad_in, igrad),
            )
        )
    ]
    for copy in loads:
        copy.start()
    loads[0].wait()

    rows_f32 = jnp.concatenate([keyval_w[...].astype(F32), jnp.zeros((3, 2048), F32)], axis=0).astype(BF16)
    for c in range(2):
        wpl[c, :, :512] = rows_f32[:, c * 512 : c * 512 + 512]
        wpl[c, :, 512:] = rows_f32[:, 1024 + c * 512 : 1536 + c * 512]
    w_own = pltpu.make_async_copy(wpl.at[core], wg.at[pc.x, pc.y, pc.z, at16(core)], loc.at[3])
    w_own.start()
    pl.semaphore_wait(barrier, CHIPS)

    w_sib = over(0, wpl.at[1 - core], wg.at[pc.x, pc.y, pc.z, at16(core)], sib)
    w_sib.start()

    for copy in loads[1:]:
        copy.wait()
    feats_f32 = lt[...].astype(F32)
    lat = feats_f32.T.astype(BF16)
    squares = jnp.sum(feats_f32 * feats_f32, axis=0, keepdims=True)
    squares = jnp.broadcast_to(squares, (128, 256)).T.astype(BF16)
    for c in range(2):
        for p in range(2):
            columns = (c * 2 + p) * 256
            qpart[c, p, :, :256] = dot(lat, qw[:, columns : columns + 256]).astype(BF16)
            qpart[c, p, :, 256:] = squares
    spot = lax.broadcasted_iota(jnp.int32, (1, 256), 1)
    kept = ((keep[...] == 1) | (spot == 0)) & (spot < count[...])
    val[...] = jnp.broadcast_to(jnp.where(kept, 1.0, 0.0), (128, 256)).T
    gain[...] = jnp.broadcast_to(gain_in[...].astype(F32), (256, 128)).T

    q_sib = over(1, qpart.at[1 - core], qx, sib)
    q_sib.start()
    weight = Gather(pc, wg, view_weight, w_s, w_r)
    output = Gather(pc, owe, view_output, ow_s, ow_r, False)
    latents = Gather(pc, lown, view_own, lo_s, lo_r, False)
    resampled = Gather(pc, la, functools.partial(view_latents, core), l_s, l_r)
    w_own.wait()
    w_sib.wait_recv()
    weight.start(0)
    group_half = pl.ds(pl.multiple_of(pc.g * 512, 512), 512)
    local_copies = [
        pltpu.make_async_copy(owt.at[:, group_half], owe.at[pc.y, pc.xl, pc.z], loc.at[0]),
        pltpu.make_async_copy(lt, lown.at[pc.y, pc.xl, pc.z], loc.at[1]),
        pltpu.make_async_copy(lt, ltp.at[pc.g], loc.at[11]),
        pltpu.make_async_copy(val, valb.at[core], loc.at[2]),
    ]
    for copy in local_copies:
        copy.start()

    q_sib.wait_recv()
    for p in range(2):
        qsum[p] = (qpart[core, p].astype(F32) + qx[p].astype(F32)).astype(BF16)

    def q_copy(k):
        j = pc.group_peer(k)
        return remote(
            qsum.at[j % 2, at16(j // 2), :], recvq.at[k], q_s.at[k], q_r.at[k], chip_device(pc.g, j)
        )

    q_push = Pushes(GROUP, q_copy)
    q_push.start()

    for block in range(16):
        x, y = block // 4, block % 4
        begin = (((x // 2) * 4 + y) * 2 + x % 2) * 104
        base = begin // 128 * 128
        width = min(256, 1664 - base)
        row = lax.broadcasted_iota(jnp.int32, (width, 128), 0)
        col = lax.broadcasted_iota(jnp.int32, (width, 128), 1)
        rest = col & 15
        hit = (row == (begin - base) + (col >> 4) * 13 + rest) & (rest < 13)
        place = jnp.where(hit, 1.0, 0.0).astype(BF16)
        tokb[core, :, pl.ds(block * 128, 128)] = dot(tokens[:, pl.ds(base, width)], place).astype(BF16)

    t_sib = over(2, tokb.at[core], tokb.at[core], sib)
    t_sib.start()
    for copy in local_copies:
        copy.wait()
    latents.start(0)
    output.start(0)
    v_sib = over(3, val, valb.at[core], sib)
    v_sib.start()
    pw_sib = over(4, pw.at[:, 1 - core], pwx, sib)
    pw_sib.start()
    weight.wait(0)
    weight.start(1)
    for y in range(4):
        pw_t[0, :, pl.ds(y * 512, 512)] = turned(pw[pl.ds(y * 8, 8), core].reshape(512, 128))
    latents.wait(0)
    latents.start(1)
    output.wait(0)
    output.start(1)
    weight.wait(1)
    weight.start(2)
    q_push.landed()
    total = total_slots(qsum[pair, own_rows, :], recvq, GROUP)
    rinv = lax.rsqrt(total[:, 256:] / D_LAT + 1e-06)
    proj = total[:, :256]
    q_spot = (pc.g, pc.y, pc.xl, pc.z // 2, pair)
    qg[q_spot] = (proj * rinv[:, :1]).astype(BF16)
    queries = Gather(pc, qg, view_rows, qa_s, qa_r, True, PAIR_ORDERS, False)
    queries.start(0)
    t_sib.wait()
    v_sib.wait()
    for block in range(2):
        tok_t[pl.ds(block * 512, 512), :] = turned(
            tokb[:, :, pl.ds(block * 512, 512)].reshape(512, 512)
        )
    weight.relay()
    queries.wait(0)
    queries.start(1)
    queries.wait(1)
    queries.start(2)
    for block in range(2, 4):
        tok_t[pl.ds(block * 512, 512), :] = turned(
            tokb[:, :, pl.ds(block * 512, 512)].reshape(512, 512)
        )
    pw_sib.wait()
    for y in range(4):
        pw_t[1, :, pl.ds(y * 512, 512)] = turned(pwx[pl.ds(y * 8, 8)].reshape(512, 128))
    lt_part = over(16, lt, ltp.at[pc.g], partner)
    lt_part.start()
    q_push.drain()
    weight.wait(2)
    latents.wait(1)
    latents.start(2)
    output.wait(1)
    output.start(2)

    tok = tokb[...].reshape(512, 2048)

    def project(n, carry):
        columns = at256(n)
        kv[:, columns] = dot(tok, wg[:, :, :, :, columns].reshape(2048, 256)).astype(BF16)
        return carry

    lax.fori_loop(0, 4, project, 0)
    for n in range(4):
        kv_t[pl.ds(n * 256, 256), :] = turned(kv[:, n * 256 : n * 256 + 256])
    queries.wait(2)
    qo_sib = over(17, qg.at[pc.g], qo, sib)
    qo_sib.start()

    def n_copy(k):
        g, j = pc.plane_peer(k)
        return remote(
            npk.at[j % 2, at16(g * 16 + j // 2), :], recvn.at[k], n_s.at[k], n_r.at[k], chip_device(g, j)
        )

    n_push = PairPushes(pc, n_copy)
    for p in range(2):
        packed = []
        sums = []
        for side in range(2):
            head = p * 2 + side
            columns = pl.ds(head * 128, 128)
            query = heads_of(qg, p, side)
            total = jnp.zeros((1, 512), F32)
            for chunk in range(4):
                slots = pl.ds(chunk * 128, 128)
                raw = col_dot(kv[slots, columns], query)
                squash = jnp.tanh(raw * (SCALE / SCORE_CAP))
                keep = valb[chunk // 2, pl.ds(chunk % 2 * 128, 128), :][:, :1]
                weights = jnp.exp(SCORE_CAP * squash) * keep
                half[head, slots, :] = weights.astype(BF16)
                fac[head, slots, :] = weights * (1.0 - squash * squash) * SCALE
                total = total + jnp.sum(weights, axis=0, keepdims=True)
            packed.append(dot(kv_t[pl.ds(512 + head * 128, 128), :], half[head]))
            sums.append(jnp.broadcast_to(total, (64, 512)))
        npk[p] = jnp.concatenate(packed + sums, axis=0).T.astype(BF16)
        n_push.start_pair(p)
        if p == 0:
            latents.relay()
            output.relay()

    weight.drain()
    queries.drain()
    n_push.landed()
    total = total_slots(npk[pair, all_rows, :], recvn, CHIPS)
    whole = jnp.concatenate(
        [jnp.broadcast_to(total[:, 256:257], (16, 128)), jnp.broadcast_to(total[:, 320:321], (16, 128))],
        axis=1,
    )
    ablk[...] = (total[:, :256] / whole).astype(BF16)
    a_spot = attf.at[core, all_rows, at256(pair)]
    a_push = Pushes(
        CHIPS,
        lambda k: remote(ablk, a_spot, a_s.at[k], a_r.at[k], chip_device(*pc.plane_peer(k))),
    )
    a_push.start()
    a_own = pltpu.make_async_copy(ablk, a_spot, loc.at[5])
    a_own.start()

    n_push.drain()
    latents.wait(2)
    feats = lown[...].reshape(2048, 256)
    lat_s[:128, :] = dot(pw_t[1], feats)
    squares = jnp.zeros((1, 256), F32)
    for y in range(4):
        block = lown[y].reshape(512, 256).astype(F32)
        squares = squares + jnp.sum(block * block, axis=0, keepdims=True)
    lat_s[128:, :] = jnp.broadcast_to(squares, (8, 256))
    lat_sib = over(5, lat_s, lat_x, sib)
    lat_sib.start()
    hidden = dot(pw_t[0], feats)
    output.wait(2)

    rows = owe[...].reshape(2048, 512)
    fold_s[...] = dot(pw_t[1], rows).astype(BF16)
    fold_sib = over(6, fold_s, fold_x, sib)
    fold_sib.start()
    folded = dot(pw_t[0], rows)
    fold_sib.wait()
    fold[:, group_half] = (folded + fold_x[...].astype(F32)).astype(BF16)
    f_part = over(18, fold.at[:, group_half], fold.at[:, group_half], partner)
    f_part.start()
    lat_sib.wait()
    hidden = hidden + lat_x[:128, :]
    rinv_row = lax.rsqrt((squares + lat_x[128:129, :]) / D_LAT + 1e-06)
    a_own.wait()
    a_push.landed()
    a_sib = over(7, attf.at[core], attf.at[core], sib)
    a_sib.start()
    f_part.wait()
    f_sib = over(8, fold.at[:, pl.ds(pl.multiple_of((1 - core) * 512, 512), 512)], foldx, sib)
    f_sib.start()
    a_sib.wait()
    group_rows = at256(pc.g)
    hidden = hidden + col_dot(fold[:, :512], attf[0, group_rows, :])
    hidden = (hidden + col_dot(fold[:, 512:], attf[1, group_rows, :])).astype(BF16).astype(F32)
    grad_y = igrad[...].astype(F32).T
    scaled_dy = grad_y * gain[...]
    square_row = jnp.sum(hidden * hidden, axis=0, keepdims=True)
    inner_row = jnp.sum(hidden * scaled_dy, axis=0, keepdims=True)
    sumo[...] = jnp.concatenate(
        [
            square_row[:, :128], square_row[:, 128:], inner_row[:, :128], inner_row[:, 128:],
            jnp.zeros((4, 128), F32),
        ],
        axis=0,
    )
    s_sib = over(9, sumo, sumx.at[0], sib)
    s_sib.start()
    s_sib.wait()
    sumx[1] = sumx[0] + sumo[...]
    t_push = Pushes(
        GROUP,
        lambda k: remote(sumx.at[1], sumr.at[k], t_s.at[k], t_r.at[k], chip_device(pc.g, pc.group_peer(k))),
    )
    t_push.start()
    lat_out = lt[...].astype(F32) + col_dot(owt[:, :512], attf[0, group_rows, :])
    la[pc.g, pc.y, pc.xl, pc.z, core] = (lat_out + col_dot(owt[:, 512:], attf[1, group_rows, :])).astype(BF16)
    resampled.start(0)
    resampled.wait(0)
    resampled.start(1)
    t_push.landed()
    total = total_slots(sumx[1], sumr, GROUP)
    square_row = jnp.concatenate([total[0:1], total[1:2]], axis=1)
    inner_row = jnp.concatenate([total[2:3], total[3:4]], axis=1)
    hrinv = lax.rsqrt(square_row / D_LLM + 1e-05)
    normed = hidden * hrinv
    llm[...] = turned(normed * gain[...])
    give_llm = pltpu.make_async_copy(llm, llm_to, out_s.at[0])
    give_llm.start()
    gain_own = jnp.broadcast_to(jnp.sum(grad_y * normed, axis=1, keepdims=True), (128, 128))
    grad_h = hrinv * scaled_dy - (hrinv * hrinv * hrinv / D_LLM * inner_row) * hidden
    gh_t[...] = grad_h.astype(BF16)
    h_sib = over(10, gh_t, ghx, sib)
    h_sib.start()
    ghp[pc.g] = gh_t[...]
    h_part = over(11, gh_t, ghp.at[pc.g], partner)
    h_part.start()
    gain_out[pc.g] = gain_own
    gain_part = over(12, gain_out.at[pc.g], gain_out.at[pc.g], partner)
    gain_part.start()

    f_sib.wait()
    own_half = fold[:, pl.ds(pl.multiple_of(core * 512, 512), 512)]
    partial = dot(turned(gh_t[...]), own_half)
    h_sib.wait()
    gap[...] = (partial + dot(turned(ghx[...]), foldx[...])).astype(BF16)

    def g_copy(k):
        j = pc.group_peer(k)
        return remote(
            gap.at[at16(j // 2), at256(j % 2)], recvg.at[k], g_s.at[k], g_r.at[k], chip_device(pc.g, j)
        )

    g_push = Pushes(GROUP, g_copy)
    g_push.start()

    resampled.wait(1)
    resampled.start(2)

    for n in range(4):
        part = dot(pw[pl.ds(n * 8, 8), core].reshape(512, 128), gh_t[...])
        part = part + dot(pwx[pl.ds(n * 8, 8)].reshape(512, 128), ghx[...])
        glp[pl.ds(n * 8, 8)] = part.astype(BF16).reshape(8, 64, 256)

    def l_copy(k):
        j = pc.group_peer(k)
        return remote(glp.at[j], recvl.at[k], gl_s.at[k], gl_r.at[k], chip_device(pc.g, j))

    l_push = Pushes(GROUP, l_copy)
    g_push.landed()
    grad = total_slots(gap[own_rows, at256(pair)], recvg, GROUP).astype(BF16).astype(F32)
    gblk[...] = (grad / whole).astype(BF16)
    g_spot = gg.at[all_rows, at256(pair)]
    gga_push = Pushes(
        CHIPS,
        lambda k: remote(gblk, g_spot, gga_s.at[k], gga_r.at[k], chip_device(*pc.plane_peer(k))),
    )
    gga_push.start()
    l_push.start()
    g_own = pltpu.make_async_copy(gblk, g_spot, loc.at[6])
    g_own.start()
    resampled.relay()
    for push in (a_push, t_push, g_push):
        push.drain()
    g_own.wait()
    gga_push.landed()

    def gq_copy(k):
        g, j = pc.plane_peer(k)
        return remote(
            gqp.at[at16(g * 16 + j // 2), at256(j % 2)], recvgq.at[k], gq_s.at[k], gq_r.at[k], chip_device(g, j)
        )

    gq_push = PairPushes(pc, gq_copy)
    ones = jnp.ones((8, 128), BF16)
    for p in range(2):
        parts = []
        for head in (p * 2, p * 2 + 1):
            columns = pl.ds(head * 128, 128)
            grads = gg[:, columns]
            prod = grads.astype(F32) * attf[core, :, columns].astype(F32)
            high = prod.astype(BF16)
            rest = (prod - high.astype(F32)).astype(BF16)
            delta = (col_dot(ones, high) + col_dot(ones, rest))[:1, :].astype(BF16).astype(F32)
            for chunk in range(4):
                slots = pl.ds(chunk * 128, 128)
                prob = col_dot(kv[slots, 512 + head * 128 : 640 + head * 128], grads)
                ds[head, slots, :] = (fac[head, slots, :] * (prob - delta)).astype(BF16)
            parts.append(dot(kv_t[pl.ds(head * 128, 128), :], ds[head]))
        gqp[:, p * 256 : p * 256 + 256] = jnp.concatenate(parts, axis=0).T.astype(BF16)
        gq_push.start_pair(p)
    for head in range(4):
        columns = pl.ds(head * 128, 128)
        gkv[:, columns] = dot(ds[head], heads_of(qg, head // 2, head % 2)).astype(BF16)
        gkv[:, 512 + head * 128 : 640 + head * 128] = dot(half[head], gg[:, columns]).astype(BF16)

    first, once = (r1a, r1b, r1c), (s1a, s1b, s1c)
    second, twice = (r2a, r2b, r2c), (s2a, s2b, s2c)
    third = (r3a, r3b, r3c)

    for x in range(4):
        for n in range(2):
            wg[x, :, :, :, n * 512 : n * 512 + 512] = (
                dot(tok_t[x * 512 : x * 512 + 512, :], gkv[:, n * 512 : n * 512 + 512])
                .astype(BF16)
                .reshape(4, 4, 32, 512)
            )

    far = (fara, farb, farc)

    def slab(part, spot, half=None):
        axis = ORDERS[part][0]
        index = [pick(None if half is None else Half(half))] + [slice(None)]
        index.insert(axis, spot)
        return wg.at[(*index, slice(None), pl.ds(*WIDE[part]))]

    def ring(part):
        axis = ORDERS[part][0]
        up, down = (mine[axis] + 1) % 4, (mine[axis] + 3) % 4
        beyond = (mine[axis] + 2) % 4
        above, below = list(mine), list(mine)
        above[axis], below[axis] = up, down
        moves = (
            (slab(part, beyond, 0), far[part].at[0], above),
            (slab(part, beyond, 1), far[part].at[1], below),
            (slab(part, up, 1), first[part].at[1, 2:4], above),
            (slab(part, down, 0), first[part].at[2, 0:2], below),
            (slab(part, up, 0), first[part].at[1, 0:2], above),
            (slab(part, down, 1), first[part].at[2, 2:4], below),
        )

        def move(n):
            src, dst, peer = moves[n]
            spot = part * 6 + n
            return remote(src, dst, p_s.at[spot], p_r.at[spot], chip_device(*pc.chip(*peer)))

        return [Later(functools.partial(move, n)) for n in range(6)]

    def add_far(part, spot, half):
        axis = ORDERS[part][0]
        columns = pl.ds(*WIDE[part])

        def body(n, carry):
            index = [half * 2 + n // 4, n % 4]
            index.insert(axis, spot)
            held = wg[(*index, slice(None), columns)].astype(F32)
            wg[(*index, slice(None), columns)] = (held + far[part][half, n // 4, n % 4].astype(F32)).astype(BF16)
            return carry

        lax.fori_loop(0, 8, body, 0)

    def copies(part, phase):
        axis = ORDERS[part][phase]
        for step in (1, 3, 2):
            peer = list(mine)
            peer[axis] = (peer[axis] + step) % 4
            spot = 18 + (part * 2 + phase - 1) * 3 + step - 1
            order = ORDERS[part]
            index = [
                peer[axis] if n == axis else slice(None) for n in range(3) if n not in order[:phase]
            ]
            yield remote(
                (once, twice)[phase - 1][part].at[tuple(index)],
                (second, third)[phase - 1][part].at[step],
                p_s.at[spot], p_r.at[spot], chip_device(*pc.chip(*peer)),
            )

    gq_push.landed()
    grad = total_slots(gqp[all_rows, at256(pair)], recvgq, CHIPS)
    sq[core, q_spot[0], q_spot[1], q_spot[2], q_spot[3], pair] = (grad * rinv[:, :1]).astype(BF16)
    scaled = Gather(pc, sq.at[core], view_rows, sqa_s, sqa_r, True, PAIR_ORDERS, False)
    scaled.start(0)
    for part in range(3):
        sent = ring(part)
        for n in range(2):
            sent[n].start()
    held_first = []
    for part in range(3):
        sent = ring(part)
        for n in range(2, 4):
            sent[n].start()
        copy = pltpu.make_async_copy(slab(part, mine[ORDERS[part][0]]), first[part].at[0], loc.at[7 + part])
        copy.start()
        held_first.append(copy)
    l_push.landed()
    lblk[...] = total_slots(glp[pc.j], recvl, GROUP).astype(BF16)
    glf[pc.g] = lblk[...]
    l_part = over(13, lblk, glf.at[pc.g], partner)
    l_part.start()
    resampled.wait(2)
    la_sib = over(14, la.at[:, :, :, :, core], la.at[:, :, :, :, core], sib)
    la_sib.start()
    scaled.wait(0)
    scaled.start(1)
    for part in range(3):
        sent = ring(part)
        place = mine[ORDERS[part][0]]
        sent[0].wait_recv()
        add_far(part, (place + 1) % 4, 0)
        sent[4].start()
        sent[1].wait_recv()
        add_far(part, (place + 3) % 4, 1)
        sent[5].start()
    scaled.wait(1)
    scaled.start(2)
    h_part.wait()
    la_sib.wait()
    gh_both = [turned(ghp[n]) for n in range(2)]

    def project_grad(n, carry):
        y, xl = n // 2, n % 2
        gpw[y, xl] = dot(la[0, y, xl].reshape(512, 256), gh_both[0]) + dot(
            la[1, y, xl].reshape(512, 256), gh_both[1]
        )
        return carry

    lax.fori_loop(0, 8, project_grad, 0)
    give_gpw = pltpu.make_async_copy(gpw, gpw_to, out_s.at[1])
    give_gpw.start()
    gga_push.drain()

    for part in range(3):
        held_first[part].wait()
        sent = ring(part)
        for n in range(2, 6):
            sent[n].wait_recv()
        src, dst = first[part], once[part]

        def add_first(n, carry, src=src, dst=dst):
            a, b = n // 4, n % 4
            dst[a, b] = sum(src[s, a, b].astype(F32) for s in range(3)).astype(BF16)
            return carry

        lax.fori_loop(0, 16, add_first, 0)
        for copy in copies(part, 1):
            copy.start()

    scaled.wait(2)
    s_sib2 = over(15, sq.at[core], sq.at[core], sib)
    s_sib2.start()
    l_part.wait()
    l_push.drain()
    gq_push.drain()
    for c in range(2):
        gow_t[:, c * 512 : c * 512 + 512] = dot(glf[0], attf[c, :256, :]) + dot(glf[1], attf[c, 256:, :])
    give_gow = pltpu.make_async_copy(gow_t, gow_to, out_s.at[2])
    give_gow.start()
    gain_part.wait()
    gain_row[...] = (gain_out[0] + gain_out[1]).T[:1, :]
    give_gain = pltpu.make_async_copy(gain_row, gain_to, out_s.at[3])
    give_gain.start()

    for part in range(3):
        for copy in copies(part, 1):
            copy.wait_recv()
        src, dst, held = second[part], twice[part], once[part]
        left = [axis for axis in range(3) if axis != ORDERS[part][0]]
        leading = left[0] == ORDERS[part][1]
        here = mine[ORDERS[part][1]]

        def add_second(n, carry, src=src, dst=dst, held=held, leading=leading, here=here):
            base = held[here, n] if leading else held[n, here]
            dst[n] = (base.astype(F32) + sum(src[s, n].astype(F32) for s in range(1, 4))).astype(BF16)
            return carry

        lax.fori_loop(0, 4, add_second, 0)
        for copy in copies(part, 2):
            copy.start()

    lt_part.wait()
    qo_sib.wait()
    s_sib2.wait()
    back = glf[pc.g].astype(F32)
    ratio = jnp.zeros((256, 128), F32)
    for c in range(2):
        for p in range(2):
            columns = pl.ds(c * 512 + p * 256, 256)
            blocks = [sq[c, n, :, :, :, p].reshape(256, 256) for n in range(2)]
            gqw[:, columns] = dot(ltp[0], blocks[0]) + dot(ltp[1], blocks[1])
            back = back + col_dot(qw[:, columns], sq[c, pc.g, :, :, :, p].reshape(256, 256))
    for p in range(2):
        for block, query in (
            (sq[core, pc.g, :, :, :, p], qg[pc.g, :, :, :, p]),
            (sq[1 - core, pc.g, :, :, :, p], qo[:, :, :, p]),
        ):
            prod = block.astype(F32).reshape(256, 256) * query.astype(F32).reshape(256, 256)
            ratio = ratio + prod[:, :128] + prod[:, 128:]
    coef = jnp.sum(ratio.T, axis=0, keepdims=True) * rinv_row / D_LAT
    gl_out[...] = back - coef * lt[...].astype(F32)
    give_gl = pltpu.make_async_copy(gl_out, gl_to, out_s.at[4])
    give_gl.start()
    give_gqw = pltpu.make_async_copy(gqw, gqw_to, out_s.at[5])
    give_gqw.start()
    for gather in (latents, output, resampled, scaled):
        gather.drain()

    for part in range(3):
        for copy in copies(part, 2):
            copy.wait_recv()
        here = mine[ORDERS[part][2]]
        fin[:, pl.ds(*WIDE[part])] = twice[part][here].astype(F32) + sum(
            third[part][s].astype(F32) for s in range(1, 4)
        )
    give = over(19, fin.at[at16(1 - core), :], oth, sib)
    give.start()

    def put(plane, rows):
        for n in range(2):
            spot = pl.multiple_of(n * 1024 + plane * 512, 512)
            gkw[:, pl.ds(spot, 512)] = rows[:13, n * 512 : n * 512 + 512]

    put(core, fin[at16(core), :])
    w_sib.wait_send()
    q_sib.wait_send()
    for part in range(3):
        for copy in ring(part):
            copy.wait_send()
        for phase in (1, 2):
            for copy in copies(part, phase):
                copy.wait_send()
    give.wait()
    put(1 - core, oth[...])
    give_gkw = pltpu.make_async_copy(gkw, gkw_to, out_s.at[6])
    give_gkw.start()
    for copy in (give_llm, give_gpw, give_gow, give_gain, give_gl, give_gqw, give_gkw):
        copy.wait()


def sems(*counts):
    return [pltpu.SemaphoreType.DMA((n,)) for n in counts]


def finish_kernel(*refs):
    got, done = refs[-2:]
    n = len(refs) // 3
    moves = []
    for i in range(n):
        src, dst, held = refs[i], refs[n + i], refs[2 * n + i]
        if len(src.shape) > 2:
            moves += [(src.at[m], held.at[m], dst.at[m]) for m in range(src.shape[0])]
        else:
            moves.append((src, held, dst))
    loads = [pltpu.make_async_copy(src, held, got.at[m]) for m, (src, held, dst) in enumerate(moves)]
    stores = [pltpu.make_async_copy(held, dst, done.at[m]) for m, (src, held, dst) in enumerate(moves)]
    for copy in loads:
        copy.start()
    for load, store in zip(loads, stores):
        load.wait()
        store.start()
    for copy in stores:
        copy.wait()


def local(
    tokens, keep_mask, shard_counts, latents, query_weight, keyval_weight, output_weight,
    project_weight, llm_gain, input_grad,
):
    widths = [w for _, w in WIDE]
    scratch = [
        ((256, 1664), BF16),
        ((13, 2048), BF16),
        ((64, 1024), BF16),
        ((64, 256), BF16),
        ((64, 1024), BF16),
        ((32, 2, 64, 128), BF16),
        ((256, 128), BF16),
        ((256, 128), BF16),
        ((64, 256), F32),
        ((64, 1024), F32),
        ((13, 2048), F32),
        ((64, 1024), F32),
        ((4, 2, 512, 128), F32),
        ((1, 128), F32),
        ((2, 128, 128), F32),
        ((256, 128), F32),
        ((2, 2, 256, 384), BF16),
        ((2, 16, 1024), BF16),
        ((128, 256), F32),
        ((4, 4, 4, 32, 1024), BF16),
        ((2, 256, 2048), BF16),
        ((2048, 512), BF16),
        ((2, 256, 128), F32),
        ((2, 256, 384), BF16),
        ((2, 256, 384), BF16),
        ((32, 16, 384), BF16),
        ((2, 4, 2, 2, 2, 16, 256), BF16),
        ((4, 2, 2, 2, 16, 256), BF16),
        ((4, 2, 4, 64, 512), BF16),
        ((4, 2, 4, 64, 256), BF16),
        ((2, 64, 256), BF16),
        ((2, 4, 2, 4, 2, 64, 256), BF16),
        ((512, 1024), BF16),
        ((1024, 512), BF16),
        ((4, 512, 512), F32),
        ((4, 512, 512), BF16),
        ((2, 512, 384), BF16),
        ((64, 16, 384), BF16),
        ((16, 256), BF16),
        ((2, 512, 512), BF16),
        ((2, 128, 2048), BF16),
        ((32, 64, 128), BF16),
        ((136, 256), F32),
        ((136, 256), F32),
        ((128, 512), BF16),
        ((128, 512), BF16),
        ((128, 1024), BF16),
        ((128, 512), BF16),
        ((2, 8, 128), F32),
        ((8, 128), F32),
        ((32, 8, 128), F32),
        ((128, 256), BF16),
        ((128, 256), BF16),
        ((2, 128, 256), BF16),
        ((256, 512), BF16),
        ((32, 16, 256), BF16),
        ((32, 64, 256), BF16),
        ((32, 64, 256), BF16),
        ((64, 256), BF16),
        ((2, 64, 256), BF16),
        ((16, 256), BF16),
        ((512, 512), BF16),
        ((4, 512, 512), BF16),
        ((512, 512), BF16),
        ((64, 16, 256), BF16),
        ((512, 1024), BF16),
        ((2, 2, 4, 2, 2, 2, 16, 256), BF16),
        *[((3, 4, 4, 32, w), BF16) for w in widths],
        *[((4, 4, 32, w), BF16) for w in widths],
        *[((4, 4, 32, w), BF16) for w in widths],
        *[((4, 32, w), BF16) for w in widths],
        *[((4, 32, w), BF16) for w in widths],
        *[((2, 2, 4, 32, w), BF16) for w in widths],
        ((32, 1024), F32),
        ((16, 1024), F32),
    ]
    results = [
        jax.ShapeDtypeStruct(shape, dtype)
        for shape, dtype in (
            ((256, 128), BF16),
            ((64, 256), F32),
            ((64, 1024), F32),
            ((13, 2048), F32),
            ((64, 1024), F32),
            ((4, 2, 512, 128), F32),
            ((1, 128), F32),
        )
    ]
    made = pl.pallas_call(
        whole_kernel,
        out_shape=results,
        in_specs=[VMEM] * 3 + [ANY] * 7,
        out_specs=[ANY] * 7,
        scratch_shapes=[pltpu.VMEM(s, d) for s, d in scratch]
        + sems(36, 36, 36, 36, 36, 36, 36, 36, 32, 32, 18, 18, 64, 64, 64, 64, 32, 32)
        + sems(32, 32, 32, 32, 64, 64, 64, 64, 18, 18, 36, 36, 20, 20, 20, 7),
        compiler_params=pltpu.CompilerParams(
            has_side_effects=True, vmem_limit_bytes=62 << 20, collective_id=0
        ),
        name="whole",
    )(
        keep_mask.reshape(1, 256), shard_counts.reshape(1, 1), llm_gain.reshape(1, 128), tokens,
        keyval_weight, query_weight, latents.T, output_weight.T, project_weight.reshape(32, 2, 64, 128),
        input_grad,
    )
    llm, gl, gqw, gkw, gow, gpw, gain = pl.pallas_call(
        finish_kernel,
        out_shape=results,
        in_specs=[ANY] * 7,
        out_specs=[ANY] * 7,
        scratch_shapes=[pltpu.VMEM(r.shape, r.dtype) for r in results] + sems(10, 10),
        compiler_params=pltpu.CompilerParams(vmem_limit_bytes=62 << 20),
        name="finish",
    )(*made)
    return (llm, gl.T, gqw, gkw, gow.T, gpw.reshape(4096, 128), gain.reshape(128))


def solution(mesh):
    in_specs = (
        P(("grp", "tp"), None),
        P(("grp", "tp")),
        P(("grp", "tp")),
        P("grp", "tp"),
        P("tp", None),
        P(("grp", "tp"), None),
        P(None, "tp"),
        P(None, "tp"),
        P("tp"),
        P("grp", "tp"),
    )
    out_specs = (
        P("grp", "tp"),
        P("grp", "tp"),
        P("tp", None),
        P(("grp", "tp"), None),
        P(None, "tp"),
        P(None, "tp"),
        P("tp"),
    )
    return jax.shard_map(local, mesh=mesh, in_specs=in_specs, out_specs=out_specs, check_vma=False)
```

```python
import functools
import math

import jax
import jax.numpy as jnp
import numpy as np
from jax import lax
from jax.experimental import pallas as pl
from jax.experimental.pallas import tpu as pltpu
from jax.sharding import PartitionSpec as P

D_LAT = 4096
HEAD_DIM = 128
D_LLM = 8192
SCORE_CAP = 5.0
SCALE = 1.0 / math.sqrt(HEAD_DIM)
CHIPS = 64
GROUP = 32

F32 = jnp.float32
BF16 = jnp.bfloat16
MESH = pl.DeviceIdType.MESH
ANY = pl.BlockSpec(memory_space=pl.ANY)
VMEM = pl.BlockSpec(memory_space=pltpu.VMEM)

ORDERS = ((2, 1, 0), (1, 0, 2), (0, 2, 1))
WIDE = ((0, 384), (384, 384), (768, 256))
SPLIT = ((0, 256), (256, 128), (384, 128), (512, 128), (640, 128), (768, 256))
SPLIT_ORDERS = ORDERS + ORDERS
KEYS, VALUES = (0, 1, 2), (3, 4, 5)
COLUMNS_512 = ((0, 128), (128, 256), (384, 128))
ROWS_64 = ((0, 16), (16, 32), (48, 16))
ROWS_OWN = ((0, 16), (16, 16), (32, 32))
PAIR_ORDERS = ((2, 1, 0), (1, 0, 2))


def row_dot(left, right):
    return lax.dot_general(left, right, (((0,), (0,)), ((), ())), preferred_element_type=F32)


def col_dot(left, right):
    return lax.dot_general(left, right, (((1,), (1,)), ((), ())), preferred_element_type=F32)


def dot(left, right):
    return jnp.dot(left, right, preferred_element_type=F32)


class Place:
    def __init__(self):
        self.g = lax.axis_index("grp")
        self.t = lax.axis_index("tp")
        self.core = self.t % 2
        self.j = self.t // 2
        self.z = self.j % 4
        self.xl = (self.j // 4) % 2
        self.y = self.j // 8
        self.x = self.g * 2 + self.xl

    def chip(self, x, y, z):
        return x // 2, (y * 2 + x % 2) * 4 + z

    def plane_peer(self, k):
        return self.chip((self.x + k // 16) % 4, (self.y + (k // 4) % 4) % 4, (self.z + k % 4) % 4)

    def group_peer(self, k):
        y = (self.y + k // 8) % 4
        xl = (self.xl + (k // 4) % 2) % 2
        z = (self.z + k % 4) % 4
        return (y * 2 + xl) * 4 + z

    def sibling(self):
        return self.g, self.j * 2 + 1 - self.core


def remote(src, dst, sends, recvs, device):
    return pltpu.make_async_remote_copy(
        src_ref=src, dst_ref=dst, send_sem=sends, recv_sem=recvs, device_id=device, device_id_type=MESH
    )


class Later:
    def __init__(self, make):
        self.make = make

    def start(self):
        self.make().start()

    def wait_recv(self):
        self.make().wait_recv()

    def wait_send(self):
        self.make().wait_send()


def each_peer(n, do):
    def body(k, carry):
        do(k)
        return carry

    lax.fori_loop(1, n, body, 0)


class Gather:
    def __init__(self, place, ref, view, sends, recvs, whole=True, orders=ORDERS, ring=True):
        self.place, self.ref, self.view, self.sends, self.recvs = place, ref, view, sends, recvs
        self.whole, self.orders, self.ring = whole, orders, ring

    def copies(self, phase, parts=None):
        pc = self.place
        mine = [pc.x, pc.y, pc.z]
        for part in self.parts(parts):
            order = self.orders[part]
            held = list(mine)
            for axis in order[:phase]:
                held[axis] = None
            block = self.view(self.ref, *held, part)
            near = order[phase] == 0 and not self.whole
            for step in (1,) if near else (1, 3, 2):
                peer = list(mine)
                if near:
                    peer[0] = pc.g * 2 + 1 - pc.xl
                else:
                    peer[order[phase]] = (peer[order[phase]] + step) % 4
                yield self.push(block, (part * (2 if self.ring else 3) + phase) * 3 + step - 1, peer)

    def push(self, block, spot, peer):
        g, j = self.place.chip(*peer)
        device = (g, j * 2 + self.place.core)
        return Later(lambda: remote(block, block, self.sends.at[spot], self.recvs.at[spot], device))

    def last(self, part):
        pc = self.place
        order = self.orders[part]
        axis = order[2]
        mine = [pc.x, pc.y, pc.z]
        base = (len(self.orders) + part) * 6
        if axis == 0 and not self.whole:
            held = [mine[0], None, None]
            block = self.view(self.ref, *held, part)
            return [self.push(block, base, [pc.g * 2 + 1 - pc.xl, pc.y, pc.z])]

        def at(place, half):
            held = [None, None, None]
            held[axis] = place
            held[order[0]] = Half(half)
            return self.view(self.ref, *held, part)

        here, up, down = mine[axis], (mine[axis] + 1) % 4, (mine[axis] + 3) % 4
        above, below = list(mine), list(mine)
        above[axis], below[axis] = up, down
        return [
            self.push(at(here, 0), base, above),
            self.push(at(here, 1), base + 1, above),
            self.push(at(here, 1), base + 2, below),
            self.push(at(here, 0), base + 3, below),
            self.push(at(down, 0), base + 4, above),
            self.push(at(up, 1), base + 5, below),
        ]

    def parts(self, some):
        return range(len(self.orders)) if some is None else some

    def start(self, phase, parts=None):
        if phase < 2 or not self.ring:
            for copy in self.copies(phase, parts):
                copy.start()
            return
        for part in self.parts(parts):
            copies = self.last(part)
            for n in (0,) if len(copies) == 1 else (0, 2, 1, 3):
                copies[n].start()

    def relay(self, parts=None):
        for part in self.parts(parts):
            copies = self.last(part)
            if len(copies) > 1:
                copies[0].wait_recv()
                copies[4].start()
                copies[2].wait_recv()
                copies[5].start()

    def wait(self, phase, parts=None):
        if phase < 2 or not self.ring:
            for copy in self.copies(phase, parts):
                copy.wait_recv()
            return
        for part in self.parts(parts):
            copies = self.last(part)
            for n in (0,) if len(copies) == 1 else (1, 3, 4, 5):
                copies[n].wait_recv()

    def drain(self):
        for phase in range(2 if self.ring else 3):
            for copy in self.copies(phase):
                copy.wait_send()
        for part in self.parts(None) if self.ring else ():
            for copy in self.last(part):
                copy.wait_send()


class Half:
    def __init__(self, n):
        self.n = n


def pick(value):
    if isinstance(value, Half):
        return slice(value.n * 2, value.n * 2 + 2)
    return slice(None) if value is None else value


def halves(x):
    if isinstance(x, Half):
        return x.n, slice(None)
    return (slice(None), slice(None)) if x is None else (x // 2, x % 2)


def in_group(x):
    if isinstance(x, Half):
        return slice(x.n, x.n + 1)
    return slice(None) if x is None else x % 2


def view_weight(ref, x, y, z, part):
    return ref.at[pick(x), pick(y), pick(z), :, pl.ds(*SPLIT[part])]


def view_output(ref, x, y, z, part):
    return ref.at[pick(y), in_group(x), pick(z), :, pl.ds(*COLUMNS_512[part])]


def view_own(ref, x, y, z, part):
    return ref.at[pick(y), in_group(x), pick(z), pl.ds(*ROWS_OWN[part]), :]


def view_rows(ref, x, y, z, part):
    hi, lo = halves(x)
    up, pair = halves(z)
    return ref.at[hi, pick(y), lo, up, pair, :, pl.ds(part * 128, 128)]


def view_latents(core, ref, x, y, z, part):
    hi, lo = halves(x)
    return ref.at[hi, pick(y), lo, pick(z), core, pl.ds(*ROWS_64[part]), :]


def total_slots(own, slots, n):
    def body(k, total):
        return total + slots[k].astype(F32)

    return lax.fori_loop(1, n, body, own.astype(F32))


class Pushes:
    def __init__(self, n, make):
        self.n, self.make = n, make

    def start(self):
        each_peer(self.n, lambda k: self.make(k).start())

    def landed(self):
        each_peer(self.n, lambda k: self.make(k).wait_recv())

    def drain(self):
        each_peer(self.n, lambda k: self.make(k).wait_send())


class PairPushes(Pushes):
    def __init__(self, place, make):
        super().__init__(CHIPS, make)
        self.place = place

    def start_pair(self, p):
        def body(i, carry):
            k = (i // 2) * 4 + (i % 2) * 2 + (self.place.z + p) % 2

            @pl.when(k > 0)
            def _():
                self.make(k).start()

            return carry

        lax.fori_loop(0, 32, body, 0)


def at16(n):
    return pl.ds(pl.multiple_of(n * 16, 16), 16)


def at256(n):
    return pl.ds(pl.multiple_of(n * 256, 256), 256)


def heads_of(ref, pair, side):
    return ref[:, :, :, :, pair, :, side * 128 : side * 128 + 128].reshape(512, 128)


def turned(value, dtype=BF16):
    return value.astype(F32).T.astype(dtype)


def whole_kernel(
    keep, count, gain_in, tokens_in, keyval_in, qw_in, lt_in, owt_in, pw_in, igrad_in,
    llm_to, gl_to, gqw_to, gkw_to, gow_to, gpw_to, gain_to,
    tokens, keyval_w, qw, lt, owt, pw, igrad, llm, gl_out, gqw, gkw, gow_t, gpw, gain_row, gain_out,
    val, qpart, wpl, gain,
    wg, tokb, tok_t, valb, qx, qsum, recvq, qg, qo, owe, lown, ltp, la, kv, kv_t, fac, half, npk, recvn,
    ablk, attf, pw_t, pwx, lat_s, lat_x, fold_s, fold_x, fold, foldx, sumx, sumo, sumr, gh_t, ghx, ghp, gap, recvg, glp, u1a, u1b, v1a, v1b, u2, v2, u3,
    lblk, glf, gblk, gg, ds, gqp, recvgq, gkv, sq, r1a, r1b, r1c, s1a, s1b, s1c,
    r2a, r2b, r2c, s2a, s2b, s2c, r3a, r3b, r3c, fara, farb, farc, fin, oth,
    w_s, w_r, ow_s, ow_r, lo_s, lo_r, l_s, l_r, q_s, q_r, qa_s, qa_r, n_s, n_r, a_s, a_r, t_s, t_r,
    g_s, g_r, gl_s, gl_r, gga_s, gga_r, gq_s, gq_r, sqa_s, sqa_r, p_s, p_r, x_s, x_r, loc, out_s,
):
    pc = Place()
    core = pc.core
    sib = pc.sibling()
    partner = (1 - pc.g, pc.t)
    mine = [pc.x, pc.y, pc.z]
    pair = pc.j % 2
    own_rows = at16(pc.j // 2)
    all_rows = at16(pc.g * 16 + pc.j // 2)

    def chip_device(g, j):
        return (g, j * 2 + core)

    def over(index, src, dst, device):
        return remote(src, dst, x_s.at[index], x_r.at[index], device)

    barrier = pltpu.get_barrier_semaphore()

    def greet(k):
        pl.semaphore_signal(barrier, inc=1, device_id=chip_device(*pc.plane_peer(k)), device_id_type=MESH)

    pl.semaphore_signal(barrier, inc=1, device_id=sib, device_id_type=MESH)
    each_peer(CHIPS, greet)

    loads = [
        pltpu.make_async_copy(src, dst, loc.at[12 + n])
        for n, (src, dst) in enumerate(
            (
                (keyval_in, keyval_w), (lt_in, lt), (qw_in, qw), (owt_in, owt),
                (tokens_in, tokens), (pw_in, pw), (igrad_in, igrad),
            )
        )
    ]
    for copy in loads:
        copy.start()
    loads[0].wait()

    rows_f32 = jnp.concatenate([keyval_w[...].astype(F32), jnp.zeros((3, 2048), F32)], axis=0).astype(BF16)
    for c in range(2):
        wpl[c, :, :512] = rows_f32[:, c * 512 : c * 512 + 512]
        wpl[c, :, 512:] = rows_f32[:, 1024 + c * 512 : 1536 + c * 512]
    w_own = pltpu.make_async_copy(wpl.at[core], wg.at[pc.x, pc.y, pc.z, at16(core)], loc.at[3])
    w_own.start()
    for copy in loads[1:]:
        copy.wait()
    feats_f32 = lt[...].astype(F32)
    lat = feats_f32.T.astype(BF16)
    squares = jnp.sum(feats_f32 * feats_f32, axis=0, keepdims=True)
    squares = jnp.broadcast_to(squares, (128, 256)).T.astype(BF16)
    for c in range(2):
        for p in range(2):
            columns = (c * 2 + p) * 256
            qpart[c, p, :, :256] = dot(lat, qw[:, columns : columns + 256]).astype(BF16)
            qpart[c, p, :, 256:] = squares
    spot = lax.broadcasted_iota(jnp.int32, (1, 256), 1)
    kept = ((keep[...] == 1) | (spot == 0)) & (spot < count[...])
    val[...] = jnp.broadcast_to(jnp.where(kept, 1.0, 0.0), (128, 256)).T
    gain[...] = jnp.broadcast_to(gain_in[...].astype(F32), (256, 128)).T

    pl.semaphore_wait(barrier, CHIPS)

    w_sib = over(0, wpl.at[1 - core], wg.at[pc.x, pc.y, pc.z, at16(core)], sib)
    w_sib.start()

    q_sib = over(1, qpart.at[1 - core], qx, sib)
    q_sib.start()
    weight = Gather(pc, wg, view_weight, w_s, w_r, True, SPLIT_ORDERS)
    output = Gather(pc, owe, view_output, ow_s, ow_r, False)
    latents = Gather(pc, lown, view_own, lo_s, lo_r, False)
    resampled = Gather(pc, la, functools.partial(view_latents, core), l_s, l_r)
    w_own.wait()
    w_sib.wait_recv()
    weight.start(0)
    group_half = pl.ds(pl.multiple_of(pc.g * 512, 512), 512)
    local_copies = [
        pltpu.make_async_copy(owt.at[:, group_half], owe.at[pc.y, pc.xl, pc.z], loc.at[0]),
        pltpu.make_async_copy(lt, lown.at[pc.y, pc.xl, pc.z], loc.at[1]),
        pltpu.make_async_copy(lt, ltp.at[pc.g], loc.at[11]),
        pltpu.make_async_copy(val, valb.at[core], loc.at[2]),
    ]
    for copy in local_copies:
        copy.start()

    q_sib.wait_recv()
    for p in range(2):
        qsum[p] = (qpart[core, p].astype(F32) + qx[p].astype(F32)).astype(BF16)

    def q_copy(k):
        j = pc.group_peer(k)
        return remote(
            qsum.at[j % 2, at16(j // 2), :], recvq.at[k], q_s.at[k], q_r.at[k], chip_device(pc.g, j)
        )

    q_push = Pushes(GROUP, q_copy)
    q_push.start()

    for block in range(16):
        x, y = block // 4, block % 4
        begin = (((x // 2) * 4 + y) * 2 + x % 2) * 104
        base = begin // 128 * 128
        width = min(256, 1664 - base)
        row = lax.broadcasted_iota(jnp.int32, (width, 128), 0)
        col = lax.broadcasted_iota(jnp.int32, (width, 128), 1)
        rest = col & 15
        hit = (row == (begin - base) + (col >> 4) * 13 + rest) & (rest < 13)
        place = jnp.where(hit, 1.0, 0.0).astype(BF16)
        tokb[core, :, pl.ds(block * 128, 128)] = dot(tokens[:, pl.ds(base, width)], place).astype(BF16)

    t_sib = over(2, tokb.at[core], tokb.at[core], sib)
    t_sib.start()
    for copy in local_copies:
        copy.wait()
    latents.start(0)
    output.start(0)
    v_sib = over(3, val, valb.at[core], sib)
    v_sib.start()
    pw_sib = over(4, pw.at[:, 1 - core], pwx, sib)
    pw_sib.start()
    weight.wait(0)
    weight.start(1)
    for y in range(4):
        pw_t[0, :, pl.ds(y * 512, 512)] = turned(pw[pl.ds(y * 8, 8), core].reshape(512, 128))
    latents.wait(0)
    latents.start(1)
    output.wait(0)
    output.start(1)
    q_push.landed()
    total = total_slots(qsum[pair, own_rows, :], recvq, GROUP)
    rinv = lax.rsqrt(total[:, 256:] / D_LAT + 1e-06)
    proj = total[:, :256]
    q_spot = (pc.g, pc.y, pc.xl, pc.z // 2, pair)
    qg[q_spot] = (proj * rinv[:, :1]).astype(BF16)
    queries = Gather(pc, qg, view_rows, qa_s, qa_r, True, PAIR_ORDERS, False)
    queries.start(0)
    weight.wait(1)
    weight.start(2, KEYS)
    queries.wait(0)
    queries.start(1)
    weight.start(2, VALUES)
    queries.wait(1)
    queries.start(2)
    t_sib.wait()
    v_sib.wait()
    for block in range(2):
        tok_t[pl.ds(block * 512, 512), :] = turned(
            tokb[:, :, pl.ds(block * 512, 512)].reshape(512, 512)
        )
    weight.relay(KEYS)
    for block in range(2, 4):
        tok_t[pl.ds(block * 512, 512), :] = turned(
            tokb[:, :, pl.ds(block * 512, 512)].reshape(512, 512)
        )
    pw_sib.wait()
    for y in range(4):
        pw_t[1, :, pl.ds(y * 512, 512)] = turned(pwx[pl.ds(y * 8, 8)].reshape(512, 128))
    lt_part = over(16, lt, ltp.at[pc.g], partner)
    lt_part.start()
    q_push.drain()
    weight.relay(VALUES)
    weight.wait(2, KEYS)
    latents.wait(1)
    latents.start(2)
    output.wait(1)
    output.start(2)

    tok = tokb[...].reshape(512, 2048)

    def project(n, carry):
        columns = at256(n)
        kv[:, columns] = dot(tok, wg[:, :, :, :, columns].reshape(2048, 256)).astype(BF16)
        return carry

    lax.fori_loop(0, 2, project, 0)
    queries.wait(2)
    qo_sib = over(17, qg.at[pc.g], qo, sib)
    qo_sib.start()
    totals = []
    for head in range(4):
        query = heads_of(qg, head // 2, head % 2)
        total = jnp.zeros((1, 512), F32)
        for chunk in range(4):
            slots = pl.ds(chunk * 128, 128)
            raw = col_dot(kv[slots, head * 128 : head * 128 + 128], query)
            squash = jnp.tanh(raw * (SCALE / SCORE_CAP))
            kept = valb[chunk // 2, pl.ds(chunk % 2 * 128, 128), :][:, :1]
            weights = jnp.exp(SCORE_CAP * squash) * kept
            half[head, slots, :] = weights.astype(BF16)
            fac[head, slots, :] = weights * (1.0 - squash * squash) * SCALE
            total = total + jnp.sum(weights, axis=0, keepdims=True)
        totals.append(total)
    weight.wait(2, VALUES)
    lax.fori_loop(2, 4, project, 0)

    def n_copy(k):
        g, j = pc.plane_peer(k)
        return remote(
            npk.at[j % 2, at16(g * 16 + j // 2), :], recvn.at[k], n_s.at[k], n_r.at[k], chip_device(g, j)
        )

    n_push = PairPushes(pc, n_copy)
    for p in range(2):
        heads = (p * 2, p * 2 + 1)
        packed = [
            dot(turned(kv[:, 512 + head * 128 : 640 + head * 128]), half[head]) for head in heads
        ] + [jnp.broadcast_to(totals[head], (64, 512)) for head in heads]
        npk[p] = jnp.concatenate(packed, axis=0).T.astype(BF16)
        n_push.start_pair(p)

    latents.relay()
    output.relay()
    for n in range(2):
        kv_t[pl.ds(n * 256, 256), :] = turned(kv[:, n * 256 : n * 256 + 256])
    weight.drain()
    queries.drain()
    n_push.landed()
    total = total_slots(npk[pair, all_rows, :], recvn, CHIPS)
    whole = jnp.concatenate(
        [jnp.broadcast_to(total[:, 256:257], (16, 128)), jnp.broadcast_to(total[:, 320:321], (16, 128))],
        axis=1,
    )
    ablk[...] = (total[:, :256] / whole).astype(BF16)
    a_spot = attf.at[core, all_rows, at256(pair)]
    a_push = Pushes(
        CHIPS,
        lambda k: remote(ablk, a_spot, a_s.at[k], a_r.at[k], chip_device(*pc.plane_peer(k))),
    )
    a_push.start()
    a_own = pltpu.make_async_copy(ablk, a_spot, loc.at[5])
    a_own.start()

    n_push.drain()
    latents.wait(2)
    feats = lown[...].reshape(2048, 256)
    lat_s[:128, :] = dot(pw_t[1], feats)
    squares = jnp.zeros((1, 256), F32)
    for y in range(4):
        block = lown[y].reshape(512, 256).astype(F32)
        squares = squares + jnp.sum(block * block, axis=0, keepdims=True)
    lat_s[128:, :] = jnp.broadcast_to(squares, (8, 256))
    lat_sib = over(5, lat_s, lat_x, sib)
    lat_sib.start()
    hidden = dot(pw_t[0], feats)
    output.wait(2)

    rows = owe[...].reshape(2048, 512)
    fold_s[...] = dot(pw_t[1], rows).astype(BF16)
    fold_sib = over(6, fold_s, fold_x, sib)
    fold_sib.start()
    folded = dot(pw_t[0], rows)
    fold_sib.wait()
    fold[:, group_half] = (folded + fold_x[...].astype(F32)).astype(BF16)
    f_part = over(18, fold.at[:, group_half], fold.at[:, group_half], partner)
    f_part.start()
    lat_sib.wait()
    hidden = hidden + lat_x[:128, :]
    rinv_row = lax.rsqrt((squares + lat_x[128:129, :]) / D_LAT + 1e-06)
    a_own.wait()
    a_push.landed()
    a_sib = over(7, attf.at[core], attf.at[core], sib)
    a_sib.start()
    f_part.wait()
    f_sib = over(8, fold.at[:, pl.ds(pl.multiple_of((1 - core) * 512, 512), 512)], foldx, sib)
    f_sib.start()
    a_sib.wait()
    group_rows = at256(pc.g)
    hidden = hidden + col_dot(fold[:, :512], attf[0, group_rows, :])
    hidden = (hidden + col_dot(fold[:, 512:], attf[1, group_rows, :])).astype(BF16).astype(F32)
    grad_y = igrad[...].astype(F32).T
    scaled_dy = grad_y * gain[...]
    square_row = jnp.sum(hidden * hidden, axis=0, keepdims=True)
    inner_row = jnp.sum(hidden * scaled_dy, axis=0, keepdims=True)
    sumo[...] = jnp.concatenate(
        [
            square_row[:, :128], square_row[:, 128:], inner_row[:, :128], inner_row[:, 128:],
            jnp.zeros((4, 128), F32),
        ],
        axis=0,
    )
    s_sib = over(9, sumo, sumx.at[0], sib)
    s_sib.start()
    s_sib.wait()
    sumx[1] = sumx[0] + sumo[...]
    t_push = Pushes(
        GROUP,
        lambda k: remote(sumx.at[1], sumr.at[k], t_s.at[k], t_r.at[k], chip_device(pc.g, pc.group_peer(k))),
    )
    t_push.start()
    lat_out = lt[...].astype(F32) + col_dot(owt[:, :512], attf[0, group_rows, :])
    la[pc.g, pc.y, pc.xl, pc.z, core] = (lat_out + col_dot(owt[:, 512:], attf[1, group_rows, :])).astype(BF16)
    resampled.start(0)
    resampled.wait(0)
    resampled.start(1)
    t_push.landed()
    total = total_slots(sumx[1], sumr, GROUP)
    square_row = jnp.concatenate([total[0:1], total[1:2]], axis=1)
    inner_row = jnp.concatenate([total[2:3], total[3:4]], axis=1)
    hrinv = lax.rsqrt(square_row / D_LLM + 1e-05)
    normed = hidden * hrinv
    llm[...] = turned(normed * gain[...])
    give_llm = pltpu.make_async_copy(llm, llm_to, out_s.at[0])
    give_llm.start()
    gain_own = jnp.broadcast_to(jnp.sum(grad_y * normed, axis=1, keepdims=True), (128, 128))
    grad_h = hrinv * scaled_dy - (hrinv * hrinv * hrinv / D_LLM * inner_row) * hidden
    gh_t[...] = grad_h.astype(BF16)
    h_sib = over(10, gh_t, ghx, sib)
    h_sib.start()
    ghp[pc.g] = gh_t[...]
    h_part = over(11, gh_t, ghp.at[pc.g], partner)
    h_part.start()
    gain_out[pc.g] = gain_own
    gain_part = over(12, gain_out.at[pc.g], gain_out.at[pc.g], partner)
    gain_part.start()

    f_sib.wait()
    own_half = fold[:, pl.ds(pl.multiple_of(core * 512, 512), 512)]
    partial = dot(turned(gh_t[...]), own_half)
    h_sib.wait()
    gap[...] = (partial + dot(turned(ghx[...]), foldx[...])).astype(BF16)

    def g_copy(k):
        j = pc.group_peer(k)
        return remote(
            gap.at[at16(j // 2), at256(j % 2)], recvg.at[k], g_s.at[k], g_r.at[k], chip_device(pc.g, j)
        )

    g_push = Pushes(GROUP, g_copy)
    g_push.start()

    resampled.wait(1)
    resampled.start(2)

    for n in range(4):
        part = dot(pw[pl.ds(n * 8, 8), core].reshape(512, 128), gh_t[...])
        part = part + dot(pwx[pl.ds(n * 8, 8)].reshape(512, 128), ghx[...])
        glp[n] = part.astype(BF16).reshape(2, 4, 64, 256)

    def gl_copies(phase):
        for part in range(2):
            axis = ((1, 2), (2, 1))[part][phase] if phase < 2 else 0
            for step in (1, 3, 2) if phase < 2 else (1,):
                peer = list(mine)
                if phase < 2:
                    peer[axis] = (peer[axis] + step) % 4
                else:
                    peer[0] = pc.g * 2 + 1 - pc.xl
                spot = part * 7 + phase * 3 + step - 1
                if phase == 0:
                    rows = pl.ds(part * 32, 32)
                    src = glp.at[peer[1], :, :, rows] if axis == 1 else glp.at[:, :, peer[2], rows]
                    dst = (u1a, u1b)[part].at[step - 1]
                elif phase == 1:
                    src = v1a.at[:, peer[2]] if axis == 2 else v1b.at[peer[1]]
                    dst = u2.at[part, step - 1]
                else:
                    src, dst = v2.at[part, 1 - pc.xl], u3.at[part]
                yield remote(src, dst, gl_s.at[spot], gl_r.at[spot], chip_device(*pc.chip(*peer)))

    def gl_start(phase):
        for copy in gl_copies(phase):
            copy.start()

    def gl_add(phase):
        for copy in gl_copies(phase):
            copy.wait_recv()
        if phase == 0:
            for n in range(4):
                for xl in range(2):
                    own = glp[pc.y, xl, n, :32, :].astype(F32)
                    v1a[xl, n] = (own + sum(u1a[i, xl, n].astype(F32) for i in range(3))).astype(BF16)
                    own = glp[n, xl, pc.z, 32:, :].astype(F32)
                    v1b[n, xl] = (own + sum(u1b[i, n, xl].astype(F32) for i in range(3))).astype(BF16)
        elif phase == 1:
            for xl in range(2):
                for part, own in ((0, v1a[xl, pc.z]), (1, v1b[pc.y, xl])):
                    added = own.astype(F32) + sum(u2[part, i, xl].astype(F32) for i in range(3))
                    v2[part, xl] = added.astype(BF16)
        else:
            for part in range(2):
                added = v2[part, pc.xl].astype(F32) + u3[part].astype(F32)
                lblk[part * 32 : part * 32 + 32, :] = added.astype(BF16)

    g_push.landed()
    grad = total_slots(gap[own_rows, at256(pair)], recvg, GROUP).astype(BF16).astype(F32)
    gblk[...] = (grad / whole).astype(BF16)
    g_spot = gg.at[all_rows, at256(pair)]
    gga_push = Pushes(
        CHIPS,
        lambda k: remote(gblk, g_spot, gga_s.at[k], gga_r.at[k], chip_device(*pc.plane_peer(k))),
    )
    gga_push.start()
    gl_start(0)
    g_own = pltpu.make_async_copy(gblk, g_spot, loc.at[6])
    g_own.start()
    resampled.relay()
    for push in (a_push, t_push, g_push):
        push.drain()
    g_own.wait()
    gga_push.landed()

    def gq_copy(k):
        g, j = pc.plane_peer(k)
        return remote(
            gqp.at[at16(g * 16 + j // 2), at256(j % 2)], recvgq.at[k], gq_s.at[k], gq_r.at[k], chip_device(g, j)
        )

    gq_push = PairPushes(pc, gq_copy)
    ones = jnp.ones((8, 128), BF16)
    for p in range(2):
        parts = []
        for head in (p * 2, p * 2 + 1):
            columns = pl.ds(head * 128, 128)
            grads = gg[:, columns]
            prod = grads.astype(F32) * attf[core, :, columns].astype(F32)
            high = prod.astype(BF16)
            rest = (prod - high.astype(F32)).astype(BF16)
            delta = (col_dot(ones, high) + col_dot(ones, rest))[:1, :].astype(BF16).astype(F32)
            for chunk in range(4):
                slots = pl.ds(chunk * 128, 128)
                prob = col_dot(kv[slots, 512 + head * 128 : 640 + head * 128], grads)
                ds[head, slots, :] = (fac[head, slots, :] * (prob - delta)).astype(BF16)
            parts.append(dot(kv_t[pl.ds(head * 128, 128), :], ds[head]))
        gqp[:, p * 256 : p * 256 + 256] = jnp.concatenate(parts, axis=0).T.astype(BF16)
        gq_push.start_pair(p)
    gl_add(0)
    gl_start(1)
    for head in range(4):
        columns = pl.ds(head * 128, 128)
        gkv[:, columns] = dot(ds[head], heads_of(qg, head // 2, head % 2)).astype(BF16)
        gkv[:, 512 + head * 128 : 640 + head * 128] = dot(half[head], gg[:, columns]).astype(BF16)

    first, once = (r1a, r1b, r1c), (s1a, s1b, s1c)
    second, twice = (r2a, r2b, r2c), (s2a, s2b, s2c)
    third = (r3a, r3b, r3c)

    for x in range(4):
        for n in range(2):
            wg[x, :, :, :, n * 512 : n * 512 + 512] = (
                dot(tok_t[x * 512 : x * 512 + 512, :], gkv[:, n * 512 : n * 512 + 512])
                .astype(BF16)
                .reshape(4, 4, 32, 512)
            )

    far = (fara, farb, farc)

    def slab(part, spot, half=None):
        axis = ORDERS[part][0]
        index = [pick(None if half is None else Half(half))] + [slice(None)]
        index.insert(axis, spot)
        return wg.at[(*index, slice(None), pl.ds(*WIDE[part]))]

    def ring(part):
        axis = ORDERS[part][0]
        up, down = (mine[axis] + 1) % 4, (mine[axis] + 3) % 4
        beyond = (mine[axis] + 2) % 4
        above, below = list(mine), list(mine)
        above[axis], below[axis] = up, down
        moves = (
            (slab(part, beyond, 0), far[part].at[0], above),
            (slab(part, beyond, 1), far[part].at[1], below),
            (slab(part, up, 1), first[part].at[1, 2:4], above),
            (slab(part, down, 0), first[part].at[2, 0:2], below),
            (slab(part, up, 0), first[part].at[1, 0:2], above),
            (slab(part, down, 1), first[part].at[2, 2:4], below),
        )

        def move(n):
            src, dst, peer = moves[n]
            spot = part * 6 + n
            return remote(src, dst, p_s.at[spot], p_r.at[spot], chip_device(*pc.chip(*peer)))

        return [Later(functools.partial(move, n)) for n in range(6)]

    def add_far(part, spot, half):
        axis = ORDERS[part][0]
        columns = pl.ds(*WIDE[part])

        def body(n, carry):
            index = [half * 2 + n // 4, n % 4]
            index.insert(axis, spot)
            held = wg[(*index, slice(None), columns)].astype(F32)
            wg[(*index, slice(None), columns)] = (held + far[part][half, n // 4, n % 4].astype(F32)).astype(BF16)
            return carry

        lax.fori_loop(0, 8, body, 0)

    def copies(part, phase):
        axis = ORDERS[part][phase]
        for step in (1, 3, 2):
            peer = list(mine)
            peer[axis] = (peer[axis] + step) % 4
            spot = 18 + (part * 2 + phase - 1) * 3 + step - 1
            order = ORDERS[part]
            index = [
                peer[axis] if n == axis else slice(None) for n in range(3) if n not in order[:phase]
            ]
            yield remote(
                (once, twice)[phase - 1][part].at[tuple(index)],
                (second, third)[phase - 1][part].at[step],
                p_s.at[spot], p_r.at[spot], chip_device(*pc.chip(*peer)),
            )

    for part in range(3):
        sent = ring(part)
        for n in range(2):
            sent[n].start()
    gl_add(1)
    gl_start(2)
    gq_push.landed()
    grad = total_slots(gqp[all_rows, at256(pair)], recvgq, CHIPS)
    sq[core, q_spot[0], q_spot[1], q_spot[2], q_spot[3], pair] = (grad * rinv[:, :1]).astype(BF16)
    scaled = Gather(pc, sq.at[core], view_rows, sqa_s, sqa_r, True, PAIR_ORDERS, False)
    scaled.start(0)
    held_first = []
    for part in range(3):
        sent = ring(part)
        for n in range(2, 4):
            sent[n].start()
        copy = pltpu.make_async_copy(slab(part, mine[ORDERS[part][0]]), first[part].at[0], loc.at[7 + part])
        copy.start()
        held_first.append(copy)
    resampled.wait(2)
    la_sib = over(14, la.at[:, :, :, :, core], la.at[:, :, :, :, core], sib)
    la_sib.start()
    scaled.wait(0)
    scaled.start(1)
    gl_add(2)
    glf[pc.g] = lblk[...]
    l_part = over(13, lblk, glf.at[pc.g], partner)
    l_part.start()
    for part in range(3):
        sent = ring(part)
        place = mine[ORDERS[part][0]]
        sent[0].wait_recv()
        add_far(part, (place + 1) % 4, 0)
        sent[4].start()
        sent[1].wait_recv()
        add_far(part, (place + 3) % 4, 1)
        sent[5].start()
    scaled.wait(1)
    scaled.start(2)
    h_part.wait()
    la_sib.wait()
    gh_both = [turned(ghp[n]) for n in range(2)]

    def project_grad(n, carry):
        y, xl = n // 2, n % 2
        gpw[y, xl] = dot(la[0, y, xl].reshape(512, 256), gh_both[0]) + dot(
            la[1, y, xl].reshape(512, 256), gh_both[1]
        )
        return carry

    lax.fori_loop(0, 8, project_grad, 0)
    give_gpw = pltpu.make_async_copy(gpw, gpw_to, out_s.at[1])
    give_gpw.start()
    gga_push.drain()

    for part in range(3):
        held_first[part].wait()
        sent = ring(part)
        for n in range(2, 6):
            sent[n].wait_recv()
        src, dst = first[part], once[part]

        def add_first(n, carry, src=src, dst=dst):
            a, b = n // 4, n % 4
            dst[a, b] = sum(src[s, a, b].astype(F32) for s in range(3)).astype(BF16)
            return carry

        lax.fori_loop(0, 16, add_first, 0)
        for copy in copies(part, 1):
            copy.start()

    scaled.wait(2)
    s_sib2 = over(15, sq.at[core], sq.at[core], sib)
    s_sib2.start()
    l_part.wait()
    for phase in range(3):
        for copy in gl_copies(phase):
            copy.wait_send()
    gq_push.drain()
    for c in range(2):
        gow_t[:, c * 512 : c * 512 + 512] = dot(glf[0], attf[c, :256, :]) + dot(glf[1], attf[c, 256:, :])
    give_gow = pltpu.make_async_copy(gow_t, gow_to, out_s.at[2])
    give_gow.start()
    gain_part.wait()
    gain_row[...] = (gain_out[0] + gain_out[1]).T[:1, :]
    give_gain = pltpu.make_async_copy(gain_row, gain_to, out_s.at[3])
    give_gain.start()

    for part in range(3):
        for copy in copies(part, 1):
            copy.wait_recv()
        src, dst, held = second[part], twice[part], once[part]
        left = [axis for axis in range(3) if axis != ORDERS[part][0]]
        leading = left[0] == ORDERS[part][1]
        here = mine[ORDERS[part][1]]

        def add_second(n, carry, src=src, dst=dst, held=held, leading=leading, here=here):
            base = held[here, n] if leading else held[n, here]
            dst[n] = (base.astype(F32) + sum(src[s, n].astype(F32) for s in range(1, 4))).astype(BF16)
            return carry

        lax.fori_loop(0, 4, add_second, 0)
        for copy in copies(part, 2):
            copy.start()

    lt_part.wait()
    qo_sib.wait()
    s_sib2.wait()
    back = glf[pc.g].astype(F32)
    ratio = jnp.zeros((256, 128), F32)
    for c in range(2):
        for p in range(2):
            columns = pl.ds(c * 512 + p * 256, 256)
            blocks = [sq[c, n, :, :, :, p].reshape(256, 256) for n in range(2)]
            gqw[:, columns] = dot(ltp[0], blocks[0]) + dot(ltp[1], blocks[1])
            back = back + col_dot(qw[:, columns], sq[c, pc.g, :, :, :, p].reshape(256, 256))
    for p in range(2):
        for block, query in (
            (sq[core, pc.g, :, :, :, p], qg[pc.g, :, :, :, p]),
            (sq[1 - core, pc.g, :, :, :, p], qo[:, :, :, p]),
        ):
            prod = block.astype(F32).reshape(256, 256) * query.astype(F32).reshape(256, 256)
            ratio = ratio + prod[:, :128] + prod[:, 128:]
    coef = jnp.sum(ratio.T, axis=0, keepdims=True) * rinv_row / D_LAT
    gl_out[...] = back - coef * lt[...].astype(F32)
    give_gl = pltpu.make_async_copy(gl_out, gl_to, out_s.at[4])
    give_gl.start()
    give_gqw = pltpu.make_async_copy(gqw, gqw_to, out_s.at[5])
    give_gqw.start()
    for gather in (latents, output, resampled, scaled):
        gather.drain()

    for part in range(3):
        for copy in copies(part, 2):
            copy.wait_recv()
        here = mine[ORDERS[part][2]]
        fin[:, pl.ds(*WIDE[part])] = twice[part][here].astype(F32) + sum(
            third[part][s].astype(F32) for s in range(1, 4)
        )
    give = over(19, fin.at[at16(1 - core), :], oth, sib)
    give.start()

    def put(plane, rows):
        for n in range(2):
            spot = pl.multiple_of(n * 1024 + plane * 512, 512)
            gkw[:, pl.ds(spot, 512)] = rows[:13, n * 512 : n * 512 + 512]

    put(core, fin[at16(core), :])
    w_sib.wait_send()
    q_sib.wait_send()
    for part in range(3):
        for copy in ring(part):
            copy.wait_send()
        for phase in (1, 2):
            for copy in copies(part, phase):
                copy.wait_send()
    give.wait()
    put(1 - core, oth[...])
    give_gkw = pltpu.make_async_copy(gkw, gkw_to, out_s.at[6])
    give_gkw.start()
    for copy in (give_llm, give_gpw, give_gow, give_gain, give_gl, give_gqw, give_gkw):
        copy.wait()


def sems(*counts):
    return [pltpu.SemaphoreType.DMA((n,)) for n in counts]


def finish_kernel(*refs):
    got, done = refs[-2:]
    n = len(refs) // 3
    moves = []
    for i in range(n):
        src, dst, held = refs[i], refs[n + i], refs[2 * n + i]
        if len(src.shape) > 2:
            moves += [(src.at[m], held.at[m], dst.at[m]) for m in range(src.shape[0])]
        else:
            moves.append((src, held, dst))
    loads = [pltpu.make_async_copy(src, held, got.at[m]) for m, (src, held, dst) in enumerate(moves)]
    stores = [pltpu.make_async_copy(held, dst, done.at[m]) for m, (src, held, dst) in enumerate(moves)]
    for copy in loads:
        copy.start()
    for load, store in zip(loads, stores):
        load.wait()
        store.start()
    for copy in stores:
        copy.wait()


def local(
    tokens, keep_mask, shard_counts, latents, query_weight, keyval_weight, output_weight,
    project_weight, llm_gain, input_grad,
):
    widths = [w for _, w in WIDE]
    scratch = [
        ((256, 1664), BF16),
        ((13, 2048), BF16),
        ((64, 1024), BF16),
        ((64, 256), BF16),
        ((64, 1024), BF16),
        ((32, 2, 64, 128), BF16),
        ((256, 128), BF16),
        ((256, 128), BF16),
        ((64, 256), F32),
        ((64, 1024), F32),
        ((13, 2048), F32),
        ((64, 1024), F32),
        ((4, 2, 512, 128), F32),
        ((1, 128), F32),
        ((2, 128, 128), F32),
        ((256, 128), F32),
        ((2, 2, 256, 384), BF16),
        ((2, 16, 1024), BF16),
        ((128, 256), F32),
        ((4, 4, 4, 32, 1024), BF16),
        ((2, 256, 2048), BF16),
        ((2048, 512), BF16),
        ((2, 256, 128), F32),
        ((2, 256, 384), BF16),
        ((2, 256, 384), BF16),
        ((32, 16, 384), BF16),
        ((2, 4, 2, 2, 2, 16, 256), BF16),
        ((4, 2, 2, 2, 16, 256), BF16),
        ((4, 2, 4, 64, 512), BF16),
        ((4, 2, 4, 64, 256), BF16),
        ((2, 64, 256), BF16),
        ((2, 4, 2, 4, 2, 64, 256), BF16),
        ((512, 1024), BF16),
        ((512, 512), BF16),
        ((4, 512, 512), F32),
        ((4, 512, 512), BF16),
        ((2, 512, 384), BF16),
        ((64, 16, 384), BF16),
        ((16, 256), BF16),
        ((2, 512, 512), BF16),
        ((2, 128, 2048), BF16),
        ((32, 64, 128), BF16),
        ((136, 256), F32),
        ((136, 256), F32),
        ((128, 512), BF16),
        ((128, 512), BF16),
        ((128, 1024), BF16),
        ((128, 512), BF16),
        ((2, 8, 128), F32),
        ((8, 128), F32),
        ((32, 8, 128), F32),
        ((128, 256), BF16),
        ((128, 256), BF16),
        ((2, 128, 256), BF16),
        ((256, 512), BF16),
        ((32, 16, 256), BF16),
        ((4, 2, 4, 64, 256), BF16),
        ((3, 2, 4, 32, 256), BF16),
        ((3, 4, 2, 32, 256), BF16),
        ((2, 4, 32, 256), BF16),
        ((4, 2, 32, 256), BF16),
        ((2, 3, 2, 32, 256), BF16),
        ((2, 2, 32, 256), BF16),
        ((2, 32, 256), BF16),
        ((64, 256), BF16),
        ((2, 64, 256), BF16),
        ((16, 256), BF16),
        ((512, 512), BF16),
        ((4, 512, 512), BF16),
        ((512, 512), BF16),
        ((64, 16, 256), BF16),
        ((512, 1024), BF16),
        ((2, 2, 4, 2, 2, 2, 16, 256), BF16),
        *[((3, 4, 4, 32, w), BF16) for w in widths],
        *[((4, 4, 32, w), BF16) for w in widths],
        *[((4, 4, 32, w), BF16) for w in widths],
        *[((4, 32, w), BF16) for w in widths],
        *[((4, 32, w), BF16) for w in widths],
        *[((2, 2, 4, 32, w), BF16) for w in widths],
        ((32, 1024), F32),
        ((16, 1024), F32),
    ]
    results = [
        jax.ShapeDtypeStruct(shape, dtype)
        for shape, dtype in (
            ((256, 128), BF16),
            ((64, 256), F32),
            ((64, 1024), F32),
            ((13, 2048), F32),
            ((64, 1024), F32),
            ((4, 2, 512, 128), F32),
            ((1, 128), F32),
        )
    ]
    made = pl.pallas_call(
        whole_kernel,
        out_shape=results,
        in_specs=[VMEM] * 3 + [ANY] * 7,
        out_specs=[ANY] * 7,
        scratch_shapes=[pltpu.VMEM(s, d) for s, d in scratch]
        + sems(72, 72, 36, 36, 36, 36, 36, 36, 32, 32, 18, 18, 64, 64, 64, 64, 32, 32)
        + sems(32, 32, 14, 14, 64, 64, 64, 64, 18, 18, 36, 36, 20, 20, 20, 7),
        compiler_params=pltpu.CompilerParams(
            has_side_effects=True, vmem_limit_bytes=62 << 20, collective_id=0
        ),
        name="whole",
    )(
        keep_mask.reshape(1, 256), shard_counts.reshape(1, 1), llm_gain.reshape(1, 128), tokens,
        keyval_weight, query_weight, latents.T, output_weight.T, project_weight.reshape(32, 2, 64, 128),
        input_grad,
    )
    llm, gl, gqw, gkw, gow, gpw, gain = pl.pallas_call(
        finish_kernel,
        out_shape=results,
        in_specs=[ANY] * 7,
        out_specs=[ANY] * 7,
        scratch_shapes=[pltpu.VMEM(r.shape, r.dtype) for r in results] + sems(10, 10),
        compiler_params=pltpu.CompilerParams(vmem_limit_bytes=62 << 20),
        name="finish",
    )(*made)
    return (llm, gl.T, gqw, gkw, gow.T, gpw.reshape(4096, 128), gain.reshape(128))


def solution(mesh):
    in_specs = (
        P(("grp", "tp"), None),
        P(("grp", "tp")),
        P(("grp", "tp")),
        P("grp", "tp"),
        P("tp", None),
        P(("grp", "tp"), None),
        P(None, "tp"),
        P(None, "tp"),
        P("tp"),
        P("grp", "tp"),
    )
    out_specs = (
        P("grp", "tp"),
        P("grp", "tp"),
        P("tp", None),
        P(("grp", "tp"), None),
        P(None, "tp"),
        P(None, "tp"),
        P("tp"),
    )
    return jax.shard_map(local, mesh=mesh, in_specs=in_specs, out_specs=out_specs, check_vma=False)
```

```python
import functools
import math

import jax
import jax.numpy as jnp
import numpy as np
from jax import lax
from jax.experimental import pallas as pl
from jax.experimental.pallas import tpu as pltpu
from jax.sharding import PartitionSpec as P

D_LAT = 4096
HEAD_DIM = 128
D_LLM = 8192
SCORE_CAP = 5.0
SCALE = 1.0 / math.sqrt(HEAD_DIM)
CHIPS = 64
GROUP = 32

F32 = jnp.float32
BF16 = jnp.bfloat16
MESH = pl.DeviceIdType.MESH
ANY = pl.BlockSpec(memory_space=pl.ANY)
VMEM = pl.BlockSpec(memory_space=pltpu.VMEM)

ORDERS = ((2, 1, 0), (1, 0, 2), (0, 2, 1))
WIDE = ((0, 384), (384, 384), (768, 256))
SPLIT = ((0, 256), (256, 128), (384, 128), (512, 128), (640, 128), (768, 256))
SPLIT_ORDERS = ORDERS + ORDERS
KEYS, VALUES = (0, 1, 2), (3, 4, 5)
COLUMNS_512 = ((0, 128), (128, 256), (384, 128))
ROWS_64 = ((0, 16), (16, 32), (48, 16))
ROWS_OWN = ((0, 16), (16, 16), (32, 32))
PAIR_ORDERS = ((2, 1, 0), (1, 0, 2))


def row_dot(left, right):
    return lax.dot_general(left, right, (((0,), (0,)), ((), ())), preferred_element_type=F32)


def col_dot(left, right):
    return lax.dot_general(left, right, (((1,), (1,)), ((), ())), preferred_element_type=F32)


def dot(left, right):
    return jnp.dot(left, right, preferred_element_type=F32)


class Place:
    def __init__(self):
        self.g = lax.axis_index("grp")
        self.t = lax.axis_index("tp")
        self.core = self.t % 2
        self.j = self.t // 2
        self.z = self.j % 4
        self.xl = (self.j // 4) % 2
        self.y = self.j // 8
        self.x = self.g * 2 + self.xl

    def chip(self, x, y, z):
        return x // 2, (y * 2 + x % 2) * 4 + z

    def plane_peer(self, k):
        return self.chip((self.x + k // 16) % 4, (self.y + (k // 4) % 4) % 4, (self.z + k % 4) % 4)

    def group_peer(self, k):
        y = (self.y + k // 8) % 4
        xl = (self.xl + (k // 4) % 2) % 2
        z = (self.z + k % 4) % 4
        return (y * 2 + xl) * 4 + z

    def sibling(self):
        return self.g, self.j * 2 + 1 - self.core


def remote(src, dst, sends, recvs, device):
    return pltpu.make_async_remote_copy(
        src_ref=src, dst_ref=dst, send_sem=sends, recv_sem=recvs, device_id=device, device_id_type=MESH
    )


class Later:
    def __init__(self, make):
        self.make = make

    def start(self):
        self.make().start()

    def wait_recv(self):
        self.make().wait_recv()

    def wait_send(self):
        self.make().wait_send()


def each_peer(n, do):
    def body(k, carry):
        do(k)
        return carry

    lax.fori_loop(1, n, body, 0, unroll=9 if n == 64 else 31)


class Gather:
    def __init__(self, place, ref, view, sends, recvs, whole=True, orders=ORDERS, ring=True):
        self.place, self.ref, self.view, self.sends, self.recvs = place, ref, view, sends, recvs
        self.whole, self.orders, self.ring = whole, orders, ring

    def copies(self, phase, parts=None):
        pc = self.place
        mine = [pc.x, pc.y, pc.z]
        for part in self.parts(parts):
            order = self.orders[part]
            held = list(mine)
            for axis in order[:phase]:
                held[axis] = None
            block = self.view(self.ref, *held, part)
            near = order[phase] == 0 and not self.whole
            for step in (1,) if near else (1, 3, 2):
                peer = list(mine)
                if near:
                    peer[0] = pc.g * 2 + 1 - pc.xl
                else:
                    peer[order[phase]] = (peer[order[phase]] + step) % 4
                yield self.push(block, (part * (2 if self.ring else 3) + phase) * 3 + step - 1, peer)

    def push(self, block, spot, peer):
        g, j = self.place.chip(*peer)
        device = (g, j * 2 + self.place.core)
        return Later(lambda: remote(block, block, self.sends.at[spot], self.recvs.at[spot], device))

    def last(self, part):
        pc = self.place
        order = self.orders[part]
        axis = order[2]
        mine = [pc.x, pc.y, pc.z]
        base = (len(self.orders) + part) * 6
        if axis == 0 and not self.whole:
            held = [mine[0], None, None]
            block = self.view(self.ref, *held, part)
            return [self.push(block, base, [pc.g * 2 + 1 - pc.xl, pc.y, pc.z])]

        def at(place, half):
            held = [None, None, None]
            held[axis] = place
            held[order[0]] = Half(half)
            return self.view(self.ref, *held, part)

        here, up, down = mine[axis], (mine[axis] + 1) % 4, (mine[axis] + 3) % 4
        above, below = list(mine), list(mine)
        above[axis], below[axis] = up, down
        return [
            self.push(at(here, 0), base, above),
            self.push(at(here, 1), base + 1, above),
            self.push(at(here, 1), base + 2, below),
            self.push(at(here, 0), base + 3, below),
            self.push(at(down, 0), base + 4, above),
            self.push(at(up, 1), base + 5, below),
        ]

    def parts(self, some):
        return range(len(self.orders)) if some is None else some

    def start(self, phase, parts=None):
        if phase < 2 or not self.ring:
            for copy in self.copies(phase, parts):
                copy.start()
            return
        for part in self.parts(parts):
            copies = self.last(part)
            for n in (0,) if len(copies) == 1 else (0, 2, 1, 3):
                copies[n].start()

    def relay(self, parts=None):
        for part in self.parts(parts):
            copies = self.last(part)
            if len(copies) > 1:
                copies[0].wait_recv()
                copies[4].start()
                copies[2].wait_recv()
                copies[5].start()

    def wait(self, phase, parts=None):
        if phase < 2 or not self.ring:
            for copy in self.copies(phase, parts):
                copy.wait_recv()
            return
        for part in self.parts(parts):
            copies = self.last(part)
            for n in (0,) if len(copies) == 1 else (1, 3, 4, 5):
                copies[n].wait_recv()

    def drain(self):
        for phase in range(2 if self.ring else 3):
            for copy in self.copies(phase):
                copy.wait_send()
        for part in self.parts(None) if self.ring else ():
            for copy in self.last(part):
                copy.wait_send()


class Half:
    def __init__(self, n):
        self.n = n


def pick(value):
    if isinstance(value, Half):
        return slice(value.n * 2, value.n * 2 + 2)
    return slice(None) if value is None else value


def halves(x):
    if isinstance(x, Half):
        return x.n, slice(None)
    return (slice(None), slice(None)) if x is None else (x // 2, x % 2)


def in_group(x):
    if isinstance(x, Half):
        return slice(x.n, x.n + 1)
    return slice(None) if x is None else x % 2


def view_weight(ref, x, y, z, part):
    return ref.at[pick(x), pick(y), pick(z), :, pl.ds(*SPLIT[part])]


def view_output(ref, x, y, z, part):
    return ref.at[pick(y), in_group(x), pick(z), :, pl.ds(*COLUMNS_512[part])]


def view_own(ref, x, y, z, part):
    return ref.at[pick(y), in_group(x), pick(z), pl.ds(*ROWS_OWN[part]), :]


def view_rows(ref, x, y, z, part):
    hi, lo = halves(x)
    up, pair = halves(z)
    return ref.at[hi, pick(y), lo, up, pair, :, pl.ds(part * 128, 128)]


def view_latents(core, ref, x, y, z, part):
    hi, lo = halves(x)
    return ref.at[hi, pick(y), lo, pick(z), core, pl.ds(*ROWS_64[part]), :]


def total_slots(own, slots, n):
    def body(k, total):
        return total + slots[k].astype(F32)

    return lax.fori_loop(1, n, body, own.astype(F32), unroll=9 if n == 64 else 31)


class Pushes:
    def __init__(self, n, make):
        self.n, self.make = n, make

    def start(self):
        each_peer(self.n, lambda k: self.make(k).start())

    def landed(self):
        each_peer(self.n, lambda k: self.make(k).wait_recv())

    def drain(self):
        each_peer(self.n, lambda k: self.make(k).wait_send())


class PairPushes(Pushes):
    def __init__(self, place, make):
        super().__init__(CHIPS, make)
        self.place = place

    def start_pair(self, p):
        def body(i, carry):
            k = (i // 2) * 4 + (i % 2) * 2 + (self.place.z + p) % 2

            @pl.when(k > 0)
            def _():
                self.make(k).start()

            return carry

        lax.fori_loop(0, 32, body, 0, unroll=4)


def at16(n):
    return pl.ds(pl.multiple_of(n * 16, 16), 16)


def at256(n):
    return pl.ds(pl.multiple_of(n * 256, 256), 256)


def heads_of(ref, pair, side):
    return ref[:, :, :, :, pair, :, side * 128 : side * 128 + 128].reshape(512, 128)


def turned(value, dtype=BF16):
    return value.astype(F32).T.astype(dtype)


def whole_kernel(
    keep, count, gain_in, tokens_in, keyval_in, qw_in, lt_in, owt_in, pw_in, igrad_in,
    llm_to, gl_to, gqw_to, gkw_to, gow_to, gpw_to, gain_to,
    tokens, keyval_w, qw, lt, owt, pw, igrad, llm, gl_out, gqw, gkw, gow_t, gpw, gain_row, gain_out,
    val, qpart, wpl, gain,
    wg, tokb, tok_t, valb, qx, qsum, recvq, qg, qo, owe, lown, ltp, la, kv, kv_t, fac, half, npk, recvn, tot_all, tots, rtot,
    ablk, attf, pw_t, pwx, lat_s, lat_x, fold_s, fold_x, fold, foldx, sumx, sumo, sumr, gh_t, ghx, ghp, gap, recvg, glp, u1a, u1b, v1a, v1b, u2, v2, u3,
    lblk, glf, gblk, gg, ds, gqp, recvgq, gkv, sq, r1a, r1b, r1c, s1a, s1b, s1c,
    r2a, r2b, r2c, s2a, s2b, s2c, r3a, r3b, r3c, fara, farb, farc, fin, oth,
    w_s, w_r, ow_s, ow_r, lo_s, lo_r, l_s, l_r, q_s, q_r, qa_s, qa_r, n_s, n_r, a_s, a_r, t_s, t_r,
    g_s, g_r, gl_s, gl_r, tot_s, tot_r, gga_s, gga_r, gq_s, gq_r, sqa_s, sqa_r, p_s, p_r, x_s, x_r, loc, out_s,
):
    pc = Place()
    core = pc.core
    sib = pc.sibling()
    partner = (1 - pc.g, pc.t)
    mine = [pc.x, pc.y, pc.z]
    pair = pc.j % 2
    own_rows = at16(pc.j // 2)
    all_rows = at16(pc.g * 16 + pc.j // 2)

    def chip_device(g, j):
        return (g, j * 2 + core)

    def over(index, src, dst, device):
        return remote(src, dst, x_s.at[index], x_r.at[index], device)

    barrier = pltpu.get_barrier_semaphore()

    def greet(k):
        pl.semaphore_signal(barrier, inc=1, device_id=chip_device(*pc.plane_peer(k)), device_id_type=MESH)

    pl.semaphore_signal(barrier, inc=1, device_id=sib, device_id_type=MESH)
    each_peer(CHIPS, greet)

    loads = [
        pltpu.make_async_copy(src, dst, loc.at[12 + n])
        for n, (src, dst) in enumerate(
            (
                (keyval_in, keyval_w), (lt_in, lt), (qw_in, qw), (owt_in, owt),
                (tokens_in, tokens), (pw_in, pw), (igrad_in, igrad),
            )
        )
    ]
    for copy in loads:
        copy.start()
    loads[0].wait()

    rows_f32 = jnp.concatenate([keyval_w[...].astype(F32), jnp.zeros((3, 2048), F32)], axis=0).astype(BF16)
    for c in range(2):
        wpl[c, :, :512] = rows_f32[:, c * 512 : c * 512 + 512]
        wpl[c, :, 512:] = rows_f32[:, 1024 + c * 512 : 1536 + c * 512]
    w_own = pltpu.make_async_copy(wpl.at[core], wg.at[pc.x, pc.y, pc.z, at16(core)], loc.at[3])
    w_own.start()
    for copy in loads[1:]:
        copy.wait()
    feats_f32 = lt[...].astype(F32)
    lat = feats_f32.T.astype(BF16)
    squares = jnp.sum(feats_f32 * feats_f32, axis=0, keepdims=True)
    squares = jnp.broadcast_to(squares, (128, 256)).T.astype(BF16)
    for c in range(2):
        for p in range(2):
            columns = (c * 2 + p) * 256
            qpart[c, p, :, :256] = dot(lat, qw[:, columns : columns + 256]).astype(BF16)
            qpart[c, p, :, 256:] = squares
    spot = lax.broadcasted_iota(jnp.int32, (1, 256), 1)
    kept = ((keep[...] == 1) | (spot == 0)) & (spot < count[...])
    val[...] = jnp.broadcast_to(jnp.where(kept, 1.0, 0.0), (128, 256)).T
    gain[...] = jnp.broadcast_to(gain_in[...].astype(F32), (256, 128)).T

    pl.semaphore_wait(barrier, CHIPS)

    w_sib = over(0, wpl.at[1 - core], wg.at[pc.x, pc.y, pc.z, at16(core)], sib)
    w_sib.start()

    q_sib = over(1, qpart.at[1 - core], qx, sib)
    q_sib.start()
    weight = Gather(pc, wg, view_weight, w_s, w_r, True, SPLIT_ORDERS)
    output = Gather(pc, owe, view_output, ow_s, ow_r, False)
    latents = Gather(pc, lown, view_own, lo_s, lo_r, False)
    resampled = Gather(pc, la, functools.partial(view_latents, core), l_s, l_r)
    w_own.wait()
    w_sib.wait_recv()
    weight.start(0)
    group_half = pl.ds(pl.multiple_of(pc.g * 512, 512), 512)
    local_copies = [
        pltpu.make_async_copy(owt.at[:, group_half], owe.at[pc.y, pc.xl, pc.z], loc.at[0]),
        pltpu.make_async_copy(lt, lown.at[pc.y, pc.xl, pc.z], loc.at[1]),
        pltpu.make_async_copy(lt, ltp.at[pc.g], loc.at[11]),
        pltpu.make_async_copy(val, valb.at[core], loc.at[2]),
    ]
    for copy in local_copies:
        copy.start()

    q_sib.wait_recv()
    for p in range(2):
        qsum[p] = (qpart[core, p].astype(F32) + qx[p].astype(F32)).astype(BF16)

    def q_copy(k):
        j = pc.group_peer(k)
        return remote(
            qsum.at[j % 2, at16(j // 2), :], recvq.at[k], q_s.at[k], q_r.at[k], chip_device(pc.g, j)
        )

    q_push = Pushes(GROUP, q_copy)
    q_push.start()

    for block in range(16):
        x, y = block // 4, block % 4
        begin = (((x // 2) * 4 + y) * 2 + x % 2) * 104
        base = begin // 128 * 128
        width = min(256, 1664 - base)
        row = lax.broadcasted_iota(jnp.int32, (width, 128), 0)
        col = lax.broadcasted_iota(jnp.int32, (width, 128), 1)
        rest = col & 15
        hit = (row == (begin - base) + (col >> 4) * 13 + rest) & (rest < 13)
        place = jnp.where(hit, 1.0, 0.0).astype(BF16)
        tokb[core, :, pl.ds(block * 128, 128)] = dot(tokens[:, pl.ds(base, width)], place).astype(BF16)

    t_sib = over(2, tokb.at[core], tokb.at[core], sib)
    t_sib.start()
    for copy in local_copies:
        copy.wait()
    latents.start(0)
    output.start(0)
    v_sib = over(3, val, valb.at[core], sib)
    v_sib.start()
    pw_sib = over(4, pw.at[:, 1 - core], pwx, sib)
    pw_sib.start()
    weight.wait(0)
    weight.start(1)
    for y in range(4):
        pw_t[0, :, pl.ds(y * 512, 512)] = turned(pw[pl.ds(y * 8, 8), core].reshape(512, 128))
    latents.wait(0)
    latents.start(1)
    output.wait(0)
    output.start(1)
    q_push.landed()
    total = total_slots(qsum[pair, own_rows, :], recvq, GROUP)
    rinv = lax.rsqrt(total[:, 256:] / D_LAT + 1e-06)
    proj = total[:, :256]
    q_spot = (pc.g, pc.y, pc.xl, pc.z // 2, pair)
    qg[q_spot] = (proj * rinv[:, :1]).astype(BF16)
    queries = Gather(pc, qg, view_rows, qa_s, qa_r, True, PAIR_ORDERS, False)
    queries.start(0)
    weight.wait(1)
    weight.start(2, KEYS)
    queries.wait(0)
    queries.start(1)
    weight.start(2, VALUES)
    queries.wait(1)
    queries.start(2)
    t_sib.wait()
    v_sib.wait()
    for block in range(2):
        tok_t[pl.ds(block * 512, 512), :] = turned(
            tokb[:, :, pl.ds(block * 512, 512)].reshape(512, 512)
        )
    weight.relay(KEYS)
    for block in range(2, 4):
        tok_t[pl.ds(block * 512, 512), :] = turned(
            tokb[:, :, pl.ds(block * 512, 512)].reshape(512, 512)
        )
    pw_sib.wait()
    for y in range(4):
        pw_t[1, :, pl.ds(y * 512, 512)] = turned(pwx[pl.ds(y * 8, 8)].reshape(512, 128))
    lt_part = over(16, lt, ltp.at[pc.g], partner)
    lt_part.start()
    q_push.drain()
    weight.relay(VALUES)
    weight.wait(2, KEYS)
    latents.wait(1)
    latents.start(2)
    output.wait(1)
    output.start(2)

    tok = tokb[...].reshape(512, 2048)

    def project(n, carry):
        columns = at256(n)
        kv[:, columns] = dot(tok, wg[:, :, :, :, columns].reshape(2048, 256)).astype(BF16)
        return carry

    lax.fori_loop(0, 2, project, 0)
    queries.wait(2)
    qo_sib = over(17, qg.at[pc.g], qo, sib)
    qo_sib.start()
    totals = []
    for head in range(4):
        query = heads_of(qg, head // 2, head % 2)
        total = jnp.zeros((1, 512), F32)
        for chunk in range(4):
            slots = pl.ds(chunk * 128, 128)
            raw = col_dot(kv[slots, head * 128 : head * 128 + 128], query)
            squash = jnp.tanh(raw * (SCALE / SCORE_CAP))
            kept = valb[chunk // 2, pl.ds(chunk % 2 * 128, 128), :][:, :1]
            weights = jnp.exp(SCORE_CAP * squash) * kept
            half[head, slots, :] = weights.astype(BF16)
            fac[head, slots, :] = weights * (1.0 - squash * squash) * SCALE
            total = total + jnp.sum(weights, axis=0, keepdims=True)
        totals.append(total)
    weight.wait(2, VALUES)
    lax.fori_loop(2, 4, project, 0)

    def n_copy(k):
        g, j = pc.plane_peer(k)
        return remote(
            npk.at[j % 2, at16(g * 16 + j // 2), :], recvn.at[k], n_s.at[k], n_r.at[k], chip_device(g, j)
        )

    def tot_copy(k):
        g, j = pc.plane_peer(k)
        return remote(
            tots.at[g * 2 + j // 16, pl.ds(j % 2 * 2, 2)], rtot.at[k], tot_s.at[k], tot_r.at[k], chip_device(g, j)
        )

    n_push = PairPushes(pc, n_copy)
    tot_push = Pushes(CHIPS, tot_copy)
    tot_all[...] = jnp.concatenate(totals + [jnp.zeros((4, 512), F32)], axis=0)
    for head in range(4):
        for n in range(4):
            tots[n, head] = tot_all[head : head + 1, n * 128 : n * 128 + 128]
    for p in range(2):
        heads = (p * 2, p * 2 + 1)
        packed = [
            dot(turned(kv[:, 512 + head * 128 : 640 + head * 128]), half[head]) for head in heads
        ]
        npk[p] = jnp.concatenate(packed, axis=0).T.astype(BF16)
        n_push.start_pair(p)
    tot_push.start()

    latents.relay()
    output.relay()
    for n in range(2):
        kv_t[pl.ds(n * 256, 256), :] = turned(kv[:, n * 256 : n * 256 + 256])
    weight.drain()
    queries.drain()
    n_push.landed()
    total = total_slots(npk[pair, all_rows, :], recvn, CHIPS)
    tot_push.landed()

    def add_rows(k, held):
        return (held[0] + rtot[k, 0], held[1] + rtot[k, 1])

    here = pc.g * 2 + pc.j // 16
    row_sums = lax.fori_loop(1, CHIPS, add_rows, (tots[here, pair * 2], tots[here, pair * 2 + 1]))
    row = lax.broadcasted_iota(jnp.int32, (16, 128), 0)
    hit = lax.broadcasted_iota(jnp.int32, (16, 128), 1) == row + (pc.j // 2) % 8 * 16
    whole = jnp.concatenate(
        [
            jnp.broadcast_to(
                jnp.sum(jnp.where(hit, row_sums[n], 0.0), axis=1, keepdims=True), (16, 128)
            )
            for n in range(2)
        ],
        axis=1,
    )
    ablk[...] = (total / whole).astype(BF16)
    a_spot = attf.at[core, all_rows, at256(pair)]
    a_push = Pushes(
        CHIPS,
        lambda k: remote(ablk, a_spot, a_s.at[k], a_r.at[k], chip_device(*pc.plane_peer(k))),
    )
    a_push.start()
    a_own = pltpu.make_async_copy(ablk, a_spot, loc.at[5])
    a_own.start()

    n_push.drain()
    tot_push.drain()
    latents.wait(2)
    feats = lown[...].reshape(2048, 256)
    lat_s[:128, :] = dot(pw_t[1], feats)
    squares = jnp.zeros((1, 256), F32)
    for y in range(4):
        block = lown[y].reshape(512, 256).astype(F32)
        squares = squares + jnp.sum(block * block, axis=0, keepdims=True)
    lat_s[128:, :] = jnp.broadcast_to(squares, (8, 256))
    lat_sib = over(5, lat_s, lat_x, sib)
    lat_sib.start()
    hidden = dot(pw_t[0], feats)
    output.wait(2)

    rows = owe[...].reshape(2048, 512)
    fold_s[...] = dot(pw_t[1], rows).astype(BF16)
    fold_sib = over(6, fold_s, fold_x, sib)
    fold_sib.start()
    folded = dot(pw_t[0], rows)
    fold_sib.wait()
    fold[:, group_half] = (folded + fold_x[...].astype(F32)).astype(BF16)
    f_part = over(18, fold.at[:, group_half], fold.at[:, group_half], partner)
    f_part.start()
    lat_sib.wait()
    hidden = hidden + lat_x[:128, :]
    rinv_row = lax.rsqrt((squares + lat_x[128:129, :]) / D_LAT + 1e-06)
    a_own.wait()
    a_push.landed()
    a_sib = over(7, attf.at[core], attf.at[core], sib)
    a_sib.start()
    f_part.wait()
    f_sib = over(8, fold.at[:, pl.ds(pl.multiple_of((1 - core) * 512, 512), 512)], foldx, sib)
    f_sib.start()
    a_sib.wait()
    group_rows = at256(pc.g)
    hidden = hidden + col_dot(fold[:, :512], attf[0, group_rows, :])
    hidden = (hidden + col_dot(fold[:, 512:], attf[1, group_rows, :])).astype(BF16).astype(F32)
    grad_y = igrad[...].astype(F32).T
    scaled_dy = grad_y * gain[...]
    square_row = jnp.sum(hidden * hidden, axis=0, keepdims=True)
    inner_row = jnp.sum(hidden * scaled_dy, axis=0, keepdims=True)
    sumo[...] = jnp.concatenate(
        [
            square_row[:, :128], square_row[:, 128:], inner_row[:, :128], inner_row[:, 128:],
            jnp.zeros((4, 128), F32),
        ],
        axis=0,
    )
    s_sib = over(9, sumo, sumx.at[0], sib)
    s_sib.start()
    s_sib.wait()
    sumx[1] = sumx[0] + sumo[...]
    t_push = Pushes(
        GROUP,
        lambda k: remote(sumx.at[1], sumr.at[k], t_s.at[k], t_r.at[k], chip_device(pc.g, pc.group_peer(k))),
    )
    t_push.start()
    lat_out = lt[...].astype(F32) + col_dot(owt[:, :512], attf[0, group_rows, :])
    la[pc.g, pc.y, pc.xl, pc.z, core] = (lat_out + col_dot(owt[:, 512:], attf[1, group_rows, :])).astype(BF16)
    resampled.start(0)
    resampled.wait(0)
    resampled.start(1)
    t_push.landed()
    total = total_slots(sumx[1], sumr, GROUP)
    square_row = jnp.concatenate([total[0:1], total[1:2]], axis=1)
    inner_row = jnp.concatenate([total[2:3], total[3:4]], axis=1)
    hrinv = lax.rsqrt(square_row / D_LLM + 1e-05)
    normed = hidden * hrinv
    llm[...] = turned(normed * gain[...])
    give_llm = pltpu.make_async_copy(llm, llm_to, out_s.at[0])
    give_llm.start()
    gain_own = jnp.broadcast_to(jnp.sum(grad_y * normed, axis=1, keepdims=True), (128, 128))
    grad_h = hrinv * scaled_dy - (hrinv * hrinv * hrinv / D_LLM * inner_row) * hidden
    gh_t[...] = grad_h.astype(BF16)
    h_sib = over(10, gh_t, ghx, sib)
    h_sib.start()
    ghp[pc.g] = gh_t[...]
    h_part = over(11, gh_t, ghp.at[pc.g], partner)
    h_part.start()
    gain_out[pc.g] = gain_own
    gain_part = over(12, gain_out.at[pc.g], gain_out.at[pc.g], partner)
    gain_part.start()

    f_sib.wait()
    own_half = fold[:, pl.ds(pl.multiple_of(core * 512, 512), 512)]
    partial = dot(turned(gh_t[...]), own_half)
    h_sib.wait()
    gap[...] = (partial + dot(turned(ghx[...]), foldx[...])).astype(BF16)

    def g_copy(k):
        j = pc.group_peer(k)
        return remote(
            gap.at[at16(j // 2), at256(j % 2)], recvg.at[k], g_s.at[k], g_r.at[k], chip_device(pc.g, j)
        )

    g_push = Pushes(GROUP, g_copy)
    g_push.start()

    resampled.wait(1)
    resampled.start(2)

    for n in range(4):
        part = dot(pw[pl.ds(n * 8, 8), core].reshape(512, 128), gh_t[...])
        part = part + dot(pwx[pl.ds(n * 8, 8)].reshape(512, 128), ghx[...])
        glp[n] = part.astype(BF16).reshape(2, 4, 64, 256)

    def gl_copies(phase):
        for part in range(2):
            axis = ((1, 2), (2, 1))[part][phase] if phase < 2 else 0
            for step in (1, 3, 2) if phase < 2 else (1,):
                peer = list(mine)
                if phase < 2:
                    peer[axis] = (peer[axis] + step) % 4
                else:
                    peer[0] = pc.g * 2 + 1 - pc.xl
                spot = part * 7 + phase * 3 + step - 1
                if phase == 0:
                    rows = pl.ds(part * 32, 32)
                    src = glp.at[peer[1], :, :, rows] if axis == 1 else glp.at[:, :, peer[2], rows]
                    dst = (u1a, u1b)[part].at[step - 1]
                elif phase == 1:
                    src = v1a.at[:, peer[2]] if axis == 2 else v1b.at[peer[1]]
                    dst = u2.at[part, step - 1]
                else:
                    src, dst = v2.at[part, 1 - pc.xl], u3.at[part]
                yield remote(src, dst, gl_s.at[spot], gl_r.at[spot], chip_device(*pc.chip(*peer)))

    def gl_start(phase):
        for copy in gl_copies(phase):
            copy.start()

    def gl_add(phase):
        for copy in gl_copies(phase):
            copy.wait_recv()
        if phase == 0:
            for n in range(4):
                for xl in range(2):
                    own = glp[pc.y, xl, n, :32, :].astype(F32)
                    v1a[xl, n] = (own + sum(u1a[i, xl, n].astype(F32) for i in range(3))).astype(BF16)
                    own = glp[n, xl, pc.z, 32:, :].astype(F32)
                    v1b[n, xl] = (own + sum(u1b[i, n, xl].astype(F32) for i in range(3))).astype(BF16)
        elif phase == 1:
            for xl in range(2):
                for part, own in ((0, v1a[xl, pc.z]), (1, v1b[pc.y, xl])):
                    added = own.astype(F32) + sum(u2[part, i, xl].astype(F32) for i in range(3))
                    v2[part, xl] = added.astype(BF16)
        else:
            for part in range(2):
                added = v2[part, pc.xl].astype(F32) + u3[part].astype(F32)
                lblk[part * 32 : part * 32 + 32, :] = added.astype(BF16)

    g_push.landed()
    grad = total_slots(gap[own_rows, at256(pair)], recvg, GROUP).astype(BF16).astype(F32)
    gblk[...] = (grad / whole).astype(BF16)
    g_spot = gg.at[all_rows, at256(pair)]
    gga_push = Pushes(
        CHIPS,
        lambda k: remote(gblk, g_spot, gga_s.at[k], gga_r.at[k], chip_device(*pc.plane_peer(k))),
    )
    gga_push.start()
    gl_start(0)
    g_own = pltpu.make_async_copy(gblk, g_spot, loc.at[6])
    g_own.start()
    resampled.relay()
    for push in (a_push, t_push, g_push):
        push.drain()
    g_own.wait()
    gga_push.landed()

    def gq_copy(k):
        g, j = pc.plane_peer(k)
        return remote(
            gqp.at[at16(g * 16 + j // 2), at256(j % 2)], recvgq.at[k], gq_s.at[k], gq_r.at[k], chip_device(g, j)
        )

    gq_push = PairPushes(pc, gq_copy)
    ones = jnp.ones((8, 128), BF16)
    for p in range(2):
        parts = []
        for head in (p * 2, p * 2 + 1):
            columns = pl.ds(head * 128, 128)
            grads = gg[:, columns]
            prod = grads.astype(F32) * attf[core, :, columns].astype(F32)
            high = prod.astype(BF16)
            rest = (prod - high.astype(F32)).astype(BF16)
            delta = (col_dot(ones, high) + col_dot(ones, rest))[:1, :].astype(BF16).astype(F32)
            for chunk in range(4):
                slots = pl.ds(chunk * 128, 128)
                prob = col_dot(kv[slots, 512 + head * 128 : 640 + head * 128], grads)
                ds[head, slots, :] = (fac[head, slots, :] * (prob - delta)).astype(BF16)
            parts.append(dot(kv_t[pl.ds(head * 128, 128), :], ds[head]))
        gqp[:, p * 256 : p * 256 + 256] = jnp.concatenate(parts, axis=0).T.astype(BF16)
        gq_push.start_pair(p)
    gl_add(0)
    gl_start(1)
    for head in range(4):
        columns = pl.ds(head * 128, 128)
        gkv[:, columns] = dot(ds[head], heads_of(qg, head // 2, head % 2)).astype(BF16)
        gkv[:, 512 + head * 128 : 640 + head * 128] = dot(half[head], gg[:, columns]).astype(BF16)

    first, once = (r1a, r1b, r1c), (s1a, s1b, s1c)
    second, twice = (r2a, r2b, r2c), (s2a, s2b, s2c)
    third = (r3a, r3b, r3c)

    for x in range(4):
        for n in range(2):
            wg[x, :, :, :, n * 512 : n * 512 + 512] = (
                dot(tok_t[x * 512 : x * 512 + 512, :], gkv[:, n * 512 : n * 512 + 512])
                .astype(BF16)
                .reshape(4, 4, 32, 512)
            )

    far = (fara, farb, farc)

    def slab(part, spot, half=None):
        axis = ORDERS[part][0]
        index = [pick(None if half is None else Half(half))] + [slice(None)]
        index.insert(axis, spot)
        return wg.at[(*index, slice(None), pl.ds(*WIDE[part]))]

    def ring(part):
        axis = ORDERS[part][0]
        up, down = (mine[axis] + 1) % 4, (mine[axis] + 3) % 4
        beyond = (mine[axis] + 2) % 4
        above, below = list(mine), list(mine)
        above[axis], below[axis] = up, down
        moves = (
            (slab(part, beyond, 0), far[part].at[0], above),
            (slab(part, beyond, 1), far[part].at[1], below),
            (slab(part, up, 1), first[part].at[1, 2:4], above),
            (slab(part, down, 0), first[part].at[2, 0:2], below),
            (slab(part, up, 0), first[part].at[1, 0:2], above),
            (slab(part, down, 1), first[part].at[2, 2:4], below),
        )

        def move(n):
            src, dst, peer = moves[n]
            spot = part * 6 + n
            return remote(src, dst, p_s.at[spot], p_r.at[spot], chip_device(*pc.chip(*peer)))

        return [Later(functools.partial(move, n)) for n in range(6)]

    def add_far(part, spot, half):
        axis = ORDERS[part][0]
        columns = pl.ds(*WIDE[part])

        def body(n, carry):
            index = [half * 2 + n // 4, n % 4]
            index.insert(axis, spot)
            held = wg[(*index, slice(None), columns)].astype(F32)
            wg[(*index, slice(None), columns)] = (held + far[part][half, n // 4, n % 4].astype(F32)).astype(BF16)
            return carry

        lax.fori_loop(0, 8, body, 0)

    def copies(part, phase):
        axis = ORDERS[part][phase]
        for step in (1, 3, 2):
            peer = list(mine)
            peer[axis] = (peer[axis] + step) % 4
            spot = 18 + (part * 2 + phase - 1) * 3 + step - 1
            order = ORDERS[part]
            index = [
                peer[axis] if n == axis else slice(None) for n in range(3) if n not in order[:phase]
            ]
            yield remote(
                (once, twice)[phase - 1][part].at[tuple(index)],
                (second, third)[phase - 1][part].at[step],
                p_s.at[spot], p_r.at[spot], chip_device(*pc.chip(*peer)),
            )

    for part in range(3):
        sent = ring(part)
        for n in range(2):
            sent[n].start()
    gl_add(1)
    gl_start(2)
    gq_push.landed()
    grad = total_slots(gqp[all_rows, at256(pair)], recvgq, CHIPS)
    sq[core, q_spot[0], q_spot[1], q_spot[2], q_spot[3], pair] = (grad * rinv[:, :1]).astype(BF16)
    scaled = Gather(pc, sq.at[core], view_rows, sqa_s, sqa_r, True, PAIR_ORDERS, False)
    scaled.start(0)
    held_first = []
    for part in range(3):
        sent = ring(part)
        for n in range(2, 4):
            sent[n].start()
        copy = pltpu.make_async_copy(slab(part, mine[ORDERS[part][0]]), first[part].at[0], loc.at[7 + part])
        copy.start()
        held_first.append(copy)
    resampled.wait(2)
    la_sib = over(14, la.at[:, :, :, :, core], la.at[:, :, :, :, core], sib)
    la_sib.start()
    scaled.wait(0)
    scaled.start(1)
    gl_add(2)
    glf[pc.g] = lblk[...]
    l_part = over(13, lblk, glf.at[pc.g], partner)
    l_part.start()
    for part in range(3):
        sent = ring(part)
        place = mine[ORDERS[part][0]]
        sent[0].wait_recv()
        add_far(part, (place + 1) % 4, 0)
        sent[4].start()
        sent[1].wait_recv()
        add_far(part, (place + 3) % 4, 1)
        sent[5].start()
    scaled.wait(1)
    scaled.start(2)
    h_part.wait()
    la_sib.wait()
    gh_both = [turned(ghp[n]) for n in range(2)]

    def project_grad(n, carry):
        y, xl = n // 2, n % 2
        gpw[y, xl] = dot(la[0, y, xl].reshape(512, 256), gh_both[0]) + dot(
            la[1, y, xl].reshape(512, 256), gh_both[1]
        )
        return carry

    lax.fori_loop(0, 8, project_grad, 0)
    give_gpw = pltpu.make_async_copy(gpw, gpw_to, out_s.at[1])
    give_gpw.start()
    gga_push.drain()

    for part in range(3):
        held_first[part].wait()
        sent = ring(part)
        for n in range(2, 6):
            sent[n].wait_recv()
        src, dst = first[part], once[part]

        def add_first(n, carry, src=src, dst=dst):
            a, b = n // 4, n % 4
            dst[a, b] = sum(src[s, a, b].astype(F32) for s in range(3)).astype(BF16)
            return carry

        lax.fori_loop(0, 16, add_first, 0)
        for copy in copies(part, 1):
            copy.start()

    scaled.wait(2)
    s_sib2 = over(15, sq.at[core], sq.at[core], sib)
    s_sib2.start()
    l_part.wait()
    for phase in range(3):
        for copy in gl_copies(phase):
            copy.wait_send()
    gq_push.drain()
    for c in range(2):
        gow_t[:, c * 512 : c * 512 + 512] = dot(glf[0], attf[c, :256, :]) + dot(glf[1], attf[c, 256:, :])
    give_gow = pltpu.make_async_copy(gow_t, gow_to, out_s.at[2])
    give_gow.start()
    gain_part.wait()
    gain_row[...] = (gain_out[0] + gain_out[1]).T[:1, :]
    give_gain = pltpu.make_async_copy(gain_row, gain_to, out_s.at[3])
    give_gain.start()

    for part in range(3):
        for copy in copies(part, 1):
            copy.wait_recv()
        src, dst, held = second[part], twice[part], once[part]
        left = [axis for axis in range(3) if axis != ORDERS[part][0]]
        leading = left[0] == ORDERS[part][1]
        here = mine[ORDERS[part][1]]

        def add_second(n, carry, src=src, dst=dst, held=held, leading=leading, here=here):
            base = held[here, n] if leading else held[n, here]
            dst[n] = (base.astype(F32) + sum(src[s, n].astype(F32) for s in range(1, 4))).astype(BF16)
            return carry

        lax.fori_loop(0, 4, add_second, 0)
        for copy in copies(part, 2):
            copy.start()

    lt_part.wait()
    qo_sib.wait()
    s_sib2.wait()
    back = glf[pc.g].astype(F32)
    ratio = jnp.zeros((256, 128), F32)
    for c in range(2):
        for p in range(2):
            columns = pl.ds(c * 512 + p * 256, 256)
            blocks = [sq[c, n, :, :, :, p].reshape(256, 256) for n in range(2)]
            gqw[:, columns] = dot(ltp[0], blocks[0]) + dot(ltp[1], blocks[1])
            back = back + col_dot(qw[:, columns], sq[c, pc.g, :, :, :, p].reshape(256, 256))
    for p in range(2):
        for block, query in (
            (sq[core, pc.g, :, :, :, p], qg[pc.g, :, :, :, p]),
            (sq[1 - core, pc.g, :, :, :, p], qo[:, :, :, p]),
        ):
            prod = block.astype(F32).reshape(256, 256) * query.astype(F32).reshape(256, 256)
            ratio = ratio + prod[:, :128] + prod[:, 128:]
    coef = jnp.sum(ratio.T, axis=0, keepdims=True) * rinv_row / D_LAT
    gl_out[...] = back - coef * lt[...].astype(F32)
    give_gl = pltpu.make_async_copy(gl_out, gl_to, out_s.at[4])
    give_gl.start()
    give_gqw = pltpu.make_async_copy(gqw, gqw_to, out_s.at[5])
    give_gqw.start()
    for gather in (latents, output, resampled, scaled):
        gather.drain()

    for part in range(3):
        for copy in copies(part, 2):
            copy.wait_recv()
        here = mine[ORDERS[part][2]]
        fin[:, pl.ds(*WIDE[part])] = twice[part][here].astype(F32) + sum(
            third[part][s].astype(F32) for s in range(1, 4)
        )
    give = over(19, fin.at[at16(1 - core), :], oth, sib)
    give.start()

    def put(plane, rows):
        for n in range(2):
            spot = pl.multiple_of(n * 1024 + plane * 512, 512)
            gkw[:, pl.ds(spot, 512)] = rows[:13, n * 512 : n * 512 + 512]

    put(core, fin[at16(core), :])
    w_sib.wait_send()
    q_sib.wait_send()
    for part in range(3):
        for copy in ring(part):
            copy.wait_send()
        for phase in (1, 2):
            for copy in copies(part, phase):
                copy.wait_send()
    give.wait()
    put(1 - core, oth[...])
    give_gkw = pltpu.make_async_copy(gkw, gkw_to, out_s.at[6])
    give_gkw.start()
    for copy in (give_llm, give_gpw, give_gow, give_gain, give_gl, give_gqw, give_gkw):
        copy.wait()


def sems(*counts):
    return [pltpu.SemaphoreType.DMA((n,)) for n in counts]


def finish_kernel(*refs):
    got, done = refs[-2:]
    n = len(refs) // 3
    moves = []
    for i in range(n):
        src, dst, held = refs[i], refs[n + i], refs[2 * n + i]
        if len(src.shape) > 2:
            moves += [(src.at[m], held.at[m], dst.at[m]) for m in range(src.shape[0])]
        else:
            moves.append((src, held, dst))
    loads = [pltpu.make_async_copy(src, held, got.at[m]) for m, (src, held, dst) in enumerate(moves)]
    stores = [pltpu.make_async_copy(held, dst, done.at[m]) for m, (src, held, dst) in enumerate(moves)]
    for copy in loads:
        copy.start()
    for load, store in zip(loads, stores):
        load.wait()
        store.start()
    for copy in stores:
        copy.wait()


def local(
    tokens, keep_mask, shard_counts, latents, query_weight, keyval_weight, output_weight,
    project_weight, llm_gain, input_grad,
):
    widths = [w for _, w in WIDE]
    scratch = [
        ((256, 1664), BF16),
        ((13, 2048), BF16),
        ((64, 1024), BF16),
        ((64, 256), BF16),
        ((64, 1024), BF16),
        ((32, 2, 64, 128), BF16),
        ((256, 128), BF16),
        ((256, 128), BF16),
        ((64, 256), F32),
        ((64, 1024), F32),
        ((13, 2048), F32),
        ((64, 1024), F32),
        ((4, 2, 512, 128), F32),
        ((1, 128), F32),
        ((2, 128, 128), F32),
        ((256, 128), F32),
        ((2, 2, 256, 384), BF16),
        ((2, 16, 1024), BF16),
        ((128, 256), F32),
        ((4, 4, 4, 32, 1024), BF16),
        ((2, 256, 2048), BF16),
        ((2048, 512), BF16),
        ((2, 256, 128), F32),
        ((2, 256, 384), BF16),
        ((2, 256, 384), BF16),
        ((32, 16, 384), BF16),
        ((2, 4, 2, 2, 2, 16, 256), BF16),
        ((4, 2, 2, 2, 16, 256), BF16),
        ((4, 2, 4, 64, 512), BF16),
        ((4, 2, 4, 64, 256), BF16),
        ((2, 64, 256), BF16),
        ((2, 4, 2, 4, 2, 64, 256), BF16),
        ((512, 1024), BF16),
        ((512, 512), BF16),
        ((4, 512, 512), F32),
        ((4, 512, 512), BF16),
        ((2, 512, 256), BF16),
        ((64, 16, 256), BF16),
        ((8, 512), F32),
        ((4, 4, 1, 128), F32),
        ((64, 2, 1, 128), F32),
        ((16, 256), BF16),
        ((2, 512, 512), BF16),
        ((2, 128, 2048), BF16),
        ((32, 64, 128), BF16),
        ((136, 256), F32),
        ((136, 256), F32),
        ((128, 512), BF16),
        ((128, 512), BF16),
        ((128, 1024), BF16),
        ((128, 512), BF16),
        ((2, 8, 128), F32),
        ((8, 128), F32),
        ((32, 8, 128), F32),
        ((128, 256), BF16),
        ((128, 256), BF16),
        ((2, 128, 256), BF16),
        ((256, 512), BF16),
        ((32, 16, 256), BF16),
        ((4, 2, 4, 64, 256), BF16),
        ((3, 2, 4, 32, 256), BF16),
        ((3, 4, 2, 32, 256), BF16),
        ((2, 4, 32, 256), BF16),
        ((4, 2, 32, 256), BF16),
        ((2, 3, 2, 32, 256), BF16),
        ((2, 2, 32, 256), BF16),
        ((2, 32, 256), BF16),
        ((64, 256), BF16),
        ((2, 64, 256), BF16),
        ((16, 256), BF16),
        ((512, 512), BF16),
        ((4, 512, 512), BF16),
        ((512, 512), BF16),
        ((64, 16, 256), BF16),
        ((512, 1024), BF16),
        ((2, 2, 4, 2, 2, 2, 16, 256), BF16),
        *[((3, 4, 4, 32, w), BF16) for w in widths],
        *[((4, 4, 32, w), BF16) for w in widths],
        *[((4, 4, 32, w), BF16) for w in widths],
        *[((4, 32, w), BF16) for w in widths],
        *[((4, 32, w), BF16) for w in widths],
        *[((2, 2, 4, 32, w), BF16) for w in widths],
        ((32, 1024), F32),
        ((16, 1024), F32),
    ]
    results = [
        jax.ShapeDtypeStruct(shape, dtype)
        for shape, dtype in (
            ((256, 128), BF16),
            ((64, 256), F32),
            ((64, 1024), F32),
            ((13, 2048), F32),
            ((64, 1024), F32),
            ((4, 2, 512, 128), F32),
            ((1, 128), F32),
        )
    ]
    made = pl.pallas_call(
        whole_kernel,
        out_shape=results,
        in_specs=[VMEM] * 3 + [ANY] * 7,
        out_specs=[ANY] * 7,
        scratch_shapes=[pltpu.VMEM(s, d) for s, d in scratch]
        + sems(72, 72, 36, 36, 36, 36, 36, 36, 32, 32, 18, 18, 64, 64, 64, 64, 32, 32)
        + sems(32, 32, 14, 14, 64, 64, 64, 64, 64, 64, 18, 18, 36, 36, 20, 20, 20, 7),
        compiler_params=pltpu.CompilerParams(
            has_side_effects=True, vmem_limit_bytes=62 << 20, collective_id=0
        ),
        name="whole",
    )(
        keep_mask.reshape(1, 256), shard_counts.reshape(1, 1), llm_gain.reshape(1, 128), tokens,
        keyval_weight, query_weight, latents.T, output_weight.T, project_weight.reshape(32, 2, 64, 128),
        input_grad,
    )
    llm, gl, gqw, gkw, gow, gpw, gain = pl.pallas_call(
        finish_kernel,
        out_shape=results,
        in_specs=[ANY] * 7,
        out_specs=[ANY] * 7,
        scratch_shapes=[pltpu.VMEM(r.shape, r.dtype) for r in results] + sems(10, 10),
        compiler_params=pltpu.CompilerParams(vmem_limit_bytes=62 << 20),
        name="finish",
    )(*made)
    return (llm, gl.T, gqw, gkw, gow.T, gpw.reshape(4096, 128), gain.reshape(128))


def solution(mesh):
    in_specs = (
        P(("grp", "tp"), None),
        P(("grp", "tp")),
        P(("grp", "tp")),
        P("grp", "tp"),
        P("tp", None),
        P(("grp", "tp"), None),
        P(None, "tp"),
        P(None, "tp"),
        P("tp"),
        P("grp", "tp"),
    )
    out_specs = (
        P("grp", "tp"),
        P("grp", "tp"),
        P("tp", None),
        P(("grp", "tp"), None),
        P(None, "tp"),
        P(None, "tp"),
        P("tp"),
    )
    return jax.shard_map(local, mesh=mesh, in_specs=in_specs, out_specs=out_specs, check_vma=False)
```

```python
import functools
import math

import jax
import jax.numpy as jnp
import numpy as np
from jax import lax
from jax.experimental import pallas as pl
from jax.experimental.pallas import tpu as pltpu
from jax.sharding import PartitionSpec as P

D_LAT = 4096
HEAD_DIM = 128
D_LLM = 8192
SCORE_CAP = 5.0
SCALE = 1.0 / math.sqrt(HEAD_DIM)
CHIPS = 64
GROUP = 32

F32 = jnp.float32
BF16 = jnp.bfloat16
MESH = pl.DeviceIdType.MESH
ANY = pl.BlockSpec(memory_space=pl.ANY)
VMEM = pl.BlockSpec(memory_space=pltpu.VMEM)

ORDERS = ((2, 1, 0), (1, 0, 2), (0, 2, 1))
WIDE = ((0, 384), (384, 384), (768, 256))
SPLIT = ((0, 256), (256, 128), (384, 128), (512, 128), (640, 128), (768, 256))
SPLIT_ORDERS = ORDERS + ORDERS
KEYS, VALUES = (0, 1, 2), (3, 4, 5)
COLUMNS_512 = ((0, 128), (128, 256), (384, 128))
ROWS_64 = ((0, 16), (16, 32), (48, 16))
ROWS_OWN = ((0, 16), (16, 16), (32, 32))
PAIR_ORDERS = ((2, 1, 0), (1, 0, 2))


def row_dot(left, right):
    return lax.dot_general(left, right, (((0,), (0,)), ((), ())), preferred_element_type=F32)


def col_dot(left, right):
    return lax.dot_general(left, right, (((1,), (1,)), ((), ())), preferred_element_type=F32)


def dot(left, right):
    return jnp.dot(left, right, preferred_element_type=F32)


class Place:
    def __init__(self):
        self.g = lax.axis_index("grp")
        self.t = lax.axis_index("tp")
        self.core = self.t % 2
        self.j = self.t // 2
        self.z = self.j % 4
        self.xl = (self.j // 4) % 2
        self.y = self.j // 8
        self.x = self.g * 2 + self.xl

    def chip(self, x, y, z):
        return x // 2, (y * 2 + x % 2) * 4 + z

    def plane_peer(self, k):
        return self.chip((self.x + k // 16) % 4, (self.y + (k // 4) % 4) % 4, (self.z + k % 4) % 4)

    def group_peer(self, k):
        y = (self.y + k // 8) % 4
        xl = (self.xl + (k // 4) % 2) % 2
        z = (self.z + k % 4) % 4
        return (y * 2 + xl) * 4 + z

    def sibling(self):
        return self.g, self.j * 2 + 1 - self.core


def remote(src, dst, sends, recvs, device):
    return pltpu.make_async_remote_copy(
        src_ref=src, dst_ref=dst, send_sem=sends, recv_sem=recvs, device_id=device, device_id_type=MESH
    )


class Later:
    def __init__(self, make):
        self.make = make

    def start(self):
        self.make().start()

    def wait_recv(self):
        self.make().wait_recv()

    def wait_send(self):
        self.make().wait_send()


def each_peer(n, do):
    def body(k, carry):
        do(k)
        return carry

    lax.fori_loop(1, n, body, 0, unroll=9 if n == 64 else 31)


class Gather:
    def __init__(self, place, ref, view, sends, recvs, whole=True, orders=ORDERS, ring=True):
        self.place, self.ref, self.view, self.sends, self.recvs = place, ref, view, sends, recvs
        self.whole, self.orders, self.ring = whole, orders, ring

    def copies(self, phase, parts=None):
        pc = self.place
        mine = [pc.x, pc.y, pc.z]
        for part in self.parts(parts):
            order = self.orders[part]
            held = list(mine)
            for axis in order[:phase]:
                held[axis] = None
            block = self.view(self.ref, *held, part)
            near = order[phase] == 0 and not self.whole
            for step in (1,) if near else (1, 3, 2):
                peer = list(mine)
                if near:
                    peer[0] = pc.g * 2 + 1 - pc.xl
                else:
                    peer[order[phase]] = (peer[order[phase]] + step) % 4
                yield self.push(block, (part * (2 if self.ring else 3) + phase) * 3 + step - 1, peer)

    def push(self, block, spot, peer):
        g, j = self.place.chip(*peer)
        device = (g, j * 2 + self.place.core)
        return Later(lambda: remote(block, block, self.sends.at[spot], self.recvs.at[spot], device))

    def last(self, part):
        pc = self.place
        order = self.orders[part]
        axis = order[2]
        mine = [pc.x, pc.y, pc.z]
        base = (len(self.orders) + part) * 6
        if axis == 0 and not self.whole:
            held = [mine[0], None, None]
            block = self.view(self.ref, *held, part)
            return [self.push(block, base, [pc.g * 2 + 1 - pc.xl, pc.y, pc.z])]

        def at(place, half):
            held = [None, None, None]
            held[axis] = place
            held[order[0]] = Half(half)
            return self.view(self.ref, *held, part)

        here, up, down = mine[axis], (mine[axis] + 1) % 4, (mine[axis] + 3) % 4
        above, below = list(mine), list(mine)
        above[axis], below[axis] = up, down
        return [
            self.push(at(here, 0), base, above),
            self.push(at(here, 1), base + 1, above),
            self.push(at(here, 1), base + 2, below),
            self.push(at(here, 0), base + 3, below),
            self.push(at(down, 0), base + 4, above),
            self.push(at(up, 1), base + 5, below),
        ]

    def parts(self, some):
        return range(len(self.orders)) if some is None else some

    def start(self, phase, parts=None):
        if phase < 2 or not self.ring:
            for copy in self.copies(phase, parts):
                copy.start()
            return
        for part in self.parts(parts):
            copies = self.last(part)
            for n in (0,) if len(copies) == 1 else (0, 2, 1, 3):
                copies[n].start()

    def relay(self, parts=None):
        for part in self.parts(parts):
            copies = self.last(part)
            if len(copies) > 1:
                copies[0].wait_recv()
                copies[4].start()
                copies[2].wait_recv()
                copies[5].start()

    def wait(self, phase, parts=None):
        if phase < 2 or not self.ring:
            for copy in self.copies(phase, parts):
                copy.wait_recv()
            return
        for part in self.parts(parts):
            copies = self.last(part)
            for n in (0,) if len(copies) == 1 else (1, 3, 4, 5):
                copies[n].wait_recv()

    def drain(self):
        for phase in range(2 if self.ring else 3):
            for copy in self.copies(phase):
                copy.wait_send()
        for part in self.parts(None) if self.ring else ():
            for copy in self.last(part):
                copy.wait_send()


class Half:
    def __init__(self, n):
        self.n = n


def pick(value):
    if isinstance(value, Half):
        return slice(value.n * 2, value.n * 2 + 2)
    return slice(None) if value is None else value


def halves(x):
    if isinstance(x, Half):
        return x.n, slice(None)
    return (slice(None), slice(None)) if x is None else (x // 2, x % 2)


def in_group(x):
    if isinstance(x, Half):
        return slice(x.n, x.n + 1)
    return slice(None) if x is None else x % 2


def view_weight(ref, x, y, z, part):
    return ref.at[pick(x), pick(y), pick(z), :, pl.ds(*SPLIT[part])]


def view_output(ref, x, y, z, part):
    return ref.at[pick(y), in_group(x), pick(z), :, pl.ds(*COLUMNS_512[part])]


def view_own(ref, x, y, z, part):
    return ref.at[pick(y), in_group(x), pick(z), pl.ds(*ROWS_OWN[part]), :]


def view_rows(ref, x, y, z, part):
    hi, lo = halves(x)
    up, pair = halves(z)
    return ref.at[hi, pick(y), lo, up, pair, :, pl.ds(part * 128, 128)]


def view_latents(core, ref, x, y, z, part):
    hi, lo = halves(x)
    return ref.at[hi, pick(y), lo, pick(z), core, pl.ds(*ROWS_64[part]), :]


def total_slots(own, slots, n):
    def body(k, total):
        return total + slots[k].astype(F32)

    return lax.fori_loop(1, n, body, own.astype(F32), unroll=9 if n == 64 else 31)


class Pushes:
    def __init__(self, n, make):
        self.n, self.make = n, make

    def start(self):
        each_peer(self.n, lambda k: self.make(k).start())

    def landed(self):
        each_peer(self.n, lambda k: self.make(k).wait_recv())

    def drain(self):
        each_peer(self.n, lambda k: self.make(k).wait_send())


class PairPushes(Pushes):
    def __init__(self, place, make):
        super().__init__(CHIPS, make)
        self.place = place

    def start_pair(self, p):
        def body(i, carry):
            k = (i // 2) * 4 + (i % 2) * 2 + (self.place.z + p) % 2

            @pl.when(k > 0)
            def _():
                self.make(k).start()

            return carry

        lax.fori_loop(0, 32, body, 0, unroll=4)


def at16(n):
    return pl.ds(pl.multiple_of(n * 16, 16), 16)


def at256(n):
    return pl.ds(pl.multiple_of(n * 256, 256), 256)


def heads_of(ref, pair, side):
    return ref[:, :, :, :, pair, :, side * 128 : side * 128 + 128].reshape(512, 128)


def turned(value, dtype=BF16):
    return value.astype(F32).T.astype(dtype)


def whole_kernel(
    keep, count, gain_in, keyval_w, tokens_in, qw_in, lt_in, owt_in, pw_in, igrad_in,
    llm_to, gl_to, gqw_to, gkw_to, gow_to, gpw_to, gain_to,
    tokens, qw, lt, owt, pw, igrad, llm, gl_out, gqw, gkw, gow_t, gpw, gain_row, gain_out,
    val, qpart, wpl, gain,
    wg, tokb, tok_t, valb, qx, qsum, recvq, qg, qo, owe, lown, ltp, la, kv, kv_t, fac, half, npk, recvn, tot_all, tots, rtot,
    ablk, attf, pw_t, pwx, lat_s, lat_x, fold_s, fold_x, fold, foldx, sumx, sumo, sumr, gh_t, ghx, ghp, gap, recvg, glp, u1a, u1b, v1a, v1b, u2, v2, u3,
    lblk, glf, gblk, gg, ds, gqp, recvgq, gkv, sq, r1a, r1b, r1c, s1a, s1b, s1c,
    r2a, r2b, r2c, s2a, s2b, s2c, r3a, r3b, r3c, fara, farb, farc, fin, oth,
    w_s, w_r, ow_s, ow_r, lo_s, lo_r, l_s, l_r, q_s, q_r, qa_s, qa_r, n_s, n_r, a_s, a_r, t_s, t_r,
    g_s, g_r, gl_s, gl_r, tot_s, tot_r, gga_s, gga_r, gq_s, gq_r, sqa_s, sqa_r, p_s, p_r, x_s, x_r, loc, out_s,
):
    pc = Place()
    core = pc.core
    sib = pc.sibling()
    partner = (1 - pc.g, pc.t)
    mine = [pc.x, pc.y, pc.z]
    pair = pc.j % 2
    own_rows = at16(pc.j // 2)
    all_rows = at16(pc.g * 16 + pc.j // 2)

    def chip_device(g, j):
        return (g, j * 2 + core)

    def over(index, src, dst, device):
        return remote(src, dst, x_s.at[index], x_r.at[index], device)

    barrier = pltpu.get_barrier_semaphore()

    def greet(k):
        pl.semaphore_signal(barrier, inc=1, device_id=chip_device(*pc.plane_peer(k)), device_id_type=MESH)

    pl.semaphore_signal(barrier, inc=1, device_id=sib, device_id_type=MESH)
    each_peer(CHIPS, greet)

    loads = [
        pltpu.make_async_copy(src, dst, loc.at[12 + n])
        for n, (src, dst) in enumerate(
            (
                (lt_in, lt), (qw_in, qw), (owt_in, owt),
                (tokens_in, tokens), (pw_in, pw), (igrad_in, igrad),
            )
        )
    ]
    for copy in loads:
        copy.start()

    rows_f32 = jnp.concatenate([keyval_w[...].astype(F32), jnp.zeros((3, 2048), F32)], axis=0).astype(BF16)
    for c in range(2):
        wpl[c, :, :512] = rows_f32[:, c * 512 : c * 512 + 512]
        wpl[c, :, 512:] = rows_f32[:, 1024 + c * 512 : 1536 + c * 512]
    w_own = pltpu.make_async_copy(wpl.at[core], wg.at[pc.x, pc.y, pc.z, at16(core)], loc.at[3])
    w_own.start()
    for copy in loads:
        copy.wait()
    feats_f32 = lt[...].astype(F32)
    lat = feats_f32.T.astype(BF16)
    squares = jnp.sum(feats_f32 * feats_f32, axis=0, keepdims=True)
    squares = jnp.broadcast_to(squares, (128, 256)).T.astype(BF16)
    for c in range(2):
        for p in range(2):
            columns = (c * 2 + p) * 256
            qpart[c, p, :, :256] = dot(lat, qw[:, columns : columns + 256]).astype(BF16)
            qpart[c, p, :, 256:] = squares
    spot = lax.broadcasted_iota(jnp.int32, (1, 256), 1)
    kept = ((keep[...] == 1) | (spot == 0)) & (spot < count[...])
    val[...] = jnp.broadcast_to(jnp.where(kept, 1.0, 0.0), (128, 256)).T
    gain[...] = jnp.broadcast_to(gain_in[...].astype(F32), (256, 128)).T

    pl.semaphore_wait(barrier, CHIPS)

    w_sib = over(0, wpl.at[1 - core], wg.at[pc.x, pc.y, pc.z, at16(core)], sib)
    w_sib.start()

    q_sib = over(1, qpart.at[1 - core], qx, sib)
    q_sib.start()
    weight = Gather(pc, wg, view_weight, w_s, w_r, True, SPLIT_ORDERS)
    output = Gather(pc, owe, view_output, ow_s, ow_r, False)
    latents = Gather(pc, lown, view_own, lo_s, lo_r, False)
    resampled = Gather(pc, la, functools.partial(view_latents, core), l_s, l_r)
    w_own.wait()
    w_sib.wait_recv()
    weight.start(0)
    group_half = pl.ds(pl.multiple_of(pc.g * 512, 512), 512)
    local_copies = [
        pltpu.make_async_copy(owt.at[:, group_half], owe.at[pc.y, pc.xl, pc.z], loc.at[0]),
        pltpu.make_async_copy(lt, lown.at[pc.y, pc.xl, pc.z], loc.at[1]),
        pltpu.make_async_copy(lt, ltp.at[pc.g], loc.at[11]),
        pltpu.make_async_copy(val, valb.at[core], loc.at[2]),
    ]
    for copy in local_copies:
        copy.start()

    q_sib.wait_recv()
    for p in range(2):
        qsum[p] = (qpart[core, p].astype(F32) + qx[p].astype(F32)).astype(BF16)

    def q_copy(k):
        j = pc.group_peer(k)
        return remote(
            qsum.at[j % 2, at16(j // 2), :], recvq.at[k], q_s.at[k], q_r.at[k], chip_device(pc.g, j)
        )

    q_push = Pushes(GROUP, q_copy)
    q_push.start()

    for block in range(16):
        x, y = block // 4, block % 4
        begin = (((x // 2) * 4 + y) * 2 + x % 2) * 104
        base = begin // 128 * 128
        width = min(256, 1664 - base)
        row = lax.broadcasted_iota(jnp.int32, (width, 128), 0)
        col = lax.broadcasted_iota(jnp.int32, (width, 128), 1)
        rest = col & 15
        hit = (row == (begin - base) + (col >> 4) * 13 + rest) & (rest < 13)
        place = jnp.where(hit, 1.0, 0.0).astype(BF16)
        tokb[core, :, pl.ds(block * 128, 128)] = dot(tokens[:, pl.ds(base, width)], place).astype(BF16)

    t_sib = over(2, tokb.at[core], tokb.at[core], sib)
    t_sib.start()
    for copy in local_copies:
        copy.wait()
    latents.start(0)
    output.start(0)
    v_sib = over(3, val, valb.at[core], sib)
    v_sib.start()
    pw_sib = over(4, pw.at[:, 1 - core], pwx, sib)
    pw_sib.start()
    weight.wait(0)
    weight.start(1)
    for y in range(4):
        pw_t[0, :, pl.ds(y * 512, 512)] = turned(pw[pl.ds(y * 8, 8), core].reshape(512, 128))
    latents.wait(0)
    latents.start(1)
    output.wait(0)
    output.start(1)
    q_push.landed()
    total = total_slots(qsum[pair, own_rows, :], recvq, GROUP)
    rinv = lax.rsqrt(total[:, 256:] / D_LAT + 1e-06)
    proj = total[:, :256]
    q_spot = (pc.g, pc.y, pc.xl, pc.z // 2, pair)
    qg[q_spot] = (proj * rinv[:, :1]).astype(BF16)
    queries = Gather(pc, qg, view_rows, qa_s, qa_r, True, PAIR_ORDERS, False)
    queries.start(0)
    weight.wait(1)
    weight.start(2, KEYS)
    queries.wait(0)
    queries.start(1)
    weight.start(2, VALUES)
    queries.wait(1)
    queries.start(2)
    t_sib.wait()
    v_sib.wait()
    for block in range(2):
        tok_t[pl.ds(block * 512, 512), :] = turned(
            tokb[:, :, pl.ds(block * 512, 512)].reshape(512, 512)
        )
    weight.relay(KEYS)
    for block in range(2, 4):
        tok_t[pl.ds(block * 512, 512), :] = turned(
            tokb[:, :, pl.ds(block * 512, 512)].reshape(512, 512)
        )
    pw_sib.wait()
    for y in range(4):
        pw_t[1, :, pl.ds(y * 512, 512)] = turned(pwx[pl.ds(y * 8, 8)].reshape(512, 128))
    lt_part = over(16, lt, ltp.at[pc.g], partner)
    lt_part.start()
    q_push.drain()
    weight.relay(VALUES)
    weight.wait(2, KEYS)
    latents.wait(1)
    latents.start(2)
    output.wait(1)
    output.start(2)

    tok = tokb[...].reshape(512, 2048)

    def project(n, carry):
        columns = at256(n)
        kv[:, columns] = dot(tok, wg[:, :, :, :, columns].reshape(2048, 256)).astype(BF16)
        return carry

    lax.fori_loop(0, 2, project, 0)
    queries.wait(2)
    qo_sib = over(17, qg.at[pc.g], qo, sib)
    qo_sib.start()
    totals = []
    for head in range(4):
        query = heads_of(qg, head // 2, head % 2)
        total = jnp.zeros((1, 512), F32)
        for chunk in range(4):
            slots = pl.ds(chunk * 128, 128)
            raw = col_dot(kv[slots, head * 128 : head * 128 + 128], query)
            squash = jnp.tanh(raw * (SCALE / SCORE_CAP))
            kept = valb[chunk // 2, pl.ds(chunk % 2 * 128, 128), :][:, :1]
            weights = jnp.exp(SCORE_CAP * squash) * kept
            half[head, slots, :] = weights.astype(BF16)
            fac[head, slots, :] = weights * (1.0 - squash * squash) * SCALE
            total = total + jnp.sum(weights, axis=0, keepdims=True)
        totals.append(total)
    weight.wait(2, VALUES)
    lax.fori_loop(2, 4, project, 0)

    def n_copy(k):
        g, j = pc.plane_peer(k)
        return remote(
            npk.at[j % 2, at16(g * 16 + j // 2), :], recvn.at[k], n_s.at[k], n_r.at[k], chip_device(g, j)
        )

    def tot_copy(k):
        g, j = pc.plane_peer(k)
        return remote(
            tots.at[g * 2 + j // 16, pl.ds(j % 2 * 2, 2)], rtot.at[k], tot_s.at[k], tot_r.at[k], chip_device(g, j)
        )

    n_push = PairPushes(pc, n_copy)
    tot_push = Pushes(CHIPS, tot_copy)
    tot_all[...] = jnp.concatenate(totals + [jnp.zeros((4, 512), F32)], axis=0)
    for head in range(4):
        for n in range(4):
            tots[n, head] = tot_all[head : head + 1, n * 128 : n * 128 + 128]
    for p in range(2):
        heads = (p * 2, p * 2 + 1)
        packed = [
            dot(turned(kv[:, 512 + head * 128 : 640 + head * 128]), half[head]) for head in heads
        ]
        npk[p] = jnp.concatenate(packed, axis=0).T.astype(BF16)
        n_push.start_pair(p)
    tot_push.start()

    latents.relay()
    output.relay()
    for n in range(2):
        kv_t[pl.ds(n * 256, 256), :] = turned(kv[:, n * 256 : n * 256 + 256])
    weight.drain()
    queries.drain()
    n_push.landed()
    total = total_slots(npk[pair, all_rows, :], recvn, CHIPS)
    tot_push.landed()

    def add_rows(k, held):
        return (held[0] + rtot[k, 0], held[1] + rtot[k, 1])

    here = pc.g * 2 + pc.j // 16
    row_sums = lax.fori_loop(1, CHIPS, add_rows, (tots[here, pair * 2], tots[here, pair * 2 + 1]))
    row = lax.broadcasted_iota(jnp.int32, (16, 128), 0)
    hit = lax.broadcasted_iota(jnp.int32, (16, 128), 1) == row + (pc.j // 2) % 8 * 16
    whole = jnp.concatenate(
        [
            jnp.broadcast_to(
                jnp.sum(jnp.where(hit, row_sums[n], 0.0), axis=1, keepdims=True), (16, 128)
            )
            for n in range(2)
        ],
        axis=1,
    )
    ablk[...] = (total / whole).astype(BF16)
    a_spot = attf.at[core, all_rows, at256(pair)]
    a_push = Pushes(
        CHIPS,
        lambda k: remote(ablk, a_spot, a_s.at[k], a_r.at[k], chip_device(*pc.plane_peer(k))),
    )
    a_push.start()
    a_own = pltpu.make_async_copy(ablk, a_spot, loc.at[5])
    a_own.start()

    n_push.drain()
    tot_push.drain()
    latents.wait(2)
    feats = lown[...].reshape(2048, 256)
    lat_s[:128, :] = dot(pw_t[1], feats)
    squares = jnp.zeros((1, 256), F32)
    for y in range(4):
        block = lown[y].reshape(512, 256).astype(F32)
        squares = squares + jnp.sum(block * block, axis=0, keepdims=True)
    lat_s[128:, :] = jnp.broadcast_to(squares, (8, 256))
    lat_sib = over(5, lat_s, lat_x, sib)
    lat_sib.start()
    hidden = dot(pw_t[0], feats)
    output.wait(2)

    rows = owe[...].reshape(2048, 512)
    fold_s[...] = dot(pw_t[1], rows).astype(BF16)
    fold_sib = over(6, fold_s, fold_x, sib)
    fold_sib.start()
    folded = dot(pw_t[0], rows)
    fold_sib.wait()
    fold[:, group_half] = (folded + fold_x[...].astype(F32)).astype(BF16)
    f_part = over(18, fold.at[:, group_half], fold.at[:, group_half], partner)
    f_part.start()
    lat_sib.wait()
    hidden = hidden + lat_x[:128, :]
    rinv_row = lax.rsqrt((squares + lat_x[128:129, :]) / D_LAT + 1e-06)
    a_own.wait()
    a_push.landed()
    a_sib = over(7, attf.at[core], attf.at[core], sib)
    a_sib.start()
    f_part.wait()
    f_sib = over(8, fold.at[:, pl.ds(pl.multiple_of((1 - core) * 512, 512), 512)], foldx, sib)
    f_sib.start()
    a_sib.wait()
    group_rows = at256(pc.g)
    hidden = hidden + col_dot(fold[:, :512], attf[0, group_rows, :])
    hidden = (hidden + col_dot(fold[:, 512:], attf[1, group_rows, :])).astype(BF16).astype(F32)
    grad_y = igrad[...].astype(F32).T
    scaled_dy = grad_y * gain[...]
    square_row = jnp.sum(hidden * hidden, axis=0, keepdims=True)
    inner_row = jnp.sum(hidden * scaled_dy, axis=0, keepdims=True)
    sumo[...] = jnp.concatenate(
        [
            square_row[:, :128], square_row[:, 128:], inner_row[:, :128], inner_row[:, 128:],
            jnp.zeros((4, 128), F32),
        ],
        axis=0,
    )
    s_sib = over(9, sumo, sumx.at[0], sib)
    s_sib.start()
    s_sib.wait()
    sumx[1] = sumx[0] + sumo[...]
    t_push = Pushes(
        GROUP,
        lambda k: remote(sumx.at[1], sumr.at[k], t_s.at[k], t_r.at[k], chip_device(pc.g, pc.group_peer(k))),
    )
    t_push.start()
    lat_out = lt[...].astype(F32) + col_dot(owt[:, :512], attf[0, group_rows, :])
    la[pc.g, pc.y, pc.xl, pc.z, core] = (lat_out + col_dot(owt[:, 512:], attf[1, group_rows, :])).astype(BF16)
    resampled.start(0)
    resampled.wait(0)
    resampled.start(1)
    t_push.landed()
    total = total_slots(sumx[1], sumr, GROUP)
    square_row = jnp.concatenate([total[0:1], total[1:2]], axis=1)
    inner_row = jnp.concatenate([total[2:3], total[3:4]], axis=1)
    hrinv = lax.rsqrt(square_row / D_LLM + 1e-05)
    normed = hidden * hrinv
    llm[...] = turned(normed * gain[...])
    give_llm = pltpu.make_async_copy(llm, llm_to, out_s.at[0])
    give_llm.start()
    gain_own = jnp.broadcast_to(jnp.sum(grad_y * normed, axis=1, keepdims=True), (128, 128))
    grad_h = hrinv * scaled_dy - (hrinv * hrinv * hrinv / D_LLM * inner_row) * hidden
    gh_t[...] = grad_h.astype(BF16)
    h_sib = over(10, gh_t, ghx, sib)
    h_sib.start()
    ghp[pc.g] = gh_t[...]
    h_part = over(11, gh_t, ghp.at[pc.g], partner)
    h_part.start()
    gain_out[pc.g] = gain_own
    gain_part = over(12, gain_out.at[pc.g], gain_out.at[pc.g], partner)
    gain_part.start()

    f_sib.wait()
    own_half = fold[:, pl.ds(pl.multiple_of(core * 512, 512), 512)]
    partial = dot(turned(gh_t[...]), own_half)
    h_sib.wait()
    gap[...] = (partial + dot(turned(ghx[...]), foldx[...])).astype(BF16)

    def g_copy(k):
        j = pc.group_peer(k)
        return remote(
            gap.at[at16(j // 2), at256(j % 2)], recvg.at[k], g_s.at[k], g_r.at[k], chip_device(pc.g, j)
        )

    g_push = Pushes(GROUP, g_copy)
    g_push.start()

    resampled.wait(1)
    resampled.start(2)

    for n in range(4):
        part = dot(pw[pl.ds(n * 8, 8), core].reshape(512, 128), gh_t[...])
        part = part + dot(pwx[pl.ds(n * 8, 8)].reshape(512, 128), ghx[...])
        glp[n] = part.astype(BF16).reshape(2, 4, 64, 256)

    def gl_copies(phase):
        for part in range(2):
            axis = ((1, 2), (2, 1))[part][phase] if phase < 2 else 0
            for step in (1, 3, 2) if phase < 2 else (1,):
                peer = list(mine)
                if phase < 2:
                    peer[axis] = (peer[axis] + step) % 4
                else:
                    peer[0] = pc.g * 2 + 1 - pc.xl
                spot = part * 7 + phase * 3 + step - 1
                if phase == 0:
                    rows = pl.ds(part * 32, 32)
                    src = glp.at[peer[1], :, :, rows] if axis == 1 else glp.at[:, :, peer[2], rows]
                    dst = (u1a, u1b)[part].at[step - 1]
                elif phase == 1:
                    src = v1a.at[:, peer[2]] if axis == 2 else v1b.at[peer[1]]
                    dst = u2.at[part, step - 1]
                else:
                    src, dst = v2.at[part, 1 - pc.xl], u3.at[part]
                yield remote(src, dst, gl_s.at[spot], gl_r.at[spot], chip_device(*pc.chip(*peer)))

    def gl_start(phase):
        for copy in gl_copies(phase):
            copy.start()

    def gl_add(phase):
        for copy in gl_copies(phase):
            copy.wait_recv()
        if phase == 0:
            for n in range(4):
                for xl in range(2):
                    own = glp[pc.y, xl, n, :32, :].astype(F32)
                    v1a[xl, n] = (own + sum(u1a[i, xl, n].astype(F32) for i in range(3))).astype(BF16)
                    own = glp[n, xl, pc.z, 32:, :].astype(F32)
                    v1b[n, xl] = (own + sum(u1b[i, n, xl].astype(F32) for i in range(3))).astype(BF16)
        elif phase == 1:
            for xl in range(2):
                for part, own in ((0, v1a[xl, pc.z]), (1, v1b[pc.y, xl])):
                    added = own.astype(F32) + sum(u2[part, i, xl].astype(F32) for i in range(3))
                    v2[part, xl] = added.astype(BF16)
        else:
            for part in range(2):
                added = v2[part, pc.xl].astype(F32) + u3[part].astype(F32)
                lblk[part * 32 : part * 32 + 32, :] = added.astype(BF16)

    g_push.landed()
    grad = total_slots(gap[own_rows, at256(pair)], recvg, GROUP).astype(BF16).astype(F32)
    gblk[...] = (grad / whole).astype(BF16)
    g_spot = gg.at[all_rows, at256(pair)]
    gga_push = Pushes(
        CHIPS,
        lambda k: remote(gblk, g_spot, gga_s.at[k], gga_r.at[k], chip_device(*pc.plane_peer(k))),
    )
    gga_push.start()
    gl_start(0)
    g_own = pltpu.make_async_copy(gblk, g_spot, loc.at[6])
    g_own.start()
    resampled.relay()
    for push in (a_push, t_push, g_push):
        push.drain()
    g_own.wait()
    gga_push.landed()

    def gq_copy(k):
        g, j = pc.plane_peer(k)
        return remote(
            gqp.at[at16(g * 16 + j // 2), at256(j % 2)], recvgq.at[k], gq_s.at[k], gq_r.at[k], chip_device(g, j)
        )

    gq_push = PairPushes(pc, gq_copy)
    ones = jnp.ones((8, 128), BF16)
    for p in range(2):
        parts = []
        for head in (p * 2, p * 2 + 1):
            columns = pl.ds(head * 128, 128)
            grads = gg[:, columns]
            prod = grads.astype(F32) * attf[core, :, columns].astype(F32)
            high = prod.astype(BF16)
            rest = (prod - high.astype(F32)).astype(BF16)
            delta = (col_dot(ones, high) + col_dot(ones, rest))[:1, :].astype(BF16).astype(F32)
            for chunk in range(4):
                slots = pl.ds(chunk * 128, 128)
                prob = col_dot(kv[slots, 512 + head * 128 : 640 + head * 128], grads)
                ds[head, slots, :] = (fac[head, slots, :] * (prob - delta)).astype(BF16)
            parts.append(dot(kv_t[pl.ds(head * 128, 128), :], ds[head]))
        gqp[:, p * 256 : p * 256 + 256] = jnp.concatenate(parts, axis=0).T.astype(BF16)
        gq_push.start_pair(p)
    gl_add(0)
    gl_start(1)
    for head in range(4):
        columns = pl.ds(head * 128, 128)
        gkv[:, columns] = dot(ds[head], heads_of(qg, head // 2, head % 2)).astype(BF16)
        gkv[:, 512 + head * 128 : 640 + head * 128] = dot(half[head], gg[:, columns]).astype(BF16)

    first, once = (r1a, r1b, r1c), (s1a, s1b, s1c)
    second, twice = (r2a, r2b, r2c), (s2a, s2b, s2c)
    third = (r3a, r3b, r3c)

    for x in range(4):
        for n in range(2):
            wg[x, :, :, :, n * 512 : n * 512 + 512] = (
                dot(tok_t[x * 512 : x * 512 + 512, :], gkv[:, n * 512 : n * 512 + 512])
                .astype(BF16)
                .reshape(4, 4, 32, 512)
            )

    far = (fara, farb, farc)

    def slab(part, spot, half=None):
        axis = ORDERS[part][0]
        index = [pick(None if half is None else Half(half))] + [slice(None)]
        index.insert(axis, spot)
        return wg.at[(*index, slice(None), pl.ds(*WIDE[part]))]

    def ring(part):
        axis = ORDERS[part][0]
        up, down = (mine[axis] + 1) % 4, (mine[axis] + 3) % 4
        beyond = (mine[axis] + 2) % 4
        above, below = list(mine), list(mine)
        above[axis], below[axis] = up, down
        moves = (
            (slab(part, beyond, 0), far[part].at[0], above),
            (slab(part, beyond, 1), far[part].at[1], below),
            (slab(part, up, 1), first[part].at[1, 2:4], above),
            (slab(part, down, 0), first[part].at[2, 0:2], below),
            (slab(part, up, 0), first[part].at[1, 0:2], above),
            (slab(part, down, 1), first[part].at[2, 2:4], below),
        )

        def move(n):
            src, dst, peer = moves[n]
            spot = part * 6 + n
            return remote(src, dst, p_s.at[spot], p_r.at[spot], chip_device(*pc.chip(*peer)))

        return [Later(functools.partial(move, n)) for n in range(6)]

    def add_far(part, spot, half):
        axis = ORDERS[part][0]
        columns = pl.ds(*WIDE[part])

        def body(n, carry):
            index = [half * 2 + n // 4, n % 4]
            index.insert(axis, spot)
            held = wg[(*index, slice(None), columns)].astype(F32)
            wg[(*index, slice(None), columns)] = (held + far[part][half, n // 4, n % 4].astype(F32)).astype(BF16)
            return carry

        lax.fori_loop(0, 8, body, 0)

    def copies(part, phase):
        axis = ORDERS[part][phase]
        for step in (1, 3, 2):
            peer = list(mine)
            peer[axis] = (peer[axis] + step) % 4
            spot = 18 + (part * 2 + phase - 1) * 3 + step - 1
            order = ORDERS[part]
            index = [
                peer[axis] if n == axis else slice(None) for n in range(3) if n not in order[:phase]
            ]
            yield remote(
                (once, twice)[phase - 1][part].at[tuple(index)],
                (second, third)[phase - 1][part].at[step],
                p_s.at[spot], p_r.at[spot], chip_device(*pc.chip(*peer)),
            )

    for part in range(3):
        sent = ring(part)
        for n in range(2):
            sent[n].start()
    gl_add(1)
    gl_start(2)
    gq_push.landed()
    grad = total_slots(gqp[all_rows, at256(pair)], recvgq, CHIPS)
    sq[core, q_spot[0], q_spot[1], q_spot[2], q_spot[3], pair] = (grad * rinv[:, :1]).astype(BF16)
    scaled = Gather(pc, sq.at[core], view_rows, sqa_s, sqa_r, True, PAIR_ORDERS, False)
    scaled.start(0)
    held_first = []
    for part in range(3):
        sent = ring(part)
        for n in range(2, 4):
            sent[n].start()
        copy = pltpu.make_async_copy(slab(part, mine[ORDERS[part][0]]), first[part].at[0], loc.at[7 + part])
        copy.start()
        held_first.append(copy)
    resampled.wait(2)
    la_sib = over(14, la.at[:, :, :, :, core], la.at[:, :, :, :, core], sib)
    la_sib.start()
    scaled.wait(0)
    scaled.start(1)
    gl_add(2)
    glf[pc.g] = lblk[...]
    l_part = over(13, lblk, glf.at[pc.g], partner)
    l_part.start()
    for part in range(3):
        sent = ring(part)
        place = mine[ORDERS[part][0]]
        sent[0].wait_recv()
        add_far(part, (place + 1) % 4, 0)
        sent[4].start()
        sent[1].wait_recv()
        add_far(part, (place + 3) % 4, 1)
        sent[5].start()
    scaled.wait(1)
    scaled.start(2)
    h_part.wait()
    la_sib.wait()
    gh_both = [turned(ghp[n]) for n in range(2)]

    def project_grad(n, carry):
        y, xl = n // 2, n % 2
        gpw[y, xl] = dot(la[0, y, xl].reshape(512, 256), gh_both[0]) + dot(
            la[1, y, xl].reshape(512, 256), gh_both[1]
        )
        return carry

    lax.fori_loop(0, 8, project_grad, 0)
    give_gpw = pltpu.make_async_copy(gpw, gpw_to, out_s.at[1])
    give_gpw.start()
    gga_push.drain()

    for part in range(3):
        held_first[part].wait()
        sent = ring(part)
        for n in range(2, 6):
            sent[n].wait_recv()
        src, dst = first[part], once[part]

        def add_first(n, carry, src=src, dst=dst):
            a, b = n // 4, n % 4
            dst[a, b] = sum(src[s, a, b].astype(F32) for s in range(3)).astype(BF16)
            return carry

        lax.fori_loop(0, 16, add_first, 0)
        for copy in copies(part, 1):
            copy.start()

    scaled.wait(2)
    s_sib2 = over(15, sq.at[core], sq.at[core], sib)
    s_sib2.start()
    l_part.wait()
    for phase in range(3):
        for copy in gl_copies(phase):
            copy.wait_send()
    gq_push.drain()
    for c in range(2):
        gow_t[:, c * 512 : c * 512 + 512] = dot(glf[0], attf[c, :256, :]) + dot(glf[1], attf[c, 256:, :])
    give_gow = pltpu.make_async_copy(gow_t, gow_to, out_s.at[2])
    give_gow.start()
    gain_part.wait()
    gain_row[...] = (gain_out[0] + gain_out[1]).T[:1, :]
    give_gain = pltpu.make_async_copy(gain_row, gain_to, out_s.at[3])
    give_gain.start()

    for part in range(3):
        for copy in copies(part, 1):
            copy.wait_recv()
        src, dst, held = second[part], twice[part], once[part]
        left = [axis for axis in range(3) if axis != ORDERS[part][0]]
        leading = left[0] == ORDERS[part][1]
        here = mine[ORDERS[part][1]]

        def add_second(n, carry, src=src, dst=dst, held=held, leading=leading, here=here):
            base = held[here, n] if leading else held[n, here]
            dst[n] = (base.astype(F32) + sum(src[s, n].astype(F32) for s in range(1, 4))).astype(BF16)
            return carry

        lax.fori_loop(0, 4, add_second, 0)
        for copy in copies(part, 2):
            copy.start()

    lt_part.wait()
    qo_sib.wait()
    s_sib2.wait()
    back = glf[pc.g].astype(F32)
    ratio = jnp.zeros((256, 128), F32)
    for c in range(2):
        for p in range(2):
            columns = pl.ds(c * 512 + p * 256, 256)
            blocks = [sq[c, n, :, :, :, p].reshape(256, 256) for n in range(2)]
            gqw[:, columns] = dot(ltp[0], blocks[0]) + dot(ltp[1], blocks[1])
            back = back + col_dot(qw[:, columns], sq[c, pc.g, :, :, :, p].reshape(256, 256))
    for p in range(2):
        for block, query in (
            (sq[core, pc.g, :, :, :, p], qg[pc.g, :, :, :, p]),
            (sq[1 - core, pc.g, :, :, :, p], qo[:, :, :, p]),
        ):
            prod = block.astype(F32).reshape(256, 256) * query.astype(F32).reshape(256, 256)
            ratio = ratio + prod[:, :128] + prod[:, 128:]
    coef = jnp.sum(ratio.T, axis=0, keepdims=True) * rinv_row / D_LAT
    gl_out[...] = back - coef * lt[...].astype(F32)
    give_gl = pltpu.make_async_copy(gl_out, gl_to, out_s.at[4])
    give_gl.start()
    give_gqw = pltpu.make_async_copy(gqw, gqw_to, out_s.at[5])
    give_gqw.start()
    for gather in (latents, output, resampled, scaled):
        gather.drain()

    for part in range(3):
        for copy in copies(part, 2):
            copy.wait_recv()
        here = mine[ORDERS[part][2]]
        fin[:, pl.ds(*WIDE[part])] = twice[part][here].astype(F32) + sum(
            third[part][s].astype(F32) for s in range(1, 4)
        )
    give = over(19, fin.at[at16(1 - core), :], oth, sib)
    give.start()

    def put(plane, rows):
        for n in range(2):
            spot = pl.multiple_of(n * 1024 + plane * 512, 512)
            gkw[:, pl.ds(spot, 512)] = rows[:13, n * 512 : n * 512 + 512]

    put(core, fin[at16(core), :])
    w_sib.wait_send()
    q_sib.wait_send()
    for part in range(3):
        for copy in ring(part):
            copy.wait_send()
        for phase in (1, 2):
            for copy in copies(part, phase):
                copy.wait_send()
    give.wait()
    put(1 - core, oth[...])
    give_gkw = pltpu.make_async_copy(gkw, gkw_to, out_s.at[6])
    give_gkw.start()
    for copy in (give_llm, give_gpw, give_gow, give_gain, give_gl, give_gqw, give_gkw):
        copy.wait()


def sems(*counts):
    return [pltpu.SemaphoreType.DMA((n,)) for n in counts]


def finish_kernel(*refs):
    got, done = refs[-2:]
    n = len(refs) // 3
    moves = []
    for i in range(n):
        src, dst, held = refs[i], refs[n + i], refs[2 * n + i]
        if len(src.shape) > 2:
            moves += [(src.at[m], held.at[m], dst.at[m]) for m in range(src.shape[0])]
        else:
            moves.append((src, held, dst))
    loads = [pltpu.make_async_copy(src, held, got.at[m]) for m, (src, held, dst) in enumerate(moves)]
    stores = [pltpu.make_async_copy(held, dst, done.at[m]) for m, (src, held, dst) in enumerate(moves)]
    for copy in loads:
        copy.start()
    for load, store in zip(loads, stores):
        load.wait()
        store.start()
    for copy in stores:
        copy.wait()


def local(
    tokens, keep_mask, shard_counts, latents, query_weight, keyval_weight, output_weight,
    project_weight, llm_gain, input_grad,
):
    widths = [w for _, w in WIDE]
    scratch = [
        ((256, 1664), BF16),
        ((64, 1024), BF16),
        ((64, 256), BF16),
        ((64, 1024), BF16),
        ((32, 2, 64, 128), BF16),
        ((256, 128), BF16),
        ((256, 128), BF16),
        ((64, 256), F32),
        ((64, 1024), F32),
        ((13, 2048), F32),
        ((64, 1024), F32),
        ((4, 2, 512, 128), F32),
        ((1, 128), F32),
        ((2, 128, 128), F32),
        ((256, 128), F32),
        ((2, 2, 256, 384), BF16),
        ((2, 16, 1024), BF16),
        ((128, 256), F32),
        ((4, 4, 4, 32, 1024), BF16),
        ((2, 256, 2048), BF16),
        ((2048, 512), BF16),
        ((2, 256, 128), F32),
        ((2, 256, 384), BF16),
        ((2, 256, 384), BF16),
        ((32, 16, 384), BF16),
        ((2, 4, 2, 2, 2, 16, 256), BF16),
        ((4, 2, 2, 2, 16, 256), BF16),
        ((4, 2, 4, 64, 512), BF16),
        ((4, 2, 4, 64, 256), BF16),
        ((2, 64, 256), BF16),
        ((2, 4, 2, 4, 2, 64, 256), BF16),
        ((512, 1024), BF16),
        ((512, 512), BF16),
        ((4, 512, 512), F32),
        ((4, 512, 512), BF16),
        ((2, 512, 256), BF16),
        ((64, 16, 256), BF16),
        ((8, 512), F32),
        ((4, 4, 1, 128), F32),
        ((64, 2, 1, 128), F32),
        ((16, 256), BF16),
        ((2, 512, 512), BF16),
        ((2, 128, 2048), BF16),
        ((32, 64, 128), BF16),
        ((136, 256), F32),
        ((136, 256), F32),
        ((128, 512), BF16),
        ((128, 512), BF16),
        ((128, 1024), BF16),
        ((128, 512), BF16),
        ((2, 8, 128), F32),
        ((8, 128), F32),
        ((32, 8, 128), F32),
        ((128, 256), BF16),
        ((128, 256), BF16),
        ((2, 128, 256), BF16),
        ((256, 512), BF16),
        ((32, 16, 256), BF16),
        ((4, 2, 4, 64, 256), BF16),
        ((3, 2, 4, 32, 256), BF16),
        ((3, 4, 2, 32, 256), BF16),
        ((2, 4, 32, 256), BF16),
        ((4, 2, 32, 256), BF16),
        ((2, 3, 2, 32, 256), BF16),
        ((2, 2, 32, 256), BF16),
        ((2, 32, 256), BF16),
        ((64, 256), BF16),
        ((2, 64, 256), BF16),
        ((16, 256), BF16),
        ((512, 512), BF16),
        ((4, 512, 512), BF16),
        ((512, 512), BF16),
        ((64, 16, 256), BF16),
        ((512, 1024), BF16),
        ((2, 2, 4, 2, 2, 2, 16, 256), BF16),
        *[((3, 4, 4, 32, w), BF16) for w in widths],
        *[((4, 4, 32, w), BF16) for w in widths],
        *[((4, 4, 32, w), BF16) for w in widths],
        *[((4, 32, w), BF16) for w in widths],
        *[((4, 32, w), BF16) for w in widths],
        *[((2, 2, 4, 32, w), BF16) for w in widths],
        ((32, 1024), F32),
        ((16, 1024), F32),
    ]
    results = [
        jax.ShapeDtypeStruct(shape, dtype)
        for shape, dtype in (
            ((256, 128), BF16),
            ((64, 256), F32),
            ((64, 1024), F32),
            ((13, 2048), F32),
            ((64, 1024), F32),
            ((4, 2, 512, 128), F32),
            ((1, 128), F32),
        )
    ]
    made = pl.pallas_call(
        whole_kernel,
        out_shape=results,
        in_specs=[VMEM] * 4 + [ANY] * 6,
        out_specs=[ANY] * 7,
        scratch_shapes=[pltpu.VMEM(s, d) for s, d in scratch]
        + sems(72, 72, 36, 36, 36, 36, 36, 36, 32, 32, 18, 18, 64, 64, 64, 64, 32, 32)
        + sems(32, 32, 14, 14, 64, 64, 64, 64, 64, 64, 18, 18, 36, 36, 20, 20, 20, 7),
        compiler_params=pltpu.CompilerParams(
            has_side_effects=True, vmem_limit_bytes=62 << 20, collective_id=0
        ),
        name="whole",
    )(
        keep_mask.reshape(1, 256), shard_counts.reshape(1, 1), llm_gain.reshape(1, 128),
        keyval_weight, tokens, query_weight, latents.T, output_weight.T, project_weight.reshape(32, 2, 64, 128),
        input_grad,
    )
    llm, gl, gqw, gkw, gow, gpw, gain = pl.pallas_call(
        finish_kernel,
        out_shape=results,
        in_specs=[ANY] * 7,
        out_specs=[ANY] * 7,
        scratch_shapes=[pltpu.VMEM(r.shape, r.dtype) for r in results] + sems(10, 10),
        compiler_params=pltpu.CompilerParams(vmem_limit_bytes=62 << 20),
        name="finish",
    )(*made)
    return (llm, gl.T, gqw, gkw, gow.T, gpw.reshape(4096, 128), gain.reshape(128))


def solution(mesh):
    in_specs = (
        P(("grp", "tp"), None),
        P(("grp", "tp")),
        P(("grp", "tp")),
        P("grp", "tp"),
        P("tp", None),
        P(("grp", "tp"), None),
        P(None, "tp"),
        P(None, "tp"),
        P("tp"),
        P("grp", "tp"),
    )
    out_specs = (
        P("grp", "tp"),
        P("grp", "tp"),
        P("tp", None),
        P(("grp", "tp"), None),
        P(None, "tp"),
        P(None, "tp"),
        P("tp"),
    )
    return jax.shard_map(local, mesh=mesh, in_specs=in_specs, out_specs=out_specs, check_vma=False)
```
